128 devices in a mesh: rows: 8 (over z, y_hi), heads: 16 (over y_lo, x, core).
Axes of the slice: x: 4, y: 4 (y_hi: 2, y_lo: 2; y = y_hi * 2 + y_lo), z: 4, core: 2. Of those that a mesh axis runs over, the one named last changes fastest.
Arguments:
- x_forward: bfloat16 [128, 256, 1152], P('rows', 'heads'), may hold values from -24 to 24
- x_backward: bfloat16 [128, 256, 1152], P('rows', 'heads'), may hold values from -24 to 24
- grad_out: bfloat16 [128, 256, 1152], P('rows', 'heads'), may hold values from -6 to 6
- w_qkv: bfloat16 [1152, 3456], replicated, may hold values from -0.1875 to 0.1875
- w_out: bfloat16 [1152, 1152], replicated, may hold values from -0.1875 to 0.1875
Outputs:
- y_forward: bfloat16 [128, 256, 1152], P('rows', 'heads')
- dx_backward: bfloat16 [128, 256, 1152], P('rows', 'heads')
The draws below stay inside these ranges and needn't reach their ends.
All inputs are finite; a program needn't handle non-finite values.
Results may differ from the reference program's by a relative error of at most 0.015.
The reference program's roundings to bfloat16 on the way count: a program that leaves them out, or rounds other values in their place, can miss the bound.
Values may be sent and summed in bfloat16 or wider, within the bound.
No kernel may reach another device: no remote copies, remote signals or barrier semaphores. Data moves between devices by JAX's collectives and lax.ppermute only.
A program may use at most 192 MiB of HBM per device.

```python
import jax
import jax.numpy as jnp
from jax import lax

HD = 72
HEADS = 16
D = 1152
ROWS_DEV = 16
RADIUS = 7
TILE = 32
HEIGHT = 128
WIDTH = 256
N_ROWS = 8


def scaled_tokens(key, low, high, bound):
    key_noise, key_scale = jax.random.split(key)
    noise = jax.random.truncated_normal(key_noise, -bound, bound, (HEIGHT, WIDTH, D), jnp.float32)
    scales = jnp.exp(jax.random.uniform(key_scale, (HEIGHT, WIDTH, 1), jnp.float32, jnp.log(low), jnp.log(high)))
    return noise * scales


def draw_x_forward(key, part):
    key = jax.random.fold_in(key, 11)
    return scaled_tokens(key, 0.5, 2.0, 4.0).astype(jnp.bfloat16)


def draw_x_backward(key, part):
    key = jax.random.fold_in(key, 23)
    return scaled_tokens(key, 0.5, 2.0, 4.0).astype(jnp.bfloat16)


def levels(rng, extent, cuts, smallest, top_value):
    loudness, own = 1.0, jax.random.fold_in(rng, 6)
    for position, blocks in cuts:
        draws = jnp.exp(jax.random.uniform(jax.random.fold_in(own, position), (blocks,), jnp.float32, smallest / len(cuts), top_value / len(cuts)))
        loudness = loudness * jnp.repeat(draws, extent[position] // blocks).reshape([-1 if axis == position else 1 for axis in range(len(extent))])
    return loudness


def scatter_about(own_key, shape, spread, limit, shards=(), held_as=jnp.bfloat16):
    factor_of = levels(own_key, shape, shards, -0.22, 0.18) if shards else 1.0
    drawn = jax.random.normal(own_key, shape, jnp.float32) * spread * factor_of
    return jnp.minimum(jnp.maximum(drawn, -limit), limit).astype(held_as)


def setup_inputs(seed: int = 0) -> dict:
    seeds = jax.random.split(jax.random.key(seed), 6)
    return {
        "x_forward": draw_x_forward(jax.random.fold_in(seeds[5], 71), 0),
        "x_backward": draw_x_backward(jax.random.fold_in(seeds[5], 71), 0),
        "grad_out": scatter_about(seeds[2], (HEIGHT, WIDTH, D), 1.0, 6.0, ((0, 8), (1, 16))),
        "w_qkv": scatter_about(seeds[3], (D, 3 * D), D ** -0.5, 0.1875),
        "w_out": scatter_about(seeds[4], (D, D), D ** -0.5, 0.1875),
    }


def window_mask(row_count, col_start, row_start, rows_total, cols_total):
    span_rows = row_count + 2 * RADIUS
    span_cols = TILE + 2 * RADIUS
    query_row = jnp.repeat(jnp.arange(row_count, dtype=jnp.int32), TILE)
    query_col = jnp.tile(jnp.arange(TILE, dtype=jnp.int32), row_count)
    key_row = jnp.repeat(jnp.arange(span_rows, dtype=jnp.int32), span_cols)
    key_col = jnp.tile(jnp.arange(span_cols, dtype=jnp.int32), span_rows)
    row_gap = key_row[None, :] - query_row[:, None]
    col_gap = key_col[None, :] - query_col[:, None]
    image_row = row_start + key_row - RADIUS
    image_col = col_start + key_col - RADIUS
    inside = (image_row >= 0) & (image_row < rows_total) & (image_col >= 0) & (image_col < cols_total)
    in_window = (row_gap >= 0) & (row_gap <= 2 * RADIUS) & (col_gap >= 0) & (col_gap <= 2 * RADIUS)
    return in_window & inside[None, :]


def tile_probs(queries, key_side, mask):
    scaling = queries.shape[0] ** -0.5
    scores = jnp.dot(queries.T, key_side, preferred_element_type=jnp.float32) * scaling
    masked = jnp.where(mask, scores, -1e30)
    row_top = jnp.max(masked, axis=1, keepdims=True)
    exp_terms = jnp.exp(masked - row_top)
    return exp_terms / jnp.sum(exp_terms, axis=1, keepdims=True)


def stripe_forward(queries, key_pad, value_pad, row_start, rows_total):
    head_dim, row_count, width = queries.shape
    span_cols = TILE + 2 * RADIUS

    def one_tile(tile_index):
        col_start = tile_index * TILE
        q_tile = lax.dynamic_slice_in_dim(queries, col_start, TILE, 2).reshape(head_dim, row_count * TILE)
        k_tile = lax.dynamic_slice_in_dim(key_pad, col_start, span_cols, 2).reshape(head_dim, -1)
        v_tile = lax.dynamic_slice_in_dim(value_pad, col_start, span_cols, 2).reshape(head_dim, -1)
        prob_rows = tile_probs(q_tile, k_tile, window_mask(row_count, col_start, row_start, rows_total, width))
        mixed_tile = jnp.dot(v_tile, prob_rows.astype(jnp.bfloat16).T, preferred_element_type=jnp.float32)
        return mixed_tile.reshape(head_dim, row_count, TILE)

    tile_outs = lax.map(one_tile, jnp.arange(width // TILE, dtype=jnp.int32))
    return jnp.transpose(tile_outs, (1, 2, 0, 3)).reshape(head_dim, row_count, width)


def stripe_backward(queries, key_pad, value_pad, grad_heads, row_start, rows_total):
    head_dim, row_count, width = queries.shape
    span_cols = TILE + 2 * RADIUS
    span_rows = row_count + 2 * RADIUS
    scaling = head_dim ** -0.5

    def one_tile(totals, tile_index):
        key_acc, value_acc = totals
        col_start = tile_index * TILE
        q_tile = lax.dynamic_slice_in_dim(queries, col_start, TILE, 2).reshape(head_dim, row_count * TILE)
        g_tile = lax.dynamic_slice_in_dim(grad_heads, col_start, TILE, 2).reshape(head_dim, row_count * TILE)
        k_tile = lax.dynamic_slice_in_dim(key_pad, col_start, span_cols, 2).reshape(head_dim, -1)
        v_tile = lax.dynamic_slice_in_dim(value_pad, col_start, span_cols, 2).reshape(head_dim, -1)
        prob_rows = tile_probs(q_tile, k_tile, window_mask(row_count, col_start, row_start, rows_total, width))
        weight_rows = prob_rows.astype(jnp.bfloat16)
        grad_probs = jnp.dot(g_tile.T, v_tile, preferred_element_type=jnp.float32)
        centre = jnp.sum(prob_rows * grad_probs, axis=1, keepdims=True)
        grad_scores = (prob_rows * (grad_probs - centre) * scaling).astype(jnp.bfloat16)
        grad_query = jnp.dot(k_tile, grad_scores.T, preferred_element_type=jnp.float32)
        grad_keys = jnp.dot(q_tile, grad_scores, preferred_element_type=jnp.float32).reshape(head_dim, span_rows, span_cols)
        grad_values = jnp.dot(g_tile, weight_rows, preferred_element_type=jnp.float32).reshape(head_dim, span_rows, span_cols)
        key_acc = lax.dynamic_update_slice_in_dim(key_acc, lax.dynamic_slice_in_dim(key_acc, col_start, span_cols, 2) + grad_keys, col_start, 2)
        value_acc = lax.dynamic_update_slice_in_dim(value_acc, lax.dynamic_slice_in_dim(value_acc, col_start, span_cols, 2) + grad_values, col_start, 2)
        return (key_acc, value_acc), grad_query.reshape(head_dim, row_count, TILE)

    empty_acc = jnp.zeros((head_dim, span_rows, width + 2 * RADIUS), jnp.float32)
    (key_acc, value_acc), tile_outs = lax.scan(one_tile, (empty_acc, empty_acc), jnp.arange(width // TILE, dtype=jnp.int32))
    grad_query = jnp.transpose(tile_outs, (1, 2, 0, 3)).reshape(head_dim, row_count, width)
    return grad_query, key_acc, value_acc


def reference(x_forward, x_backward, grad_out, w_qkv, w_out):
    def heads_layout(tokens_in):
        flat_rows = jnp.dot(tokens_in.reshape(HEIGHT * WIDTH, D), w_qkv, preferred_element_type=jnp.float32).astype(jnp.bfloat16)
        return jnp.transpose(flat_rows.reshape(HEIGHT, WIDTH, 3, HEADS, HD), (2, 3, 4, 0, 1))

    qkv_forward = heads_layout(x_forward)
    qkv_backward = heads_layout(x_backward)
    grad_flat = jnp.dot(grad_out.reshape(HEIGHT * WIDTH, D), w_out.T, preferred_element_type=jnp.float32).astype(jnp.bfloat16)
    grad_heads = jnp.transpose(grad_flat.reshape(HEIGHT, WIDTH, HEADS, HD), (2, 3, 0, 1))
    border = ((0, 0), (RADIUS, RADIUS), (RADIUS, RADIUS))
    span_rows = ROWS_DEV + 2 * RADIUS

    def head_forward(head_inputs):
        queries, key_side, value_side = head_inputs
        key_pad = jnp.pad(key_side, border)
        value_pad = jnp.pad(value_side, border)

        def stripe(stripe_index):
            row_start = stripe_index * ROWS_DEV
            return stripe_forward(lax.dynamic_slice_in_dim(queries, row_start, ROWS_DEV, 1),
                                  lax.dynamic_slice_in_dim(key_pad, row_start, span_rows, 1),
                                  lax.dynamic_slice_in_dim(value_pad, row_start, span_rows, 1),
                                  row_start, HEIGHT)

        stripe_outs = lax.map(stripe, jnp.arange(N_ROWS, dtype=jnp.int32))
        return jnp.transpose(stripe_outs, (1, 0, 2, 3)).reshape(HD, HEIGHT, WIDTH)

    attended = lax.map(head_forward, (qkv_forward[0], qkv_forward[1], qkv_forward[2])).astype(jnp.bfloat16)
    attended_rows = jnp.transpose(attended, (2, 3, 0, 1)).reshape(HEIGHT * WIDTH, D)
    y_forward = jnp.dot(attended_rows, w_out, preferred_element_type=jnp.float32).astype(jnp.bfloat16).reshape(HEIGHT, WIDTH, D)

    def head_backward(head_inputs):
        queries, key_side, value_side, head_grads = head_inputs
        key_pad = jnp.pad(key_side, border)
        value_pad = jnp.pad(value_side, border)

        def stripe(totals, stripe_index):
            key_total, value_total = totals
            row_start = stripe_index * ROWS_DEV
            grad_query, key_part, value_part = stripe_backward(
                lax.dynamic_slice_in_dim(queries, row_start, ROWS_DEV, 1),
                lax.dynamic_slice_in_dim(key_pad, row_start, span_rows, 1),
                lax.dynamic_slice_in_dim(value_pad, row_start, span_rows, 1),
                lax.dynamic_slice_in_dim(head_grads, row_start, ROWS_DEV, 1),
                row_start, HEIGHT)
            key_total = lax.dynamic_update_slice_in_dim(key_total, lax.dynamic_slice_in_dim(key_total, row_start, span_rows, 1) + key_part, row_start, 1)
            value_total = lax.dynamic_update_slice_in_dim(value_total, lax.dynamic_slice_in_dim(value_total, row_start, span_rows, 1) + value_part, row_start, 1)
            return (key_total, value_total), grad_query

        empty_acc = jnp.zeros((HD, HEIGHT + 2 * RADIUS, WIDTH + 2 * RADIUS), jnp.float32)
        (key_total, value_total), stripe_outs = lax.scan(stripe, (empty_acc, empty_acc), jnp.arange(N_ROWS, dtype=jnp.int32))
        grad_query = jnp.transpose(stripe_outs, (1, 0, 2, 3)).reshape(HD, HEIGHT, WIDTH)
        key_grad = key_total[:, RADIUS:RADIUS + HEIGHT, RADIUS:RADIUS + WIDTH]
        value_grad = value_total[:, RADIUS:RADIUS + HEIGHT, RADIUS:RADIUS + WIDTH]
        return jnp.stack((grad_query, key_grad, value_grad)).astype(jnp.bfloat16)

    grad_qkv = lax.map(head_backward, (qkv_backward[0], qkv_backward[1], qkv_backward[2], grad_heads))
    flat_grads = jnp.transpose(grad_qkv, (3, 4, 1, 0, 2)).reshape(HEIGHT * WIDTH, 3 * D)
    dx_backward = jnp.dot(flat_grads, w_qkv.T, preferred_element_type=jnp.float32).astype(jnp.bfloat16).reshape(HEIGHT, WIDTH, D)
    return y_forward, dx_backward
```

```python
import functools
import math

import jax
import jax.numpy as jnp
from jax import lax
from jax.experimental import pallas as pl
from jax.experimental.pallas import tpu as pltpu
from jax.sharding import PartitionSpec as P

RADIUS = 7
SIDE = 16
LANES = 256
GROUP = 256
HALF = 128
SPAN = 3 * GROUP
KEYS = 4 * GROUP
NEG = -1e30


def shifted(value, axis, step):
    count = lax.axis_size(axis)
    pairs = [(i, i + step) for i in range(count) if 0 <= i + step < count]
    return lax.ppermute(value, axis, pairs)


def with_rows(x):
    above = shifted(x[SIDE - RADIUS :], "rows", 1)
    below = shifted(x[:RADIUS], "rows", -1)
    return jnp.concatenate([above, x, below, jnp.zeros((2,) + x.shape[1:], x.dtype)], 0)


def side_columns(xr):
    left = shifted(xr[:, 8:], "heads", 1)
    right = shifted(xr[:, :8], "heads", -1)
    return jnp.concatenate([left, right], 1)


def window_bias():
    row_start = lax.axis_index("rows") * SIDE
    col_start = lax.axis_index("heads") * SIDE
    rows_total = lax.axis_size("rows") * SIDE
    cols_total = lax.axis_size("heads") * SIDE
    query = lax.broadcasted_iota(jnp.int32, (2 * HALF, SPAN), 0)
    place = lax.broadcasted_iota(jnp.int32, (2 * HALF, SPAN), 1)
    half = query // HALF
    query_row, query_col = query // SIDE, query % SIDE
    group, rest = place // GROUP + half, place % GROUP
    side, inner = rest // HALF, rest % HALF
    key_row, column = group * 8 + inner // SIDE, inner % SIDE
    key_col = jnp.where(side == 0, column, jnp.where(column < 8, column - 8, column + 8))
    image_row = row_start + key_row - RADIUS
    image_col = col_start + key_col
    row_gap, col_gap = key_row - query_row, key_col - query_col
    valid = (row_gap >= 0) & (row_gap <= 2 * RADIUS) & (col_gap >= -RADIUS) & (col_gap <= RADIUS)
    valid &= (image_row >= 0) & (image_row < rows_total) & (image_col >= 0) & (image_col < cols_total)
    return jnp.where(valid, 0.0, NEG).astype(jnp.float32)


def head_lanes(head, head_dim, width):
    tile = jnp.minimum(head * head_dim // 128, (width - LANES) // 128)
    start = pl.multiple_of(tile * 128, 128)
    offset = head * head_dim - start
    lane = lax.broadcasted_iota(jnp.int32, (1, LANES), 1)
    return pl.ds(start, LANES), (lane >= offset) & (lane < offset + head_dim)


def assemble(own_ref, side_ref, full_ref, start, width):
    for group in range(4):
        rows = slice(HALF * group, HALF * (group + 1))
        full_ref[GROUP * group : GROUP * group + HALF, :] = own_ref[rows, start : start + width]
        full_ref[GROUP * group + HALF : GROUP * (group + 1), :] = side_ref[rows, start : start + width]


def clear_corners(ref):
    zeros = jnp.zeros((HALF, GROUP), ref.dtype)
    ref[:HALF, SPAN:] = zeros
    ref[HALF:, :GROUP] = zeros


def span_products(rows, full_ref, lanes, out_ref):
    for group in range(4):
        low = 0 if group < 3 else HALF
        high = 2 * HALF if group > 0 else HALF
        keys = full_ref[GROUP * group : GROUP * (group + 1), lanes]
        part = lax.dot_general(
            rows[low:high], keys, (((1,), (1,)), ((), ())), preferred_element_type=jnp.float32
        )
        if group < 3:
            out_ref[:HALF, GROUP * group : GROUP * (group + 1)] = part[:HALF]
        if group > 0:
            out_ref[HALF:, GROUP * (group - 1) : GROUP * group] = part[-HALF:]


def softmax_rows(scores, bias, factor):
    scores = scores + bias
    top = jnp.max(scores, axis=1, keepdims=True)
    terms = jnp.exp2((scores - top) * factor)
    return terms * (1.0 / jnp.sum(terms, axis=1, keepdims=True))


def forward_kernel(head_dim, q_ref, own_ref, side_ref, bias_ref, out_ref, keys, values, acc, *scratch):
    step = pl.program_id(0)
    width = q_ref.shape[1]
    factor = head_dim**-0.5 * math.log2(math.e)
    scores, probs = scratch[:2], scratch[2:]

    @pl.when(step == 0)
    def _():
        assemble(own_ref, side_ref, keys, 0, width)
        assemble(own_ref, side_ref, values, width, width)
        acc[...] = jnp.zeros_like(acc)
        for ref in probs:
            clear_corners(ref)

    for u in range(2):
        lanes, mask = head_lanes(2 * step + u, head_dim, width)
        queries = jnp.where(mask, q_ref[:, lanes], 0)
        span_products(queries, keys, lanes, scores[u])
        for rows in range(0, 2 * HALF, 16):
            part = slice(rows, rows + 16)
            weights = softmax_rows(scores[u][part, :], bias_ref[part, :], factor)
            start = 0 if rows < HALF else GROUP
            probs[u][part, start : start + SPAN] = weights.astype(jnp.bfloat16)
        mixed = jnp.dot(probs[u][...], values[:, lanes], preferred_element_type=jnp.float32)
        acc[:, lanes] += jnp.where(mask, mixed, 0.0)

    @pl.when(step == pl.num_programs(0) - 1)
    def _():
        out_ref[...] = acc[...].astype(out_ref.dtype)


def backward_kernel(
    head_dim, q_ref, g_ref, qt_ref, gt_ref, own_ref, side_ref, bias_ref, dq_ref, down_ref, dside_ref,
    keys, values, acc, *scratch
):
    step = pl.program_id(0)
    width = q_ref.shape[1]
    scaling = head_dim**-0.5
    factor = scaling * math.log2(math.e)
    scores, grads, probs, dscores = scratch[:2], scratch[2:4], scratch[4:6], scratch[6:8]

    @pl.when(step == 0)
    def _():
        assemble(own_ref, side_ref, keys, 0, width)
        assemble(own_ref, side_ref, values, width, width)
        acc[...] = jnp.zeros_like(acc)
        for ref in probs + dscores:
            clear_corners(ref)

    key_grads, value_grads = [], []
    for u in range(2):
        lanes, mask = head_lanes(2 * step + u, head_dim, width)
        queries = jnp.where(mask, q_ref[:, lanes], 0)
        cotangents = jnp.where(mask, g_ref[:, lanes], 0)
        span_products(queries, keys, lanes, scores[u])
        span_products(cotangents, values, lanes, grads[u])
        for rows in range(0, 2 * HALF, 16):
            part = slice(rows, rows + 16)
            weights = softmax_rows(scores[u][part, :], bias_ref[part, :], factor)
            grad = grads[u][part, :]
            centre = jnp.sum(weights * grad, axis=1, keepdims=True)
            start = 0 if rows < HALF else GROUP
            span = slice(start, start + SPAN)
            probs[u][part, span] = weights.astype(jnp.bfloat16)
            dscores[u][part, span] = (weights * (grad - centre) * scaling).astype(jnp.bfloat16)
        dscore = dscores[u][...]
        dq = jnp.dot(dscore, keys[:, lanes], preferred_element_type=jnp.float32)
        acc[:, lanes] += jnp.where(mask, dq, 0.0)
        key_grads.append(jnp.dot(qt_ref[u], dscore, preferred_element_type=jnp.float32))
        value_grads.append(jnp.dot(gt_ref[u], probs[u][...], preferred_element_type=jnp.float32))

    for index, pair in enumerate((key_grads, value_grads)):
        both = jnp.concatenate(pair, 0).astype(jnp.bfloat16)
        for group in range(4):
            place = slice(HALF * group, HALF * (group + 1))
            down_ref[index, :, place] = both[:, GROUP * group : GROUP * group + HALF]
            dside_ref[index, :, place] = both[:, GROUP * group + HALF : GROUP * (group + 1)]

    @pl.when(step == pl.num_programs(0) - 1)
    def _():
        dq_ref[...] = acc[...].astype(dq_ref.dtype)


def whole(shape):
    return pl.BlockSpec(shape, lambda i: (0,) * len(shape))


def attention_forward(queries, own, side, bias, heads):
    tokens, width = queries.shape
    head_dim = width // heads
    square = (tokens, SPAN)
    return pl.pallas_call(
        functools.partial(forward_kernel, head_dim),
        grid=(heads // 2,),
        in_specs=[whole(queries.shape), whole(own.shape), whole(side.shape), whole(square)],
        out_specs=whole(queries.shape),
        out_shape=jax.ShapeDtypeStruct(queries.shape, jnp.bfloat16),
        scratch_shapes=[
            pltpu.VMEM((KEYS, width), jnp.bfloat16),
            pltpu.VMEM((KEYS, width), jnp.bfloat16),
            pltpu.VMEM((tokens, width), jnp.float32),
        ]
        + [pltpu.VMEM(square, jnp.float32)] * 2
        + [pltpu.VMEM((tokens, KEYS), jnp.bfloat16)] * 2,
        compiler_params=pltpu.CompilerParams(vmem_limit_bytes=48 * 2**20),
        cost_estimate=pl.CostEstimate(
            flops=4 * heads * tokens * KEYS * LANES, bytes_accessed=8 * 2**20, transcendentals=heads * tokens * SPAN
        ),
        name="attention_forward",
    )(queries, own, side, bias)


def attention_backward(queries, cotangents, own, side, bias, heads):
    tokens, width = queries.shape
    head_dim = width // heads
    square = (tokens, SPAN)
    pair = pl.BlockSpec((2, head_dim, tokens), lambda i: (i, 0, 0))
    grads = pl.BlockSpec((2, 2 * head_dim, KEYS // 2), lambda i: (0, i, 0))
    grads_shape = jax.ShapeDtypeStruct((2, width, KEYS // 2), jnp.bfloat16)
    return pl.pallas_call(
        functools.partial(backward_kernel, head_dim),
        grid=(heads // 2,),
        in_specs=[whole(queries.shape), whole(queries.shape), pair, pair]
        + [whole(own.shape), whole(side.shape), whole(square)],
        out_specs=[whole(queries.shape), grads, grads],
        out_shape=[jax.ShapeDtypeStruct(queries.shape, jnp.bfloat16), grads_shape, grads_shape],
        scratch_shapes=[
            pltpu.VMEM((KEYS, width), jnp.bfloat16),
            pltpu.VMEM((KEYS, width), jnp.bfloat16),
            pltpu.VMEM((tokens, width), jnp.float32),
        ]
        + [pltpu.VMEM(square, jnp.float32)] * 4
        + [pltpu.VMEM((tokens, KEYS), jnp.bfloat16)] * 4,
        compiler_params=pltpu.CompilerParams(vmem_limit_bytes=48 * 2**20),
        cost_estimate=pl.CostEstimate(
            flops=10 * heads * tokens * KEYS * LANES, bytes_accessed=16 * 2**20, transcendentals=heads * tokens * SPAN
        ),
        name="attention_backward",
    )(
        queries,
        cotangents,
        jnp.transpose(queries).reshape(heads, head_dim, tokens),
        jnp.transpose(cotangents).reshape(heads, head_dim, tokens),
        own,
        side,
        bias,
    )


def project(x, w):
    return jnp.dot(x, w, preferred_element_type=jnp.float32).astype(jnp.bfloat16)


def body(x_forward, x_backward, grad_out, w_qkv, w_out):
    rows, cols, width = x_forward.shape
    heads = lax.axis_size("heads")
    tokens = rows * cols
    w_q, w_kv = w_qkv[:, :width], w_qkv[:, width:]
    bias = window_bias()

    xr_backward = with_rows(x_backward)
    xs_backward = side_columns(xr_backward)
    xr_forward = with_rows(x_forward)
    xs_forward = side_columns(xr_forward)

    flat = lambda x: x.reshape(-1, width)
    q_backward = project(flat(x_backward), w_q)
    grad_heads = lax.dot_general(
        flat(grad_out), w_out, (((1,), (1,)), ((), ())), preferred_element_type=jnp.float32
    ).astype(jnp.bfloat16)
    q_forward = project(flat(x_forward), w_q)
    own_backward = project(flat(xr_backward), w_kv)
    side_backward = project(flat(xs_backward), w_kv)

    dq, down, dside = attention_backward(q_backward, grad_heads, own_backward, side_backward, bias, heads)
    contract = (((0,), (1,)), ((), ()))
    dx_side = lax.dot_general(
        dside.reshape(2 * width, -1), w_kv, contract, preferred_element_type=jnp.float32
    ).astype(jnp.bfloat16).reshape(2 * SIDE, SIDE, width)
    from_right = shifted(dx_side[:, :8], "heads", -1)
    from_left = shifted(dx_side[:, 8:], "heads", 1)
    dx_own = lax.dot_general(
        down.reshape(2 * width, -1), w_kv, contract, preferred_element_type=jnp.float32
    ).reshape(2 * SIDE, SIDE, width)
    dx_query = lax.dot_general(
        dq, w_q, (((1,), (1,)), ((), ())), preferred_element_type=jnp.float32
    ).reshape(rows, cols, width)
    total = dx_own + jnp.concatenate([from_left, from_right], 1).astype(jnp.float32)
    from_below = shifted(total[:RADIUS].astype(jnp.bfloat16), "rows", -1)
    from_above = shifted(total[RADIUS + SIDE : 2 * RADIUS + SIDE].astype(jnp.bfloat16), "rows", 1)
    middle = total[RADIUS : RADIUS + SIDE] + dx_query

    own_forward = project(flat(xr_forward), w_kv)
    side_forward = project(flat(xs_forward), w_kv)
    attended = attention_forward(q_forward, own_forward, side_forward, bias, heads)
    y_forward = project(attended, w_out).reshape(rows, cols, width)

    gap = jnp.zeros((rows - RADIUS, cols, width), jnp.float32)
    dx = (
        middle
        + jnp.concatenate([from_above.astype(jnp.float32), gap], 0)
        + jnp.concatenate([gap, from_below.astype(jnp.float32)], 0)
    )
    return (y_forward, dx.astype(jnp.bfloat16))


def solution(mesh):
    spec = P("rows", "heads", None)
    return jax.shard_map(
        body, mesh=mesh, in_specs=(spec, spec, spec, P(), P()), out_specs=(spec, spec), check_vma=False
    )
```

```python
import functools
import math

import jax
import jax.numpy as jnp
from jax import lax
from jax.experimental import pallas as pl
from jax.experimental.pallas import tpu as pltpu
from jax.sharding import PartitionSpec as P

RADIUS = 7
SIDE = 16
LANES = 256
GROUP = 256
HALF = 128
SPAN = 3 * GROUP
KEYS = 4 * GROUP
NEG = -1e30
CHUNK = 16
SPLIT = 6
LIMIT = 40 * 2**20


def shifted(value, axis, step):
    count = lax.axis_size(axis)
    pairs = [(i, i + step) for i in range(count) if 0 <= i + step < count]
    return lax.ppermute(value, axis, pairs)


def with_rows(x):
    above = shifted(x[SIDE - RADIUS :], "rows", 1)
    below = shifted(x[:RADIUS], "rows", -1)
    return jnp.concatenate([above, x, below, jnp.zeros((2,) + x.shape[1:], x.dtype)], 0)


def side_columns(xr):
    left = shifted(xr[:, 8:], "heads", 1)
    right = shifted(xr[:, :8], "heads", -1)
    return jnp.concatenate([left, right], 1)


def window_bias():
    row_start = lax.axis_index("rows") * SIDE
    col_start = lax.axis_index("heads") * SIDE
    rows_total = lax.axis_size("rows") * SIDE
    cols_total = lax.axis_size("heads") * SIDE
    query = lax.broadcasted_iota(jnp.int32, (2 * HALF, SPAN), 0)
    place = lax.broadcasted_iota(jnp.int32, (2 * HALF, SPAN), 1)
    half = query // HALF
    query_row, query_col = query // SIDE, query % SIDE
    group, rest = place // GROUP + half, place % GROUP
    side, inner = rest // HALF, rest % HALF
    key_row, column = group * 8 + inner // SIDE, inner % SIDE
    key_col = jnp.where(side == 0, column, jnp.where(column < 8, column - 8, column + 8))
    image_row = row_start + key_row - RADIUS
    image_col = col_start + key_col
    row_gap, col_gap = key_row - query_row, key_col - query_col
    valid = (row_gap >= 0) & (row_gap <= 2 * RADIUS) & (col_gap >= -RADIUS) & (col_gap <= RADIUS)
    valid &= (image_row >= 0) & (image_row < rows_total) & (image_col >= 0) & (image_col < cols_total)
    return jnp.where(valid, 0.0, NEG).astype(jnp.float32)


def head_lanes(head, head_dim, width):
    tile = jnp.clip(head * head_dim // 128, 0, (width - LANES) // 128)
    offset = head * head_dim - tile * 128
    lane = lax.broadcasted_iota(jnp.int32, (1, LANES), 1)
    return tile * 128, (lane >= offset) & (lane < offset + head_dim)


def at_lanes(start):
    return pl.ds(pl.multiple_of(start, 128), LANES)


def fill_keys(x_own, x_side, weights, starts, kv):
    skip = weights.shape[1] - kv.shape[1]
    for start in starts:
        place = slice(start - skip, start - skip + GROUP)
        for side, x_ref in enumerate((x_own, x_side)):
            part = jnp.dot(x_ref[...], weights[:, start : start + GROUP], preferred_element_type=jnp.float32)
            for group in range(4):
                low = GROUP * group + HALF * side
                kv[low : low + HALF, place] = part[HALF * group : HALF * (group + 1)].astype(kv.dtype)


def span_products(rows, kv, start, out_ref):
    def one(group):
        low = 0 if group < 3 else HALF
        high = 2 * HALF if group > 0 else HALF
        keys = kv[GROUP * group : GROUP * (group + 1), at_lanes(start)]
        part = lax.dot_general(
            rows[low:high], keys, (((1,), (1,)), ((), ())), preferred_element_type=jnp.float32
        )
        if group < 3:
            out_ref[:HALF, GROUP * group : GROUP * (group + 1)] = part[:HALF]
        if group > 0:
            out_ref[HALF:, GROUP * (group - 1) : GROUP * group] = part[-HALF:]

    return [functools.partial(one, group) for group in range(4)]


def interleave(*streams):
    marks = [((i + 0.5) / len(stream), n, step) for n, stream in enumerate(streams) for i, step in enumerate(stream)]
    for _, _, step in sorted(marks, key=lambda mark: mark[:2]):
        step()


def softmax_rows(scores, bias, factor):
    scores = scores + bias
    top = jnp.max(scores, axis=1, keepdims=True)
    terms = jnp.exp2((scores - top) * factor)
    return terms * (1.0 / jnp.sum(terms, axis=1, keepdims=True))


def span_of(rows):
    start = 0 if rows < HALF else GROUP
    return slice(start, start + SPAN)


def forward_kernel(
    head_dim, first, end, starts, last, x_own, x_side, weights, w_out, queries, bias, before, out_ref,
    kv, acc, scores0, scores1, probs0, probs1
):
    width = queries.shape[1]
    factor = head_dim**-0.5 * math.log2(math.e)
    scores, probs = (scores0, scores1), (probs0, probs1)
    acc[...] = before[...] if last else jnp.zeros_like(acc)
    for ref in probs:
        ref[...] = jnp.zeros_like(ref)
    fill_keys(x_own, x_side, weights, starts, kv)

    def scored(head, u):
        start, mask = head_lanes(head, head_dim, width)
        return span_products(jnp.where(mask, queries[:, at_lanes(start)], 0), kv, start, scores[u])

    def weighted(u):
        def one(rows):
            part = slice(rows, rows + CHUNK)
            attention = softmax_rows(scores[u][part, :], bias[part, :], factor)
            probs[u][part, span_of(rows)] = attention.astype(jnp.bfloat16)

        return [functools.partial(one, rows) for rows in range(0, 2 * HALF, CHUNK)]

    def mixed(head, u):
        start, mask = head_lanes(head, head_dim, width)

        def one():
            mix = jnp.dot(probs[u][...], kv[:, at_lanes(start + width)], preferred_element_type=jnp.float32)
            acc[:, at_lanes(start)] += jnp.where(mask & (head >= first), mix, 0.0)

        return [one]

    interleave(scored(first, 0))

    def pair(index, carry):
        head = first + 2 * index
        interleave(scored(head + 1, 1), weighted(0), mixed(head - 1, 1))
        interleave(scored(jnp.minimum(head + 2, end - 1), 0), weighted(1), mixed(head, 0))
        return carry

    lax.fori_loop(0, (end - first) // 2, pair, 0)
    interleave(mixed(end - 1, 1))
    if last:
        attended = acc[...].astype(jnp.bfloat16)
        out_ref[...] = jnp.dot(attended, w_out[...], preferred_element_type=jnp.float32).astype(out_ref.dtype)
    else:
        out_ref[...] = acc[...]


def backward_kernel(
    head_dim, starts, x_own, x_side, weights, queries, cotangents, queries_t, cotangents_t, bias, down_ref, dside_ref,
    kv, dkv, acc, scores0, scores1, grads0, grads1, probs0, probs1, dscores0, dscores1, held0, held1
):
    width = queries.shape[1]
    heads = width // head_dim
    scaling = head_dim**-0.5
    factor = scaling * math.log2(math.e)
    scores, grads, held = (scores0, scores1), (grads0, grads1), (held0, held1)
    probs, dscores = (probs0, probs1), (dscores0, dscores1)
    for ref in probs + dscores + held + (acc,):
        ref[...] = jnp.zeros_like(ref)
    fill_keys(x_own, x_side, weights, starts, kv)

    def scored(head, u):
        start, mask = head_lanes(head, head_dim, width)
        one = span_products(jnp.where(mask, queries[:, at_lanes(start)], 0), kv, start, scores[u])
        other = span_products(jnp.where(mask, cotangents[:, at_lanes(start)], 0), kv, start + width, grads[u])
        return [step for both in zip(one, other) for step in both]

    def weighted(u):
        def one(rows):
            part = slice(rows, rows + CHUNK)
            attention = softmax_rows(scores[u][part, :], bias[part, :], factor)
            grad = grads[u][part, :]
            centre = jnp.sum(attention * grad, axis=1, keepdims=True)
            probs[u][part, span_of(rows)] = attention.astype(jnp.bfloat16)
            dscores[u][part, span_of(rows)] = (attention * (grad - centre) * scaling).astype(jnp.bfloat16)

        return [functools.partial(one, rows) for rows in range(0, 2 * HALF, CHUNK)]

    def spread(head, u):
        start, mask = head_lanes(head, head_dim, width)
        row = jnp.maximum(head, 0)
        base = jnp.maximum(head - 1, 0) * head_dim

        def query_part():
            dq = jnp.dot(dscores[u][...], kv[:, at_lanes(start)], preferred_element_type=jnp.float32)
            acc[:, at_lanes(start)] += jnp.where(mask & (head >= 0), dq, 0.0)

        def key_part(index, group):
            source, spans = ((queries_t, dscores), (cotangents_t, probs))[index]
            place = slice(GROUP * group, GROUP * (group + 1))
            part = jnp.dot(source[row], spans[u][:, place], preferred_element_type=jnp.float32)
            if u == 0:
                held[index][:, place] = part
            else:
                both = jnp.concatenate([held[index][:, place], part], 0).astype(jnp.bfloat16)
                dkv[pl.ds(pl.multiple_of(base + index * width, 16), 2 * head_dim), place] = both

        parts = [functools.partial(key_part, index, group) for index in range(2) for group in range(4)]
        return parts[:4] + [query_part] + parts[4:]

    interleave(scored(0, 0))

    def pair(index, carry):
        head = 2 * index
        interleave(scored(head + 1, 1), weighted(0), spread(head - 1, 1))
        interleave(scored(jnp.minimum(head + 2, heads - 1), 0), weighted(1), spread(head, 0))
        return carry

    lax.fori_loop(0, heads // 2, pair, 0)
    interleave(spread(heads - 1, 1))

    for group in range(4):
        place = slice(GROUP * group, GROUP * (group + 1))
        part = jnp.dot(weights[:, width:], dkv[:, place], preferred_element_type=jnp.float32)
        rows = slice(HALF * group, HALF * (group + 1))
        down_ref[rows, :] = jnp.transpose(part[:, :HALF])
        dside_ref[rows, :] = jnp.transpose(part[:, HALF:]).astype(dside_ref.dtype)
    dx_query = lax.dot_general(
        acc[...].astype(jnp.bfloat16), weights[:, :width], (((1,), (1,)), ((), ())),
        preferred_element_type=jnp.float32,
    )
    mine = slice(RADIUS * SIDE, RADIUS * SIDE + 2 * HALF)
    down_ref[mine, :] += dx_query


def call_kernel(kernel, args, out_shape, scratch, flops, name):
    return pl.pallas_call(
        kernel,
        out_shape=out_shape,
        scratch_shapes=scratch,
        compiler_params=pltpu.CompilerParams(vmem_limit_bytes=LIMIT),
        cost_estimate=pl.CostEstimate(flops=flops, bytes_accessed=16 * 2**20, transcendentals=2**22),
        name=name,
    )(*args)


def attention_forward(x_own, x_side, w_qkv, w_out, queries, bias, before, first, end, heads):
    tokens, width = queries.shape
    head_dim = width // heads
    last = before is not None
    low = first * head_dim // 128 * 128
    high = low - (low - end * head_dim) // GROUP * GROUP
    if high > width:
        low, high = low - (high - width), width
    starts = [part * width + at for part in (1, 2) for at in range(low, high, GROUP)]
    half, full = jnp.bfloat16, jnp.float32
    square = (tokens, SPAN)
    scratch = [
        pltpu.VMEM((KEYS, 2 * width), half),
        pltpu.VMEM((tokens, width), full),
    ]
    scratch += [pltpu.VMEM(square, full)] * 2 + [pltpu.VMEM((tokens, KEYS), half)] * 2
    return call_kernel(
        functools.partial(forward_kernel, head_dim, first, end, starts, last),
        [x_own, x_side, w_qkv, w_out, queries, bias, before if last else queries],
        jax.ShapeDtypeStruct(queries.shape, half if last else full),
        scratch,
        2 * KEYS * width * GROUP * len(starts) + 4 * (end - first) * tokens * KEYS * LANES,
        "attention_forward",
    )


def attention_backward(x_own, x_side, w_qkv, queries, cotangents, bias, heads):
    tokens, width = queries.shape
    head_dim = width // heads
    square = (tokens, SPAN)
    half, full = jnp.bfloat16, jnp.float32
    starts = list(range(width, 3 * width, GROUP))
    by_head = (heads, head_dim, tokens)
    args = [x_own, x_side, w_qkv, queries, cotangents]
    args += [jnp.transpose(queries).reshape(by_head), jnp.transpose(cotangents).reshape(by_head), bias]
    scratch = [
        pltpu.VMEM((KEYS, 2 * width), half),
        pltpu.VMEM((2 * width, KEYS), half),
        pltpu.VMEM((tokens, width), full),
    ]
    scratch += [pltpu.VMEM(square, full)] * 4 + [pltpu.VMEM((tokens, KEYS), half)] * 4
    scratch += [pltpu.VMEM((head_dim, KEYS), full)] * 2
    return call_kernel(
        functools.partial(backward_kernel, head_dim, starts),
        args,
        [jax.ShapeDtypeStruct((KEYS // 2, width), full), jax.ShapeDtypeStruct((KEYS // 2, width), half)],
        scratch,
        8 * KEYS * width * width + 10 * heads * tokens * KEYS * LANES,
        "attention_backward",
    )


def project(x, w):
    return jnp.dot(x, w, preferred_element_type=jnp.float32).astype(jnp.bfloat16)


def body(x_forward, x_backward, grad_out, w_qkv, w_out):
    rows, cols, width = x_forward.shape
    heads = lax.axis_size("heads")
    w_q = w_qkv[:, :width]
    flat = lambda x: x.reshape(-1, width)
    bias = window_bias()

    xr_backward = with_rows(x_backward)
    xs_backward = side_columns(xr_backward)
    xr_forward = with_rows(x_forward)
    xs_forward = side_columns(xr_forward)

    q_backward = project(flat(x_backward), w_q)
    grad_heads = lax.dot_general(
        flat(grad_out), w_out, (((1,), (1,)), ((), ())), preferred_element_type=jnp.float32
    ).astype(jnp.bfloat16)
    q_forward = project(flat(x_forward), w_q)

    dx_own, dx_side = attention_backward(
        flat(xr_backward), flat(xs_backward), w_qkv, q_backward, grad_heads, bias, heads
    )
    dx_own = dx_own.reshape(2 * SIDE, SIDE, width)
    dx_side = dx_side.reshape(2 * SIDE, SIDE, width)
    from_right = shifted(dx_side[:, :8], "heads", -1)
    from_left = shifted(dx_side[:, 8:], "heads", 1)

    x_own, x_side, _ = lax.optimization_barrier((flat(xr_forward), flat(xs_forward), dx_side))
    first = attention_forward(x_own, x_side, w_qkv, w_out, q_forward, bias, None, 0, SPLIT, heads)
    from_left, from_right, first = lax.optimization_barrier((from_left, from_right, first))
    total = dx_own + jnp.concatenate([from_left, from_right], 1).astype(jnp.float32)
    from_below = shifted(total[:RADIUS].astype(jnp.bfloat16), "rows", -1)
    from_above = shifted(total[RADIUS + SIDE : 2 * RADIUS + SIDE].astype(jnp.bfloat16), "rows", 1)
    x_own, x_side, middle = lax.optimization_barrier((x_own, x_side, total[RADIUS : RADIUS + SIDE]))
    y_forward = attention_forward(x_own, x_side, w_qkv, w_out, q_forward, bias, first, SPLIT, heads, heads)

    gap = jnp.zeros((rows - RADIUS, cols, width), jnp.float32)
    dx = (
        middle
        + jnp.concatenate([from_above.astype(jnp.float32), gap], 0)
        + jnp.concatenate([gap, from_below.astype(jnp.float32)], 0)
    )
    return (y_forward.reshape(rows, cols, width), dx.astype(jnp.bfloat16))


def solution(mesh):
    spec = P("rows", "heads", None)
    return jax.shard_map(
        body, mesh=mesh, in_specs=(spec, spec, spec, P(), P()), out_specs=(spec, spec), check_vma=False
    )
```

```python
import functools
import math

import jax
import jax.numpy as jnp
from jax import lax
from jax.experimental import pallas as pl
from jax.experimental.pallas import tpu as pltpu
from jax.sharding import PartitionSpec as P

RADIUS = 7
SIDE = 16
LANES = 256
GROUP = 256
HALF = 128
SPAN = 3 * GROUP
KEYS = 4 * GROUP
NEG = -1e30
CHUNK = 16
SPLIT = 6
LIMIT = 40 * 2**20


def shifted(value, axis, step):
    count = lax.axis_size(axis)
    return lax.ppermute(value, axis, [(i, (i + step) % count) for i in range(count)])


def row_halos(x):
    return shifted(x[SIDE - RADIUS :], "rows", 1), x, shifted(x[:RADIUS], "rows", -1)


def side_columns(parts):
    zeros = jnp.zeros((2, 8) + parts[0].shape[2:], parts[0].dtype)
    left = shifted(jnp.concatenate([part[:, 8:] for part in parts] + [zeros], 0), "heads", 1)
    right = shifted(jnp.concatenate([part[:, :8] for part in parts] + [zeros], 0), "heads", -1)
    return jnp.concatenate([left, right], 1)


def window_bias():
    row_start = lax.axis_index("rows") * SIDE
    col_start = lax.axis_index("heads") * SIDE
    rows_total = lax.axis_size("rows") * SIDE
    cols_total = lax.axis_size("heads") * SIDE
    query = lax.broadcasted_iota(jnp.int32, (2 * HALF, SPAN), 0)
    place = lax.broadcasted_iota(jnp.int32, (2 * HALF, SPAN), 1)
    half = query // HALF
    query_row, query_col = query // SIDE, query % SIDE
    group, rest = place // GROUP + half, place % GROUP
    side, inner = rest // HALF, rest % HALF
    key_row, column = group * 8 + inner // SIDE, inner % SIDE
    key_col = jnp.where(side == 0, column, jnp.where(column < 8, column - 8, column + 8))
    image_row = row_start + key_row - RADIUS
    image_col = col_start + key_col
    row_gap, col_gap = key_row - query_row, key_col - query_col
    valid = (row_gap >= 0) & (row_gap <= 2 * RADIUS) & (col_gap >= -RADIUS) & (col_gap <= RADIUS)
    valid &= (image_row >= 0) & (image_row < rows_total) & (image_col >= 0) & (image_col < cols_total)
    return jnp.where(valid, 0.0, NEG).astype(jnp.float32)


def head_lanes(head, head_dim, width):
    tile = jnp.clip(head * head_dim // 128, 0, (width - LANES) // 128)
    offset = head * head_dim - tile * 128
    lane = lax.broadcasted_iota(jnp.int32, (1, LANES), 1)
    return tile * 128, (lane >= offset) & (lane < offset + head_dim)


def at_lanes(start):
    return pl.ds(pl.multiple_of(start, 128), LANES)


def fill_keys(x_parts, x_side, weights, starts, kv):
    skip = weights.shape[1] - kv.shape[1]
    sources = [(x_side, 0, HALF)]
    first = 0
    for x_ref in x_parts:
        sources.append((x_ref, first, 0))
        first += x_ref.shape[0]
    kv[GROUP * 3 + first % HALF : GROUP * 3 + HALF, :] = jnp.zeros((HALF - first % HALF, kv.shape[1]), kv.dtype)
    for start in starts:
        place = slice(start - skip, start - skip + GROUP)
        for x_ref, first, offset in sources:
            part = jnp.dot(x_ref[...], weights[:, start : start + GROUP], preferred_element_type=jnp.float32)
            part = part.astype(kv.dtype)
            low, end = first, first + x_ref.shape[0]
            while low < end:
                high = min(end, (low // HALF + 1) * HALF)
                row = low // HALF * GROUP + low % HALF + offset
                kv[row : row + high - low, place] = part[low - first : high - first]
                low = high


def turned(source, target):
    heads, head_dim, _ = target.shape
    flipped = jnp.transpose(source[...].astype(jnp.float32))
    for head in range(heads):
        target[head] = flipped[head * head_dim : (head + 1) * head_dim].astype(target.dtype)


def span_products(rows, kv, start, out_ref):
    def one(group):
        low = 0 if group < 3 else HALF
        high = 2 * HALF if group > 0 else HALF
        keys = kv[GROUP * group : GROUP * (group + 1), at_lanes(start)]
        part = lax.dot_general(
            rows[low:high], keys, (((1,), (1,)), ((), ())), preferred_element_type=jnp.float32
        )
        if group < 3:
            out_ref[:HALF, GROUP * group : GROUP * (group + 1)] = part[:HALF]
        if group > 0:
            out_ref[HALF:, GROUP * (group - 1) : GROUP * group] = part[-HALF:]

    return [functools.partial(one, group) for group in range(4)]


def interleave(*streams):
    marks = [((i + 0.5) / len(stream), n, step) for n, stream in enumerate(streams) for i, step in enumerate(stream)]
    for _, _, step in sorted(marks, key=lambda mark: mark[:2]):
        step()


def softmax_rows(scores, bias, factor):
    scores = scores + bias
    top = jnp.max(scores, axis=1, keepdims=True)
    terms = jnp.exp2((scores - top) * factor)
    return terms * (1.0 / jnp.sum(terms, axis=1, keepdims=True))


def span_of(rows):
    start = 0 if rows < HALF else GROUP
    return slice(start, start + SPAN)


def forward_kernel(
    head_dim, first, end, starts, last, above, own, below, x_side, weights, w_out, queries, bias, before, out_ref,
    kv, acc, scores0, scores1, probs0, probs1
):
    width = queries.shape[1]
    factor = head_dim**-0.5 * math.log2(math.e)
    scores, probs = (scores0, scores1), (probs0, probs1)
    acc[...] = before[...] if last else jnp.zeros_like(acc)
    for ref in probs:
        ref[...] = jnp.zeros_like(ref)
    fill_keys((above, own, below), x_side, weights, starts, kv)

    def scored(head, u):
        start, mask = head_lanes(head, head_dim, width)
        return span_products(jnp.where(mask, queries[:, at_lanes(start)], 0), kv, start, scores[u])

    def weighted(u):
        def one(rows):
            part = slice(rows, rows + CHUNK)
            attention = softmax_rows(scores[u][part, :], bias[part, :], factor)
            probs[u][part, span_of(rows)] = attention.astype(jnp.bfloat16)

        return [functools.partial(one, rows) for rows in range(0, 2 * HALF, CHUNK)]

    def mixed(head, u):
        start, mask = head_lanes(head, head_dim, width)

        def one():
            mix = jnp.dot(probs[u][...], kv[:, at_lanes(start + width)], preferred_element_type=jnp.float32)
            acc[:, at_lanes(start)] += jnp.where(mask & (head >= first), mix, 0.0)

        return [one]

    interleave(scored(first, 0))

    def pair(index, carry):
        head = first + 2 * index
        interleave(scored(head + 1, 1), weighted(0), mixed(head - 1, 1))
        interleave(scored(jnp.minimum(head + 2, end - 1), 0), weighted(1), mixed(head, 0))
        return carry

    lax.fori_loop(0, (end - first) // 2, pair, 0)
    interleave(mixed(end - 1, 1))
    if last:
        attended = acc[...].astype(jnp.bfloat16)
        out_ref[...] = jnp.dot(attended, w_out[...], preferred_element_type=jnp.float32).astype(out_ref.dtype)
    else:
        out_ref[...] = acc[...]


def backward_kernel(
    head_dim, starts, above, own, below, x_side, weights, queries, cotangents, bias, down_ref, dside_ref,
    queries_t, cotangents_t, kv, dkv, acc,
    scores0, scores1, grads0, grads1, probs0, probs1, dscores0, dscores1, held0, held1
):
    width = queries.shape[1]
    heads = width // head_dim
    scaling = head_dim**-0.5
    factor = scaling * math.log2(math.e)
    scores, grads, held = (scores0, scores1), (grads0, grads1), (held0, held1)
    probs, dscores = (probs0, probs1), (dscores0, dscores1)
    for ref in probs + dscores + held + (acc,):
        ref[...] = jnp.zeros_like(ref)
    turned(queries, queries_t)
    turned(cotangents, cotangents_t)
    fill_keys((above, own, below), x_side, weights, starts, kv)

    def scored(head, u):
        start, mask = head_lanes(head, head_dim, width)
        one = span_products(jnp.where(mask, queries[:, at_lanes(start)], 0), kv, start, scores[u])
        other = span_products(jnp.where(mask, cotangents[:, at_lanes(start)], 0), kv, start + width, grads[u])
        return [step for both in zip(one, other) for step in both]

    def weighted(u):
        def one(rows):
            part = slice(rows, rows + CHUNK)
            attention = softmax_rows(scores[u][part, :], bias[part, :], factor)
            grad = grads[u][part, :]
            centre = jnp.sum(attention * grad, axis=1, keepdims=True)
            probs[u][part, span_of(rows)] = attention.astype(jnp.bfloat16)
            dscores[u][part, span_of(rows)] = (attention * (grad - centre) * scaling).astype(jnp.bfloat16)

        return [functools.partial(one, rows) for rows in range(0, 2 * HALF, CHUNK)]

    def spread(head, u):
        start, mask = head_lanes(head, head_dim, width)
        row = jnp.maximum(head, 0)
        base = jnp.maximum(head - 1, 0) * head_dim

        def query_part():
            dq = jnp.dot(dscores[u][...], kv[:, at_lanes(start)], preferred_element_type=jnp.float32)
            acc[:, at_lanes(start)] += jnp.where(mask & (head >= 0), dq, 0.0)

        def key_part(index, group):
            source, spans = ((queries_t, dscores), (cotangents_t, probs))[index]
            place = slice(GROUP * group, GROUP * (group + 1))
            part = jnp.dot(source[row], spans[u][:, place], preferred_element_type=jnp.float32)
            if u == 0:
                held[index][:, place] = part
            else:
                both = jnp.concatenate([held[index][:, place], part], 0).astype(jnp.bfloat16)
                dkv[pl.ds(pl.multiple_of(base + index * width, 16), 2 * head_dim), place] = both

        parts = [functools.partial(key_part, index, group) for index in range(2) for group in range(4)]
        return parts[:4] + [query_part] + parts[4:]

    interleave(scored(0, 0))

    def pair(index, carry):
        head = 2 * index
        interleave(scored(head + 1, 1), weighted(0), spread(head - 1, 1))
        interleave(scored(jnp.minimum(head + 2, heads - 1), 0), weighted(1), spread(head, 0))
        return carry

    lax.fori_loop(0, heads // 2, pair, 0)
    interleave(spread(heads - 1, 1))

    for group in range(4):
        place = slice(GROUP * group, GROUP * (group + 1))
        part = jnp.dot(weights[:, width:], dkv[:, place], preferred_element_type=jnp.float32)
        rows = slice(HALF * group, HALF * (group + 1))
        down_ref[rows, :] = jnp.transpose(part[:, :HALF])
        dside_ref[rows, :] = jnp.transpose(part[:, HALF:]).astype(dside_ref.dtype)
    dx_query = lax.dot_general(
        acc[...].astype(jnp.bfloat16), weights[:, :width], (((1,), (1,)), ((), ())),
        preferred_element_type=jnp.float32,
    )
    mine = slice(RADIUS * SIDE, RADIUS * SIDE + 2 * HALF)
    down_ref[mine, :] += dx_query


def call_kernel(kernel, args, out_shape, scratch, flops, name):
    return pl.pallas_call(
        kernel,
        out_shape=out_shape,
        scratch_shapes=scratch,
        compiler_params=pltpu.CompilerParams(vmem_limit_bytes=LIMIT),
        cost_estimate=pl.CostEstimate(flops=flops, bytes_accessed=16 * 2**20, transcendentals=2**22),
        name=name,
    )(*args)


def attention_forward(x_parts, x_side, w_qkv, w_out, queries, bias, before, first, end, heads):
    tokens, width = queries.shape
    head_dim = width // heads
    last = before is not None
    low = first * head_dim // 128 * 128
    high = low - (low - end * head_dim) // GROUP * GROUP
    if high > width:
        low, high = low - (high - width), width
    starts = [part * width + at for part in (1, 2) for at in range(low, high, GROUP)]
    half, full = jnp.bfloat16, jnp.float32
    square = (tokens, SPAN)
    scratch = [
        pltpu.VMEM((KEYS, 2 * width), half),
        pltpu.VMEM((tokens, width), full),
    ]
    scratch += [pltpu.VMEM(square, full)] * 2 + [pltpu.VMEM((tokens, KEYS), half)] * 2
    return call_kernel(
        functools.partial(forward_kernel, head_dim, first, end, starts, last),
        [*x_parts, x_side, w_qkv, w_out, queries, bias, before if last else queries],
        jax.ShapeDtypeStruct(queries.shape, half if last else full),
        scratch,
        2 * KEYS * width * GROUP * len(starts) + 4 * (end - first) * tokens * KEYS * LANES,
        "attention_forward",
    )


def attention_backward(x_parts, x_side, w_qkv, queries, cotangents, bias, heads):
    tokens, width = queries.shape
    head_dim = width // heads
    square = (tokens, SPAN)
    half, full = jnp.bfloat16, jnp.float32
    starts = list(range(width, 3 * width, GROUP))
    by_head = (heads, head_dim, tokens)
    args = [*x_parts, x_side, w_qkv, queries, cotangents, bias]
    scratch = [
        pltpu.VMEM(by_head, half),
        pltpu.VMEM(by_head, half),
        pltpu.VMEM((KEYS, 2 * width), half),
        pltpu.VMEM((2 * width, KEYS), half),
        pltpu.VMEM((tokens, width), full),
    ]
    scratch += [pltpu.VMEM(square, full)] * 4 + [pltpu.VMEM((tokens, KEYS), half)] * 4
    scratch += [pltpu.VMEM((head_dim, KEYS), full)] * 2
    return call_kernel(
        functools.partial(backward_kernel, head_dim, starts),
        args,
        [jax.ShapeDtypeStruct((KEYS // 2, width), full), jax.ShapeDtypeStruct((KEYS // 2, width), half)],
        scratch,
        8 * KEYS * width * width + 10 * heads * tokens * KEYS * LANES,
        "attention_backward",
    )


def project(x, w):
    return jnp.dot(x, w, preferred_element_type=jnp.float32).astype(jnp.bfloat16)


def body(x_forward, x_backward, grad_out, w_qkv, w_out):
    rows, cols, width = x_forward.shape
    heads = lax.axis_size("heads")
    w_q = w_qkv[:, :width]
    flat = lambda x: x.reshape(-1, width)
    bias = window_bias()

    parts_backward = row_halos(x_backward)
    q_backward = project(flat(x_backward), w_q)
    x_forward, q_backward = lax.optimization_barrier((x_forward, q_backward))
    parts_forward = row_halos(x_forward)
    side_backward = flat(side_columns(parts_backward))
    side_forward = flat(side_columns(parts_forward))
    grad_heads = lax.dot_general(
        flat(grad_out), w_out, (((1,), (1,)), ((), ())), preferred_element_type=jnp.float32
    ).astype(jnp.bfloat16)
    q_forward = project(flat(x_forward), w_q)
    parts_backward = [flat(part) for part in parts_backward]
    parts_forward = [flat(part) for part in parts_forward]

    dx_own, dx_side = attention_backward(
        parts_backward, side_backward, w_qkv, q_backward, grad_heads, bias, heads
    )
    dx_own = dx_own.reshape(2 * SIDE, SIDE, width)
    dx_side = dx_side.reshape(2 * SIDE, SIDE, width)
    from_right = shifted(dx_side[:, :8], "heads", -1)
    from_left = shifted(dx_side[:, 8:], "heads", 1)

    side_forward, _ = lax.optimization_barrier((side_forward, dx_side))
    first = attention_forward(parts_forward, side_forward, w_qkv, w_out, q_forward, bias, None, 0, SPLIT, heads)
    from_left, from_right, first = lax.optimization_barrier((from_left, from_right, first))
    total = dx_own + jnp.concatenate([from_left, from_right], 1).astype(jnp.float32)
    from_below = shifted(total[:RADIUS].astype(jnp.bfloat16), "rows", -1)
    from_above = shifted(total[RADIUS + SIDE : 2 * RADIUS + SIDE].astype(jnp.bfloat16), "rows", 1)
    side_forward, middle = lax.optimization_barrier((side_forward, total[RADIUS : RADIUS + SIDE]))
    y_forward = attention_forward(
        parts_forward, side_forward, w_qkv, w_out, q_forward, bias, first, SPLIT, heads, heads
    )

    gap = jnp.zeros((rows - RADIUS, cols, width), jnp.float32)
    dx = (
        middle
        + jnp.concatenate([from_above.astype(jnp.float32), gap], 0)
        + jnp.concatenate([gap, from_below.astype(jnp.float32)], 0)
    )
    return (y_forward.reshape(rows, cols, width), dx.astype(jnp.bfloat16))


def solution(mesh):
    spec = P("rows", "heads", None)
    return jax.shard_map(
        body, mesh=mesh, in_specs=(spec, spec, spec, P(), P()), out_specs=(spec, spec), check_vma=False
    )
```

```python
import functools
import math

import jax
import jax.numpy as jnp
from jax import lax
from jax.experimental import pallas as pl
from jax.experimental.pallas import tpu as pltpu
from jax.sharding import PartitionSpec as P

RADIUS = 7
SIDE = 16
LANES = 256
GROUP = 256
HALF = 128
SPAN = 3 * GROUP
KEYS = 4 * GROUP
NEG = -1e30
CHUNK = 16
SPLIT = 6
LIMIT = 40 * 2**20


def shifted(value, axis, step):
    count = lax.axis_size(axis)
    return lax.ppermute(value, axis, [(i, (i + step) % count) for i in range(count)])


def row_halos(x):
    return shifted(x[SIDE - RADIUS :], "rows", 1), x, shifted(x[:RADIUS], "rows", -1)


def column_sends(parts):
    zeros = jnp.zeros((2, 8) + parts[0].shape[2:], parts[0].dtype)
    return [jnp.concatenate([part[:, side] for part in parts] + [zeros], 0) for side in (slice(8, 16), slice(0, 8))]


def side_columns(sends):
    return jnp.concatenate([shifted(sends[0], "heads", 1), shifted(sends[1], "heads", -1)], 1)


def window_bias():
    row_start = lax.axis_index("rows") * SIDE
    col_start = lax.axis_index("heads") * SIDE
    rows_total = lax.axis_size("rows") * SIDE
    cols_total = lax.axis_size("heads") * SIDE
    query = lax.broadcasted_iota(jnp.int32, (2 * HALF, SPAN), 0)
    place = lax.broadcasted_iota(jnp.int32, (2 * HALF, SPAN), 1)
    half = query // HALF
    query_row, query_col = query // SIDE, query % SIDE
    group, rest = place // GROUP + half, place % GROUP
    side, inner = rest // HALF, rest % HALF
    key_row, column = group * 8 + inner // SIDE, inner % SIDE
    key_col = jnp.where(side == 0, column, jnp.where(column < 8, column - 8, column + 8))
    image_row = row_start + key_row - RADIUS
    image_col = col_start + key_col
    row_gap, col_gap = key_row - query_row, key_col - query_col
    valid = (row_gap >= 0) & (row_gap <= 2 * RADIUS) & (col_gap >= -RADIUS) & (col_gap <= RADIUS)
    valid &= (image_row >= 0) & (image_row < rows_total) & (image_col >= 0) & (image_col < cols_total)
    return jnp.where(valid, 0.0, NEG).astype(jnp.float32)


def head_lanes(head, head_dim, width):
    tile = jnp.clip(head * head_dim // 128, 0, (width - LANES) // 128)
    offset = head * head_dim - tile * 128
    lane = lax.broadcasted_iota(jnp.int32, (1, LANES), 1)
    return tile * 128, (lane >= offset) & (lane < offset + head_dim)


def at_lanes(start):
    return pl.ds(pl.multiple_of(start, 128), LANES)


def fill_keys(x_parts, x_side, weights, starts, kv):
    skip = weights.shape[1] - kv.shape[1]
    sources = [(x_side, 0, HALF)]
    first = 0
    for x_ref in x_parts:
        sources.append((x_ref, first, 0))
        first += x_ref.shape[0]
    kv[GROUP * 3 + first % HALF : GROUP * 3 + HALF, :] = jnp.zeros((HALF - first % HALF, kv.shape[1]), kv.dtype)
    for start in starts:
        place = slice(start - skip, start - skip + GROUP)
        for x_ref, first, offset in sources:
            part = jnp.dot(x_ref[...], weights[:, start : start + GROUP], preferred_element_type=jnp.float32)
            part = part.astype(kv.dtype)
            low, end = first, first + x_ref.shape[0]
            while low < end:
                high = min(end, (low // HALF + 1) * HALF)
                row = low // HALF * GROUP + low % HALF + offset
                kv[row : row + high - low, place] = part[low - first : high - first]
                low = high


def turned(source, target):
    heads, head_dim, _ = target.shape
    flipped = jnp.transpose(source[...].astype(jnp.float32))
    for head in range(heads):
        target[head] = flipped[head * head_dim : (head + 1) * head_dim].astype(target.dtype)


def span_products(rows, kv, start, out_ref):
    def one(group):
        low = 0 if group < 3 else HALF
        high = 2 * HALF if group > 0 else HALF
        keys = kv[GROUP * group : GROUP * (group + 1), at_lanes(start)]
        part = lax.dot_general(
            rows[low:high], keys, (((1,), (1,)), ((), ())), preferred_element_type=jnp.float32
        )
        if group < 3:
            out_ref[:HALF, GROUP * group : GROUP * (group + 1)] = part[:HALF]
        if group > 0:
            out_ref[HALF:, GROUP * (group - 1) : GROUP * group] = part[-HALF:]

    return [functools.partial(one, group) for group in range(4)]


def interleave(*streams):
    marks = [((i + 0.5) / len(stream), n, step) for n, stream in enumerate(streams) for i, step in enumerate(stream)]
    for _, _, step in sorted(marks, key=lambda mark: mark[:2]):
        step()


def softmax_rows(scores, bias, factor):
    scores = scores + bias
    top = jnp.max(scores, axis=1, keepdims=True)
    terms = jnp.exp2((scores - top) * factor)
    return terms * (1.0 / jnp.sum(terms, axis=1, keepdims=True))


def span_of(rows):
    start = 0 if rows < HALF else GROUP
    return slice(start, start + SPAN)


def forward_kernel(
    head_dim, first, end, starts, last, above, own, below, x_side, weights, w_out, queries, bias, before, out_ref,
    kv, acc, scores0, scores1, probs0, probs1
):
    width = queries.shape[1]
    factor = head_dim**-0.5 * math.log2(math.e)
    scores, probs = (scores0, scores1), (probs0, probs1)
    acc[...] = before[...] if last else jnp.zeros_like(acc)
    for ref in probs:
        ref[...] = jnp.zeros_like(ref)
    fill_keys((above, own, below), x_side, weights, starts, kv)

    def scored(head, u):
        start, mask = head_lanes(head, head_dim, width)
        return span_products(jnp.where(mask, queries[:, at_lanes(start)], 0), kv, start, scores[u])

    def weighted(u):
        def one(rows):
            part = slice(rows, rows + CHUNK)
            attention = softmax_rows(scores[u][part, :], bias[part, :], factor)
            probs[u][part, span_of(rows)] = attention.astype(jnp.bfloat16)

        return [functools.partial(one, rows) for rows in range(0, 2 * HALF, CHUNK)]

    def mixed(head, u):
        start, mask = head_lanes(head, head_dim, width)

        def one():
            mix = jnp.dot(probs[u][...], kv[:, at_lanes(start + width)], preferred_element_type=jnp.float32)
            acc[:, at_lanes(start)] += jnp.where(mask & (head >= first), mix, 0.0)

        return [one]

    interleave(scored(first, 0))

    def pair(index, carry):
        head = first + 2 * index
        interleave(scored(head + 1, 1), weighted(0), mixed(head - 1, 1))
        interleave(scored(jnp.minimum(head + 2, end - 1), 0), weighted(1), mixed(head, 0))
        return carry

    lax.fori_loop(0, (end - first) // 2, pair, 0)
    interleave(mixed(end - 1, 1))
    if last:
        attended = acc[...].astype(jnp.bfloat16)
        out_ref[...] = jnp.dot(attended, w_out[...], preferred_element_type=jnp.float32).astype(out_ref.dtype)
    else:
        out_ref[...] = acc[...]


def backward_kernel(
    head_dim, starts, above, own, below, x_side, weights, queries, cotangents, bias, down_ref, dside_ref,
    queries_t, cotangents_t, kv, dkv, acc,
    scores0, scores1, grads0, grads1, probs0, probs1, dscores0, dscores1, held0, held1
):
    width = queries.shape[1]
    heads = width // head_dim
    scaling = head_dim**-0.5
    factor = scaling * math.log2(math.e)
    scores, grads, held = (scores0, scores1), (grads0, grads1), (held0, held1)
    probs, dscores = (probs0, probs1), (dscores0, dscores1)
    for ref in probs + dscores + held + (acc,):
        ref[...] = jnp.zeros_like(ref)
    turned(queries, queries_t)
    turned(cotangents, cotangents_t)
    fill_keys((above, own, below), x_side, weights, starts, kv)

    def scored(head, u):
        start, mask = head_lanes(head, head_dim, width)
        one = span_products(jnp.where(mask, queries[:, at_lanes(start)], 0), kv, start, scores[u])
        other = span_products(jnp.where(mask, cotangents[:, at_lanes(start)], 0), kv, start + width, grads[u])
        return [step for both in zip(one, other) for step in both]

    def weighted(u):
        def one(rows):
            part = slice(rows, rows + CHUNK)
            attention = softmax_rows(scores[u][part, :], bias[part, :], factor)
            grad = grads[u][part, :]
            centre = jnp.sum(attention * grad, axis=1, keepdims=True)
            probs[u][part, span_of(rows)] = attention.astype(jnp.bfloat16)
            dscores[u][part, span_of(rows)] = (attention * (grad - centre) * scaling).astype(jnp.bfloat16)

        return [functools.partial(one, rows) for rows in range(0, 2 * HALF, CHUNK)]

    def spread(head, u):
        start, mask = head_lanes(head, head_dim, width)
        row = jnp.maximum(head, 0)
        base = jnp.maximum(head - 1, 0) * head_dim

        def query_part():
            dq = jnp.dot(dscores[u][...], kv[:, at_lanes(start)], preferred_element_type=jnp.float32)
            acc[:, at_lanes(start)] += jnp.where(mask & (head >= 0), dq, 0.0)

        def key_part(index, group):
            source, spans = ((queries_t, dscores), (cotangents_t, probs))[index]
            place = slice(GROUP * group, GROUP * (group + 1))
            part = jnp.dot(source[row], spans[u][:, place], preferred_element_type=jnp.float32)
            if u == 0:
                held[index][:, place] = part
            else:
                both = jnp.concatenate([held[index][:, place], part], 0).astype(jnp.bfloat16)
                dkv[pl.ds(pl.multiple_of(base + index * width, 16), 2 * head_dim), place] = both

        parts = [functools.partial(key_part, index, group) for index in range(2) for group in range(4)]
        return parts[:4] + [query_part] + parts[4:]

    interleave(scored(0, 0))

    def pair(index, carry):
        head = 2 * index
        interleave(scored(head + 1, 1), weighted(0), spread(head - 1, 1))
        interleave(scored(jnp.minimum(head + 2, heads - 1), 0), weighted(1), spread(head, 0))
        return carry

    lax.fori_loop(0, heads // 2, pair, 0)
    interleave(spread(heads - 1, 1))

    for group in range(4):
        place = slice(GROUP * group, GROUP * (group + 1))
        part = jnp.dot(weights[:, width:], dkv[:, place], preferred_element_type=jnp.float32)
        rows = slice(HALF * group, HALF * (group + 1))
        down_ref[rows, :] = jnp.transpose(part[:, :HALF])
        dside_ref[rows, :] = jnp.transpose(part[:, HALF:]).astype(dside_ref.dtype)
    dx_query = lax.dot_general(
        acc[...].astype(jnp.bfloat16), weights[:, :width], (((1,), (1,)), ((), ())),
        preferred_element_type=jnp.float32,
    )
    mine = slice(RADIUS * SIDE, RADIUS * SIDE + 2 * HALF)
    down_ref[mine, :] += dx_query


def call_kernel(kernel, args, out_shape, scratch, flops, name):
    return pl.pallas_call(
        kernel,
        out_shape=out_shape,
        scratch_shapes=scratch,
        compiler_params=pltpu.CompilerParams(vmem_limit_bytes=LIMIT),
        cost_estimate=pl.CostEstimate(flops=flops, bytes_accessed=16 * 2**20, transcendentals=2**22),
        name=name,
    )(*args)


def attention_forward(x_parts, x_side, w_qkv, w_out, queries, bias, before, first, end, heads):
    tokens, width = queries.shape
    head_dim = width // heads
    last = before is not None
    low = first * head_dim // 128 * 128
    high = low - (low - end * head_dim) // GROUP * GROUP
    if high > width:
        low, high = low - (high - width), width
    starts = [part * width + at for part in (1, 2) for at in range(low, high, GROUP)]
    half, full = jnp.bfloat16, jnp.float32
    square = (tokens, SPAN)
    scratch = [
        pltpu.VMEM((KEYS, 2 * width), half),
        pltpu.VMEM((tokens, width), full),
    ]
    scratch += [pltpu.VMEM(square, full)] * 2 + [pltpu.VMEM((tokens, KEYS), half)] * 2
    return call_kernel(
        functools.partial(forward_kernel, head_dim, first, end, starts, last),
        [*x_parts, x_side, w_qkv, w_out, queries, bias, before if last else queries],
        jax.ShapeDtypeStruct(queries.shape, half if last else full),
        scratch,
        2 * KEYS * width * GROUP * len(starts) + 4 * (end - first) * tokens * KEYS * LANES,
        "attention_forward",
    )


def attention_backward(x_parts, x_side, w_qkv, queries, cotangents, bias, heads):
    tokens, width = queries.shape
    head_dim = width // heads
    square = (tokens, SPAN)
    half, full = jnp.bfloat16, jnp.float32
    starts = list(range(width, 3 * width, GROUP))
    by_head = (heads, head_dim, tokens)
    args = [*x_parts, x_side, w_qkv, queries, cotangents, bias]
    scratch = [
        pltpu.VMEM(by_head, half),
        pltpu.VMEM(by_head, half),
        pltpu.VMEM((KEYS, 2 * width), half),
        pltpu.VMEM((2 * width, KEYS), half),
        pltpu.VMEM((tokens, width), full),
    ]
    scratch += [pltpu.VMEM(square, full)] * 4 + [pltpu.VMEM((tokens, KEYS), half)] * 4
    scratch += [pltpu.VMEM((head_dim, KEYS), full)] * 2
    return call_kernel(
        functools.partial(backward_kernel, head_dim, starts),
        args,
        [jax.ShapeDtypeStruct((KEYS // 2, width), full), jax.ShapeDtypeStruct((KEYS // 2, width), half)],
        scratch,
        8 * KEYS * width * width + 10 * heads * tokens * KEYS * LANES,
        "attention_backward",
    )


def project(x, w):
    return jnp.dot(x, w, preferred_element_type=jnp.float32).astype(jnp.bfloat16)


def body(x_forward, x_backward, grad_out, w_qkv, w_out):
    rows, cols, width = x_forward.shape
    heads = lax.axis_size("heads")
    w_q = w_qkv[:, :width]
    flat = lambda x: x.reshape(-1, width)
    bias = window_bias()

    parts_backward = row_halos(x_backward)
    q_backward = project(flat(x_backward), w_q)
    x_forward, q_backward = lax.optimization_barrier((x_forward, q_backward))
    parts_forward = row_halos(x_forward)
    sends_backward = column_sends(parts_backward)
    side_backward = flat(side_columns(sends_backward))
    parts_forward, _ = lax.optimization_barrier((parts_forward, sends_backward))
    side_forward = flat(side_columns(column_sends(parts_forward)))
    grad_heads = lax.dot_general(
        flat(grad_out), w_out, (((1,), (1,)), ((), ())), preferred_element_type=jnp.float32
    ).astype(jnp.bfloat16)
    q_forward = project(flat(x_forward), w_q)
    parts_backward = [flat(part) for part in parts_backward]
    parts_forward = [flat(part) for part in parts_forward]

    dx_own, dx_side = attention_backward(
        parts_backward, side_backward, w_qkv, q_backward, grad_heads, bias, heads
    )
    dx_own = dx_own.reshape(2 * SIDE, SIDE, width)
    dx_side = dx_side.reshape(2 * SIDE, SIDE, width)
    from_right = shifted(dx_side[:, :8], "heads", -1)
    from_left = shifted(dx_side[:, 8:], "heads", 1)

    side_forward, _ = lax.optimization_barrier((side_forward, dx_side))
    first = attention_forward(parts_forward, side_forward, w_qkv, w_out, q_forward, bias, None, 0, SPLIT, heads)
    from_left, from_right, first = lax.optimization_barrier((from_left, from_right, first))
    total = dx_own + jnp.concatenate([from_left, from_right], 1).astype(jnp.float32)
    from_below = shifted(total[:RADIUS].astype(jnp.bfloat16), "rows", -1)
    from_above = shifted(total[RADIUS + SIDE : 2 * RADIUS + SIDE].astype(jnp.bfloat16), "rows", 1)
    side_forward, middle = lax.optimization_barrier((side_forward, total[RADIUS : RADIUS + SIDE]))
    y_forward = attention_forward(
        parts_forward, side_forward, w_qkv, w_out, q_forward, bias, first, SPLIT, heads, heads
    )

    gap = jnp.zeros((rows - RADIUS, cols, width), jnp.float32)
    dx = (
        middle
        + jnp.concatenate([from_above.astype(jnp.float32), gap], 0)
        + jnp.concatenate([gap, from_below.astype(jnp.float32)], 0)
    )
    return (y_forward.reshape(rows, cols, width), dx.astype(jnp.bfloat16))


def solution(mesh):
    spec = P("rows", "heads", None)
    return jax.shard_map(
        body, mesh=mesh, in_specs=(spec, spec, spec, P(), P()), out_specs=(spec, spec), check_vma=False
    )
```

```python
import functools
import math

import jax
import jax.numpy as jnp
from jax import lax
from jax.experimental import pallas as pl
from jax.experimental.pallas import tpu as pltpu
from jax.sharding import PartitionSpec as P

RADIUS = 7
SIDE = 16
LANES = 256
GROUP = 256
HALF = 128
SPAN = 3 * GROUP
KEYS = 4 * GROUP
NEG = -1e30
CHUNK = 16
LIMIT = 40 * 2**20


def shifted(value, axis, step):
    count = lax.axis_size(axis)
    return lax.ppermute(value, axis, [(i, (i + step) % count) for i in range(count)])


def row_halos(x):
    return shifted(x[SIDE - RADIUS :], "rows", 1), x, shifted(x[:RADIUS], "rows", -1)


def column_sends(parts):
    zeros = jnp.zeros((2, 8) + parts[0].shape[2:], parts[0].dtype)
    return [jnp.concatenate([part[:, side] for part in parts] + [zeros], 0) for side in (slice(8, 16), slice(0, 8))]


def side_columns(sends):
    return jnp.concatenate([shifted(sends[0], "heads", 1), shifted(sends[1], "heads", -1)], 1)


def window_bias():
    row_start = lax.axis_index("rows") * SIDE
    col_start = lax.axis_index("heads") * SIDE
    rows_total = lax.axis_size("rows") * SIDE
    cols_total = lax.axis_size("heads") * SIDE
    query = lax.broadcasted_iota(jnp.int32, (2 * HALF, SPAN), 0)
    place = lax.broadcasted_iota(jnp.int32, (2 * HALF, SPAN), 1)
    half = query // HALF
    query_row, query_col = query // SIDE, query % SIDE
    group, rest = place // GROUP + half, place % GROUP
    side, inner = rest // HALF, rest % HALF
    key_row, column = group * 8 + inner // SIDE, inner % SIDE
    key_col = jnp.where(side == 0, column, jnp.where(column < 8, column - 8, column + 8))
    image_row = row_start + key_row - RADIUS
    image_col = col_start + key_col
    row_gap, col_gap = key_row - query_row, key_col - query_col
    valid = (row_gap >= 0) & (row_gap <= 2 * RADIUS) & (col_gap >= -RADIUS) & (col_gap <= RADIUS)
    valid &= (image_row >= 0) & (image_row < rows_total) & (image_col >= 0) & (image_col < cols_total)
    return jnp.where(valid, 0.0, NEG).astype(jnp.float32)


def head_lanes(head, head_dim, width):
    tile = jnp.clip(head * head_dim // 128, 0, (width - LANES) // 128)
    offset = head * head_dim - tile * 128
    lane = lax.broadcasted_iota(jnp.int32, (1, LANES), 1)
    return tile * 128, (lane >= offset) & (lane < offset + head_dim)


def at_lanes(start):
    return pl.ds(pl.multiple_of(start, 128), LANES)


def own_keys_kernel(above, own, below, weights, out_ref):
    skip = weights.shape[1] - out_ref.shape[1]
    for start in range(0, out_ref.shape[1], GROUP):
        low = 0
        for x_ref in (above, own, below):
            part = jnp.dot(
                x_ref[...], weights[:, skip + start : skip + start + GROUP], preferred_element_type=jnp.float32
            )
            out_ref[low : low + x_ref.shape[0], start : start + GROUP] = part.astype(out_ref.dtype)
            low += x_ref.shape[0]
        out_ref[low:, start : start + GROUP] = jnp.zeros((out_ref.shape[0] - low, GROUP), out_ref.dtype)


def own_gradient_kernel(dkv, dq, weights, out_ref):
    width = dq.shape[1]
    for start in range(0, out_ref.shape[0], GROUP):
        part = jnp.dot(weights[:, width:], dkv[:, start : start + GROUP], preferred_element_type=jnp.float32)
        out_ref[start : start + GROUP, :] = jnp.transpose(part)
    mine = slice(RADIUS * SIDE, RADIUS * SIDE + dq.shape[0])
    out_ref[mine, :] += lax.dot_general(
        dq[...], weights[:, :width], (((1,), (1,)), ((), ())), preferred_element_type=jnp.float32
    )


def fill_keys(kv_own, x_side, weights, kv):
    skip = weights.shape[1] - kv.shape[1]
    for group in range(4):
        kv[GROUP * group : GROUP * group + HALF, :] = kv_own[HALF * group : HALF * (group + 1), :]
    for start in range(0, kv.shape[1], GROUP):
        part = jnp.dot(
            x_side[...], weights[:, skip + start : skip + start + GROUP], preferred_element_type=jnp.float32
        ).astype(kv.dtype)
        for group in range(4):
            low = GROUP * group + HALF
            kv[low : low + HALF, start : start + GROUP] = part[HALF * group : HALF * (group + 1)]


def turned(source, target):
    heads, head_dim, _ = target.shape
    flipped = jnp.transpose(source[...].astype(jnp.float32))
    for head in range(heads):
        target[head] = flipped[head * head_dim : (head + 1) * head_dim].astype(target.dtype)


def span_products(rows, kv, start, out_ref):
    def one(group):
        low = 0 if group < 3 else HALF
        high = 2 * HALF if group > 0 else HALF
        keys = kv[GROUP * group : GROUP * (group + 1), at_lanes(start)]
        part = lax.dot_general(
            rows[low:high], keys, (((1,), (1,)), ((), ())), preferred_element_type=jnp.float32
        )
        if group < 3:
            out_ref[:HALF, GROUP * group : GROUP * (group + 1)] = part[:HALF]
        if group > 0:
            out_ref[HALF:, GROUP * (group - 1) : GROUP * group] = part[-HALF:]

    return [functools.partial(one, group) for group in range(4)]


def interleave(*streams):
    marks = [((i + 0.5) / len(stream), n, step) for n, stream in enumerate(streams) for i, step in enumerate(stream)]
    for _, _, step in sorted(marks, key=lambda mark: mark[:2]):
        step()


def softmax_rows(scores, bias, factor):
    scores = scores + bias
    top = jnp.max(scores, axis=1, keepdims=True)
    terms = jnp.exp2((scores - top) * factor)
    return terms * (1.0 / jnp.sum(terms, axis=1, keepdims=True))


def span_of(rows):
    start = 0 if rows < HALF else GROUP
    return slice(start, start + SPAN)


def forward_kernel(
    head_dim, kv_own, x_side, weights, w_out, queries, bias, out_ref, kv, acc, scores0, scores1, probs0, probs1
):
    width = queries.shape[1]
    heads = width // head_dim
    factor = head_dim**-0.5 * math.log2(math.e)
    scores, probs = (scores0, scores1), (probs0, probs1)
    for ref in probs + (acc,):
        ref[...] = jnp.zeros_like(ref)
    fill_keys(kv_own, x_side, weights, kv)

    def scored(head, u):
        start, mask = head_lanes(head, head_dim, width)
        return span_products(jnp.where(mask, queries[:, at_lanes(start)], 0), kv, start, scores[u])

    def weighted(u):
        def one(rows):
            part = slice(rows, rows + CHUNK)
            attention = softmax_rows(scores[u][part, :], bias[part, :], factor)
            probs[u][part, span_of(rows)] = attention.astype(jnp.bfloat16)

        return [functools.partial(one, rows) for rows in range(0, 2 * HALF, CHUNK)]

    def mixed(head, u):
        start, mask = head_lanes(head, head_dim, width)

        def one():
            mix = jnp.dot(probs[u][...], kv[:, at_lanes(start + width)], preferred_element_type=jnp.float32)
            acc[:, at_lanes(start)] += jnp.where(mask & (head >= 0), mix, 0.0)

        return [one]

    interleave(scored(0, 0))

    def pair(index, carry):
        head = 2 * index
        interleave(scored(head + 1, 1), weighted(0), mixed(head - 1, 1))
        interleave(scored(jnp.minimum(head + 2, heads - 1), 0), weighted(1), mixed(head, 0))
        return carry

    lax.fori_loop(0, heads // 2, pair, 0)
    interleave(mixed(heads - 1, 1))
    attended = acc[...].astype(jnp.bfloat16)
    out_ref[...] = jnp.dot(attended, w_out[...], preferred_element_type=jnp.float32).astype(out_ref.dtype)


def backward_kernel(
    head_dim, kv_own, x_side, weights, queries, cotangents, bias, down_ref, dq_ref, dside_ref,
    queries_t, cotangents_t, kv, dkv, acc,
    scores0, scores1, grads0, grads1, probs0, probs1, dscores0, dscores1, held0, held1
):
    width = queries.shape[1]
    heads = width // head_dim
    scaling = head_dim**-0.5
    factor = scaling * math.log2(math.e)
    scores, grads, held = (scores0, scores1), (grads0, grads1), (held0, held1)
    probs, dscores = (probs0, probs1), (dscores0, dscores1)
    for ref in probs + dscores + held + (acc,):
        ref[...] = jnp.zeros_like(ref)
    turned(queries, queries_t)
    turned(cotangents, cotangents_t)
    fill_keys(kv_own, x_side, weights, kv)

    def scored(head, u):
        start, mask = head_lanes(head, head_dim, width)
        one = span_products(jnp.where(mask, queries[:, at_lanes(start)], 0), kv, start, scores[u])
        other = span_products(jnp.where(mask, cotangents[:, at_lanes(start)], 0), kv, start + width, grads[u])
        return [step for both in zip(one, other) for step in both]

    def weighted(u):
        def one(rows):
            part = slice(rows, rows + CHUNK)
            attention = softmax_rows(scores[u][part, :], bias[part, :], factor)
            grad = grads[u][part, :]
            centre = jnp.sum(attention * grad, axis=1, keepdims=True)
            probs[u][part, span_of(rows)] = attention.astype(jnp.bfloat16)
            dscores[u][part, span_of(rows)] = (attention * (grad - centre) * scaling).astype(jnp.bfloat16)

        return [functools.partial(one, rows) for rows in range(0, 2 * HALF, CHUNK)]

    def spread(head, u):
        start, mask = head_lanes(head, head_dim, width)
        row = jnp.maximum(head, 0)
        base = jnp.maximum(head - 1, 0) * head_dim

        def query_part():
            dq = jnp.dot(dscores[u][...], kv[:, at_lanes(start)], preferred_element_type=jnp.float32)
            acc[:, at_lanes(start)] += jnp.where(mask & (head >= 0), dq, 0.0)

        def key_part(index, group):
            source, spans = ((queries_t, dscores), (cotangents_t, probs))[index]
            place = slice(GROUP * group, GROUP * (group + 1))
            part = jnp.dot(source[row], spans[u][:, place], preferred_element_type=jnp.float32)
            if u == 0:
                held[index][:, place] = part
            else:
                both = jnp.concatenate([held[index][:, place], part], 0).astype(jnp.bfloat16)
                rows = pl.ds(pl.multiple_of(base + index * width, 16), 2 * head_dim)
                place = slice(HALF * group, HALF * (group + 1))
                down_ref[rows, place] = both[:, :HALF]
                dkv[rows, place] = both[:, HALF:]

        parts = [functools.partial(key_part, index, group) for index in range(2) for group in range(4)]
        return parts[:4] + [query_part] + parts[4:]

    interleave(scored(0, 0))

    def pair(index, carry):
        head = 2 * index
        interleave(scored(head + 1, 1), weighted(0), spread(head - 1, 1))
        interleave(scored(jnp.minimum(head + 2, heads - 1), 0), weighted(1), spread(head, 0))
        return carry

    lax.fori_loop(0, heads // 2, pair, 0)
    interleave(spread(heads - 1, 1))

    dq_ref[...] = acc[...].astype(dq_ref.dtype)
    for start in range(0, dside_ref.shape[0], GROUP):
        part = jnp.dot(weights[:, width:], dkv[:, start : start + GROUP], preferred_element_type=jnp.float32)
        dside_ref[start : start + GROUP, :] = jnp.transpose(part).astype(dside_ref.dtype)


def call_kernel(kernel, args, out_shape, scratch, flops, name):
    return pl.pallas_call(
        kernel,
        out_shape=out_shape,
        scratch_shapes=scratch,
        compiler_params=pltpu.CompilerParams(vmem_limit_bytes=LIMIT),
        cost_estimate=pl.CostEstimate(flops=flops, bytes_accessed=16 * 2**20, transcendentals=2**22),
        name=name,
    )(*args)


def own_keys(x_parts, w_qkv):
    width, columns = w_qkv.shape
    out_shape = jax.ShapeDtypeStruct((KEYS // 2, columns - width), jnp.bfloat16)
    return call_kernel(own_keys_kernel, [*x_parts, w_qkv], out_shape, [], 2 * KEYS * width * width, "own_keys")


def own_gradient(dkv, dq, w_qkv):
    out_shape = jax.ShapeDtypeStruct((KEYS // 2, dq.shape[1]), jnp.float32)
    flops = 2 * KEYS * dq.shape[1] ** 2
    return call_kernel(own_gradient_kernel, [dkv, dq, w_qkv], out_shape, [], flops, "own_gradient")


def attention_forward(kv_own, x_side, w_qkv, w_out, queries, bias, heads):
    tokens, width = queries.shape
    half, full = jnp.bfloat16, jnp.float32
    square = (tokens, SPAN)
    scratch = [pltpu.VMEM((KEYS, 2 * width), half), pltpu.VMEM((tokens, width), full)]
    scratch += [pltpu.VMEM(square, full)] * 2 + [pltpu.VMEM((tokens, KEYS), half)] * 2
    return call_kernel(
        functools.partial(forward_kernel, width // heads),
        [kv_own, x_side, w_qkv, w_out, queries, bias],
        jax.ShapeDtypeStruct(queries.shape, half),
        scratch,
        2 * KEYS * width * width + 4 * heads * tokens * KEYS * LANES,
        "attention_forward",
    )


def attention_backward(kv_own, x_side, w_qkv, queries, cotangents, bias, heads):
    tokens, width = queries.shape
    head_dim = width // heads
    square = (tokens, SPAN)
    half, full = jnp.bfloat16, jnp.float32
    by_head = (heads, head_dim, tokens)
    scratch = [
        pltpu.VMEM(by_head, half),
        pltpu.VMEM(by_head, half),
        pltpu.VMEM((KEYS, 2 * width), half),
        pltpu.VMEM((2 * width, KEYS // 2), half),
        pltpu.VMEM((tokens, width), full),
    ]
    scratch += [pltpu.VMEM(square, full)] * 4 + [pltpu.VMEM((tokens, KEYS), half)] * 4
    scratch += [pltpu.VMEM((head_dim, KEYS), full)] * 2
    return call_kernel(
        functools.partial(backward_kernel, head_dim),
        [kv_own, x_side, w_qkv, queries, cotangents, bias],
        [
            jax.ShapeDtypeStruct((2 * width, KEYS // 2), half),
            jax.ShapeDtypeStruct(queries.shape, half),
            jax.ShapeDtypeStruct((KEYS // 2, width), half),
        ],
        scratch,
        4 * KEYS * width * width + 10 * heads * tokens * KEYS * LANES,
        "attention_backward",
    )


def project(x, w):
    return jnp.dot(x, w, preferred_element_type=jnp.float32).astype(jnp.bfloat16)


def body(x_forward, x_backward, grad_out, w_qkv, w_out):
    rows, cols, width = x_forward.shape
    heads = lax.axis_size("heads")
    w_q = w_qkv[:, :width]
    flat = lambda x: x.reshape(-1, width)
    bias = window_bias()

    parts_backward = row_halos(x_backward)
    q_backward = project(flat(x_backward), w_q)
    x_forward, q_backward = lax.optimization_barrier((x_forward, q_backward))
    parts_forward = row_halos(x_forward)
    sends_backward = column_sends(parts_backward)
    side_backward = flat(side_columns(sends_backward))
    grad_heads = lax.dot_general(
        flat(grad_out), w_out, (((1,), (1,)), ((), ())), preferred_element_type=jnp.float32
    ).astype(jnp.bfloat16)
    q_forward = project(flat(x_forward), w_q)
    parts_backward, _ = lax.optimization_barrier((parts_backward, sends_backward))
    own_backward = own_keys([flat(part) for part in parts_backward], w_qkv)

    dkv_own, dq, dx_side = attention_backward(
        own_backward, side_backward, w_qkv, q_backward, grad_heads, bias, heads
    )
    dx_side = dx_side.reshape(2 * SIDE, SIDE, width)
    from_right = shifted(dx_side[:, :8], "heads", -1)
    from_left = shifted(dx_side[:, 8:], "heads", 1)
    parts_forward, _ = lax.optimization_barrier((parts_forward, dx_side))
    sends_forward = column_sends(parts_forward)
    side_forward = flat(side_columns(sends_forward))
    parts_forward, _ = lax.optimization_barrier((parts_forward, sends_forward))
    own_forward = own_keys([flat(part) for part in parts_forward], w_qkv)
    dx_own = own_gradient(dkv_own, dq, w_qkv).reshape(2 * SIDE, SIDE, width)
    from_left, from_right, own_forward = lax.optimization_barrier((from_left, from_right, own_forward))
    total = dx_own + jnp.concatenate([from_left, from_right], 1).astype(jnp.float32)
    from_below = shifted(total[:RADIUS].astype(jnp.bfloat16), "rows", -1)
    from_above = shifted(total[RADIUS + SIDE : 2 * RADIUS + SIDE].astype(jnp.bfloat16), "rows", 1)
    side_forward, middle = lax.optimization_barrier((side_forward, total[RADIUS : RADIUS + SIDE]))
    y_forward = attention_forward(own_forward, side_forward, w_qkv, w_out, q_forward, bias, heads)

    gap = jnp.zeros((rows - RADIUS, cols, width), jnp.float32)
    dx = (
        middle
        + jnp.concatenate([from_above.astype(jnp.float32), gap], 0)
        + jnp.concatenate([gap, from_below.astype(jnp.float32)], 0)
    )
    return (y_forward.reshape(rows, cols, width), dx.astype(jnp.bfloat16))


def solution(mesh):
    spec = P("rows", "heads", None)
    return jax.shard_map(
        body, mesh=mesh, in_specs=(spec, spec, spec, P(), P()), out_specs=(spec, spec), check_vma=False
    )
```

```python
import functools
import math

import jax
import jax.numpy as jnp
from jax import lax
from jax.experimental import pallas as pl
from jax.experimental.pallas import tpu as pltpu
from jax.sharding import PartitionSpec as P

RADIUS = 7
SIDE = 16
LANES = 256
GROUP = 256
HALF = 128
SPAN = 3 * GROUP
KEYS = 4 * GROUP
NEG = -1e30
CHUNK = 16
LIMIT = 40 * 2**20


def shifted(value, axis, step):
    count = lax.axis_size(axis)
    return lax.ppermute(value, axis, [(i, (i + step) % count) for i in range(count)])


def row_halos(x):
    return shifted(x[SIDE - RADIUS :], "rows", 1), x, shifted(x[:RADIUS], "rows", -1)


def column_sends(parts):
    zeros = jnp.zeros((2, 8) + parts[0].shape[2:], parts[0].dtype)
    return [jnp.concatenate([part[:, side] for part in parts] + [zeros], 0) for side in (slice(8, 16), slice(0, 8))]


def side_columns(sends):
    return jnp.concatenate([shifted(sends[0], "heads", 1), shifted(sends[1], "heads", -1)], 1)


def window_bias():
    row_start = lax.axis_index("rows") * SIDE
    col_start = lax.axis_index("heads") * SIDE
    rows_total = lax.axis_size("rows") * SIDE
    cols_total = lax.axis_size("heads") * SIDE
    query = lax.broadcasted_iota(jnp.int32, (2 * HALF, SPAN), 0)
    place = lax.broadcasted_iota(jnp.int32, (2 * HALF, SPAN), 1)
    half = query // HALF
    query_row, query_col = query // SIDE, query % SIDE
    group, rest = place // GROUP + half, place % GROUP
    side, inner = rest // HALF, rest % HALF
    key_row, column = group * 8 + inner // SIDE, inner % SIDE
    key_col = jnp.where(side == 0, column, jnp.where(column < 8, column - 8, column + 8))
    image_row = row_start + key_row - RADIUS
    image_col = col_start + key_col
    row_gap, col_gap = key_row - query_row, key_col - query_col
    valid = (row_gap >= 0) & (row_gap <= 2 * RADIUS) & (col_gap >= -RADIUS) & (col_gap <= RADIUS)
    valid &= (image_row >= 0) & (image_row < rows_total) & (image_col >= 0) & (image_col < cols_total)
    return jnp.where(valid, 0.0, NEG).astype(jnp.float32)


def head_lanes(head, head_dim, width):
    tile = jnp.clip(head * head_dim // 128, 0, (width - LANES) // 128)
    offset = head * head_dim - tile * 128
    lane = lax.broadcasted_iota(jnp.int32, (1, LANES), 1)
    return tile * 128, (lane >= offset) & (lane < offset + head_dim)


def at_lanes(start):
    return pl.ds(pl.multiple_of(start, 128), LANES)


def own_keys_kernel(above, own, below, weights, out_ref):
    skip = weights.shape[1] - out_ref.shape[1]
    for start in range(0, out_ref.shape[1], GROUP):
        low = 0
        for x_ref in (above, own, below):
            part = jnp.dot(
                x_ref[...], weights[:, skip + start : skip + start + GROUP], preferred_element_type=jnp.float32
            )
            out_ref[low : low + x_ref.shape[0], start : start + GROUP] = part.astype(out_ref.dtype)
            low += x_ref.shape[0]
        out_ref[low:, start : start + GROUP] = jnp.zeros((out_ref.shape[0] - low, GROUP), out_ref.dtype)


def own_gradient_kernel(dkv, dq, weights, out_ref):
    width = dq.shape[1]
    for start in range(0, out_ref.shape[0], GROUP):
        part = jnp.dot(weights[:, width:], dkv[:, start : start + GROUP], preferred_element_type=jnp.float32)
        out_ref[start : start + GROUP, :] = jnp.transpose(part)
    mine = slice(RADIUS * SIDE, RADIUS * SIDE + dq.shape[0])
    out_ref[mine, :] += lax.dot_general(
        dq[...], weights[:, :width], (((1,), (1,)), ((), ())), preferred_element_type=jnp.float32
    )


def fill_keys(kv_own, x_side, weights, kv):
    skip = weights.shape[1] - kv.shape[1]
    for group in range(4):
        kv[GROUP * group : GROUP * group + HALF, :] = kv_own[HALF * group : HALF * (group + 1), :]
    for start in range(0, kv.shape[1], GROUP):
        part = jnp.dot(
            x_side[...], weights[:, skip + start : skip + start + GROUP], preferred_element_type=jnp.float32
        ).astype(kv.dtype)
        for group in range(4):
            low = GROUP * group + HALF
            kv[low : low + HALF, start : start + GROUP] = part[HALF * group : HALF * (group + 1)]


def turned(source, target):
    heads, head_dim, _ = target.shape
    flipped = jnp.transpose(source[...].astype(jnp.float32))
    for head in range(heads):
        target[head] = flipped[head * head_dim : (head + 1) * head_dim].astype(target.dtype)


def span_products(rows, kv, start, out_ref):
    def one(group):
        low = 0 if group < 3 else HALF
        high = 2 * HALF if group > 0 else HALF
        keys = kv[GROUP * group : GROUP * (group + 1), at_lanes(start)]
        part = lax.dot_general(
            rows[low:high], keys, (((1,), (1,)), ((), ())), preferred_element_type=jnp.float32
        )
        if group < 3:
            out_ref[:HALF, GROUP * group : GROUP * (group + 1)] = part[:HALF]
        if group > 0:
            out_ref[HALF:, GROUP * (group - 1) : GROUP * group] = part[-HALF:]

    return [functools.partial(one, group) for group in range(4)]


def interleave(*streams):
    marks = [((i + 0.5) / len(stream), n, step) for n, stream in enumerate(streams) for i, step in enumerate(stream)]
    for _, _, step in sorted(marks, key=lambda mark: mark[:2]):
        step()


def softmax_rows(scores, bias, factor):
    scores = scores + bias
    top = jnp.max(scores, axis=1, keepdims=True)
    terms = jnp.exp2((scores - top) * factor)
    return terms * (1.0 / jnp.sum(terms, axis=1, keepdims=True))


def span_of(rows):
    start = 0 if rows < HALF else GROUP
    return slice(start, start + SPAN)


def forward_kernel(
    head_dim, kv_own, x_side, weights, w_out, queries, bias, out_ref, kv, acc, scores0, scores1, probs0, probs1
):
    width = queries.shape[1]
    heads = width // head_dim
    factor = head_dim**-0.5 * math.log2(math.e)
    scores, probs = (scores0, scores1), (probs0, probs1)
    for ref in probs + (acc,):
        ref[...] = jnp.zeros_like(ref)
    fill_keys(kv_own, x_side, weights, kv)

    def scored(head, u):
        start, mask = head_lanes(head, head_dim, width)
        return span_products(jnp.where(mask, queries[:, at_lanes(start)], 0), kv, start, scores[u])

    def weighted(u):
        def one(rows):
            part = slice(rows, rows + CHUNK)
            attention = softmax_rows(scores[u][part, :], bias[part, :], factor)
            probs[u][part, span_of(rows)] = attention.astype(jnp.bfloat16)

        return [functools.partial(one, rows) for rows in range(0, 2 * HALF, CHUNK)]

    def mixed(head, u):
        start, mask = head_lanes(head, head_dim, width)

        def one():
            mix = jnp.dot(probs[u][...], kv[:, at_lanes(start + width)], preferred_element_type=jnp.float32)
            acc[:, at_lanes(start)] += jnp.where(mask & (head >= 0), mix, 0.0)

        return [one]

    interleave(scored(0, 0))

    def pair(index, carry):
        head = 2 * index
        interleave(scored(head + 1, 1), weighted(0), mixed(head - 1, 1))
        interleave(scored(jnp.minimum(head + 2, heads - 1), 0), weighted(1), mixed(head, 0))
        return carry

    lax.fori_loop(0, heads // 2, pair, 0)
    interleave(mixed(heads - 1, 1))
    attended = acc[...].astype(jnp.bfloat16)
    out_ref[...] = jnp.dot(attended, w_out[...], preferred_element_type=jnp.float32).astype(out_ref.dtype)


def backward_kernel(
    head_dim, kv_own, x_side, weights, queries, cotangents, bias, down_ref, dq_ref, dside_ref,
    queries_t, cotangents_t, kv, dkv, acc,
    scores0, scores1, grads0, grads1, probs0, probs1, dscores0, dscores1, held0, held1
):
    width = queries.shape[1]
    heads = width // head_dim
    scaling = head_dim**-0.5
    factor = scaling * math.log2(math.e)
    scores, grads, held = (scores0, scores1), (grads0, grads1), (held0, held1)
    probs, dscores = (probs0, probs1), (dscores0, dscores1)
    for ref in probs + dscores + held + (acc,):
        ref[...] = jnp.zeros_like(ref)
    turned(queries, queries_t)
    turned(cotangents, cotangents_t)
    fill_keys(kv_own, x_side, weights, kv)

    def scored(head, u):
        start, mask = head_lanes(head, head_dim, width)
        one = span_products(jnp.where(mask, queries[:, at_lanes(start)], 0), kv, start, scores[u])
        other = span_products(jnp.where(mask, cotangents[:, at_lanes(start)], 0), kv, start + width, grads[u])
        return [step for both in zip(one, other) for step in both]

    def weighted(u):
        def one(rows):
            part = slice(rows, rows + CHUNK)
            attention = softmax_rows(scores[u][part, :], bias[part, :], factor)
            grad = grads[u][part, :]
            centre = jnp.sum(attention * grad, axis=1, keepdims=True)
            probs[u][part, span_of(rows)] = attention.astype(jnp.bfloat16)
            dscores[u][part, span_of(rows)] = (attention * (grad - centre) * scaling).astype(jnp.bfloat16)

        return [functools.partial(one, rows) for rows in range(0, 2 * HALF, CHUNK)]

    def spread(head, u):
        start, mask = head_lanes(head, head_dim, width)
        row = jnp.maximum(head, 0)
        base = jnp.maximum(head - 1, 0) * head_dim

        def query_part():
            dq = jnp.dot(dscores[u][...], kv[:, at_lanes(start)], preferred_element_type=jnp.float32)
            acc[:, at_lanes(start)] += jnp.where(mask & (head >= 0), dq, 0.0)

        def key_part(index, group):
            source, spans = ((queries_t, dscores), (cotangents_t, probs))[index]
            place = slice(GROUP * group, GROUP * (group + 1))
            part = jnp.dot(source[row], spans[u][:, place], preferred_element_type=jnp.float32)
            if u == 0:
                held[index][:, place] = part
            else:
                both = jnp.concatenate([held[index][:, place], part], 0).astype(jnp.bfloat16)
                rows = pl.ds(pl.multiple_of(base + index * width, 16), 2 * head_dim)
                place = slice(HALF * group, HALF * (group + 1))
                down_ref[rows, place] = both[:, :HALF]
                dkv[rows, place] = both[:, HALF:]

        parts = [functools.partial(key_part, index, group) for index in range(2) for group in range(4)]
        return parts[:4] + [query_part] + parts[4:]

    interleave(scored(0, 0))

    def pair(index, carry):
        head = 2 * index
        interleave(scored(head + 1, 1), weighted(0), spread(head - 1, 1))
        interleave(scored(jnp.minimum(head + 2, heads - 1), 0), weighted(1), spread(head, 0))
        return carry

    lax.fori_loop(0, heads // 2, pair, 0)
    interleave(spread(heads - 1, 1))

    dq_ref[...] = acc[...].astype(dq_ref.dtype)
    for start in range(0, dside_ref.shape[0], GROUP):
        part = jnp.dot(weights[:, width:], dkv[:, start : start + GROUP], preferred_element_type=jnp.float32)
        dside_ref[start : start + GROUP, :] = jnp.transpose(part).astype(dside_ref.dtype)


def call_kernel(kernel, args, out_shape, scratch, flops, name):
    return pl.pallas_call(
        kernel,
        out_shape=out_shape,
        scratch_shapes=scratch,
        compiler_params=pltpu.CompilerParams(vmem_limit_bytes=LIMIT),
        cost_estimate=pl.CostEstimate(flops=flops, bytes_accessed=16 * 2**20, transcendentals=2**22),
        name=name,
    )(*args)


def own_keys(x_parts, w_qkv):
    width, columns = w_qkv.shape
    out_shape = jax.ShapeDtypeStruct((KEYS // 2, columns - width), jnp.bfloat16)
    return call_kernel(own_keys_kernel, [*x_parts, w_qkv], out_shape, [], 2 * KEYS * width * width, "own_keys")


def own_gradient(dkv, dq, w_qkv):
    out_shape = jax.ShapeDtypeStruct((KEYS // 2, dq.shape[1]), jnp.float32)
    flops = 2 * KEYS * dq.shape[1] ** 2
    return call_kernel(own_gradient_kernel, [dkv, dq, w_qkv], out_shape, [], flops, "own_gradient")


def attention_forward(kv_own, x_side, w_qkv, w_out, queries, bias, heads):
    tokens, width = queries.shape
    half, full = jnp.bfloat16, jnp.float32
    square = (tokens, SPAN)
    scratch = [pltpu.VMEM((KEYS, 2 * width), half), pltpu.VMEM((tokens, width), full)]
    scratch += [pltpu.VMEM(square, full)] * 2 + [pltpu.VMEM((tokens, KEYS), half)] * 2
    return call_kernel(
        functools.partial(forward_kernel, width // heads),
        [kv_own, x_side, w_qkv, w_out, queries, bias],
        jax.ShapeDtypeStruct(queries.shape, half),
        scratch,
        2 * KEYS * width * width + 4 * heads * tokens * KEYS * LANES,
        "attention_forward",
    )


def attention_backward(kv_own, x_side, w_qkv, queries, cotangents, bias, heads):
    tokens, width = queries.shape
    head_dim = width // heads
    square = (tokens, SPAN)
    half, full = jnp.bfloat16, jnp.float32
    by_head = (heads, head_dim, tokens)
    scratch = [
        pltpu.VMEM(by_head, half),
        pltpu.VMEM(by_head, half),
        pltpu.VMEM((KEYS, 2 * width), half),
        pltpu.VMEM((2 * width, KEYS // 2), half),
        pltpu.VMEM((tokens, width), full),
    ]
    scratch += [pltpu.VMEM(square, full)] * 4 + [pltpu.VMEM((tokens, KEYS), half)] * 4
    scratch += [pltpu.VMEM((head_dim, KEYS), full)] * 2
    return call_kernel(
        functools.partial(backward_kernel, head_dim),
        [kv_own, x_side, w_qkv, queries, cotangents, bias],
        [
            jax.ShapeDtypeStruct((2 * width, KEYS // 2), half),
            jax.ShapeDtypeStruct(queries.shape, half),
            jax.ShapeDtypeStruct((KEYS // 2, width), half),
        ],
        scratch,
        4 * KEYS * width * width + 10 * heads * tokens * KEYS * LANES,
        "attention_backward",
    )


def project(x, w):
    return jnp.dot(x, w, preferred_element_type=jnp.float32).astype(jnp.bfloat16)


def body(x_forward, x_backward, grad_out, w_qkv, w_out):
    rows, cols, width = x_forward.shape
    heads = lax.axis_size("heads")
    w_q = w_qkv[:, :width]
    flat = lambda x: x.reshape(-1, width)
    bias = window_bias()

    parts_backward = row_halos(x_backward)
    q_backward = project(flat(x_backward), w_q)
    q_forward = project(flat(x_forward), w_q)
    grad_heads = lax.dot_general(
        flat(grad_out), w_out, (((1,), (1,)), ((), ())), preferred_element_type=jnp.float32
    ).astype(jnp.bfloat16)
    sends_backward, q_backward, q_forward, grad_heads, bias = lax.optimization_barrier(
        (column_sends(parts_backward), q_backward, q_forward, grad_heads, bias)
    )
    side_backward = flat(side_columns(sends_backward))
    x_forward, _ = lax.optimization_barrier((x_forward, sends_backward))
    parts_forward = row_halos(x_forward)
    parts_backward, _ = lax.optimization_barrier((parts_backward, sends_backward))
    own_backward = own_keys([flat(part) for part in parts_backward], w_qkv)

    dkv_own, dq, dx_side = attention_backward(
        own_backward, side_backward, w_qkv, q_backward, grad_heads, bias, heads
    )
    dx_side = dx_side.reshape(2 * SIDE, SIDE, width)
    from_right = shifted(dx_side[:, :8], "heads", -1)
    from_left = shifted(dx_side[:, 8:], "heads", 1)
    dx_own = own_gradient(dkv_own, dq, w_qkv).reshape(2 * SIDE, SIDE, width)
    parts_forward, _ = lax.optimization_barrier((parts_forward, dx_own))
    sends_forward = column_sends(parts_forward)
    side_forward = flat(side_columns(sends_forward))
    parts_forward, _ = lax.optimization_barrier((parts_forward, sends_forward))
    own_forward = own_keys([flat(part) for part in parts_forward], w_qkv)
    from_left, from_right, own_forward = lax.optimization_barrier((from_left, from_right, own_forward))
    total = dx_own + jnp.concatenate([from_left, from_right], 1).astype(jnp.float32)
    from_below = shifted(total[:RADIUS].astype(jnp.bfloat16), "rows", -1)
    from_above = shifted(total[RADIUS + SIDE : 2 * RADIUS + SIDE].astype(jnp.bfloat16), "rows", 1)
    side_forward, middle = lax.optimization_barrier((side_forward, total[RADIUS : RADIUS + SIDE]))
    y_forward = attention_forward(own_forward, side_forward, w_qkv, w_out, q_forward, bias, heads)

    gap = jnp.zeros((rows - RADIUS, cols, width), jnp.float32)
    dx = (
        middle
        + jnp.concatenate([from_above.astype(jnp.float32), gap], 0)
        + jnp.concatenate([gap, from_below.astype(jnp.float32)], 0)
    )
    return (y_forward.reshape(rows, cols, width), dx.astype(jnp.bfloat16))


def solution(mesh):
    spec = P("rows", "heads", None)
    return jax.shard_map(
        body, mesh=mesh, in_specs=(spec, spec, spec, P(), P()), out_specs=(spec, spec), check_vma=False
    )
```

```python
import functools
import math

import jax
import jax.numpy as jnp
from jax import lax
from jax.experimental import pallas as pl
from jax.experimental.pallas import tpu as pltpu
from jax.sharding import PartitionSpec as P

RADIUS = 7
SIDE = 16
LANES = 256
GROUP = 256
HALF = 128
SPAN = 3 * GROUP
KEYS = 4 * GROUP
NEG = -1e30
CHUNK = 32
LIMIT = 40 * 2**20


def shifted(value, axis, step):
    count = lax.axis_size(axis)
    return lax.ppermute(value, axis, [(i, (i + step) % count) for i in range(count)])


def row_halos(x):
    return shifted(x[SIDE - RADIUS :], "rows", 1), x, shifted(x[:RADIUS], "rows", -1)


def column_sends(parts):
    zeros = jnp.zeros((2, 8) + parts[0].shape[2:], parts[0].dtype)
    return [jnp.concatenate([part[:, side] for part in parts] + [zeros], 0) for side in (slice(8, 16), slice(0, 8))]


def side_columns(sends):
    return jnp.concatenate([shifted(sends[0], "heads", 1), shifted(sends[1], "heads", -1)], 1)


def window_bias():
    row_start = lax.axis_index("rows") * SIDE
    col_start = lax.axis_index("heads") * SIDE
    rows_total = lax.axis_size("rows") * SIDE
    cols_total = lax.axis_size("heads") * SIDE
    query = lax.broadcasted_iota(jnp.int32, (2 * HALF, SPAN), 0)
    place = lax.broadcasted_iota(jnp.int32, (2 * HALF, SPAN), 1)
    half = query // HALF
    query_row, query_col = query // SIDE, query % SIDE
    group, rest = place // GROUP + half, place % GROUP
    side, inner = rest // HALF, rest % HALF
    key_row, column = group * 8 + inner // SIDE, inner % SIDE
    key_col = jnp.where(side == 0, column, jnp.where(column < 8, column - 8, column + 8))
    image_row = row_start + key_row - RADIUS
    image_col = col_start + key_col
    row_gap, col_gap = key_row - query_row, key_col - query_col
    valid = (row_gap >= 0) & (row_gap <= 2 * RADIUS) & (col_gap >= -RADIUS) & (col_gap <= RADIUS)
    valid &= (image_row >= 0) & (image_row < rows_total) & (image_col >= 0) & (image_col < cols_total)
    return jnp.where(valid, 0.0, NEG).astype(jnp.float32)


def pair_lanes(pair, head_dim, width):
    tile = jnp.clip(2 * pair * head_dim // 128, 0, (width - LANES) // 128)
    offset = 2 * pair * head_dim - tile * 128
    lane = lax.broadcasted_iota(jnp.int32, (1, LANES), 1)
    live = pair >= 0
    first = (lane >= offset) & (lane < offset + head_dim) & live
    second = (lane >= offset + head_dim) & (lane < offset + 2 * head_dim) & live
    return tile * 128, (first, second)


def stacked(ref, start, masks):
    block = ref[:, at_lanes(start)]
    halves = (block[:HALF], block[HALF:])
    return jnp.concatenate([jnp.where(mask, half, 0) for half in halves for mask in masks], 0)


def add_heads(acc, start, masks, parts):
    for half, part in enumerate(parts):
        rows = slice(HALF * half, HALF * (half + 1))
        acc[rows, at_lanes(start)] += jnp.where(masks[0], part[:HALF], jnp.where(masks[1], part[HALF:], 0.0))


def span_mix(weights, kv, start):
    low = jnp.dot(weights[: 2 * HALF, :], kv[:SPAN, at_lanes(start)], preferred_element_type=jnp.float32)
    high = jnp.dot(weights[2 * HALF :, :], kv[GROUP:, at_lanes(start)], preferred_element_type=jnp.float32)
    return low, high


def at_lanes(start):
    return pl.ds(pl.multiple_of(start, 128), LANES)


def own_keys_kernel(above, own, below, weights, out_ref):
    skip = weights.shape[1] - out_ref.shape[1]
    for start in range(0, out_ref.shape[1], GROUP):
        low = 0
        for x_ref in (above, own, below):
            part = jnp.dot(
                x_ref[...], weights[:, skip + start : skip + start + GROUP], preferred_element_type=jnp.float32
            )
            out_ref[low : low + x_ref.shape[0], start : start + GROUP] = part.astype(out_ref.dtype)
            low += x_ref.shape[0]
        out_ref[low:, start : start + GROUP] = jnp.zeros((out_ref.shape[0] - low, GROUP), out_ref.dtype)


def own_gradient_kernel(dkv, dq, weights, out_ref):
    width = dq.shape[1]
    for start in range(0, out_ref.shape[0], GROUP):
        part = jnp.dot(weights[:, width:], dkv[:, start : start + GROUP], preferred_element_type=jnp.float32)
        out_ref[start : start + GROUP, :] = jnp.transpose(part)
    mine = slice(RADIUS * SIDE, RADIUS * SIDE + dq.shape[0])
    out_ref[mine, :] += lax.dot_general(
        dq[...], weights[:, :width], (((1,), (1,)), ((), ())), preferred_element_type=jnp.float32
    )


def fill_keys(kv_own, x_side, weights, kv):
    skip = weights.shape[1] - kv.shape[1]
    for group in range(4):
        kv[GROUP * group : GROUP * group + HALF, :] = kv_own[HALF * group : HALF * (group + 1), :]
    for start in range(0, kv.shape[1], GROUP):
        part = jnp.dot(
            x_side[...], weights[:, skip + start : skip + start + GROUP], preferred_element_type=jnp.float32
        ).astype(kv.dtype)
        for group in range(4):
            low = GROUP * group + HALF
            kv[low : low + HALF, start : start + GROUP] = part[HALF * group : HALF * (group + 1)]


def turned(source, target):
    heads, head_dim, _ = target.shape
    flipped = jnp.transpose(source[...].astype(jnp.float32))
    for head in range(heads):
        target[head] = flipped[head * head_dim : (head + 1) * head_dim].astype(target.dtype)


def span_products(rows, kv, start, out_ref):
    def one(group):
        low = 0 if group < 3 else 2 * HALF
        high = 4 * HALF if group > 0 else 2 * HALF
        keys = kv[GROUP * group : GROUP * (group + 1), at_lanes(start)]
        part = lax.dot_general(
            rows[low:high], keys, (((1,), (1,)), ((), ())), preferred_element_type=jnp.float32
        )
        if group < 3:
            out_ref[: 2 * HALF, GROUP * group : GROUP * (group + 1)] = part[: 2 * HALF]
        if group > 0:
            out_ref[2 * HALF :, GROUP * (group - 1) : GROUP * group] = part[-2 * HALF :]

    return [functools.partial(one, group) for group in range(4)]


def interleave(*streams):
    marks = [((i + 0.5) / len(stream), n, step) for n, stream in enumerate(streams) for i, step in enumerate(stream)]
    for _, _, step in sorted(marks, key=lambda mark: mark[:2]):
        step()


def softmax_rows(scores, bias, factor):
    scores = scores + bias
    top = jnp.max(scores, axis=1, keepdims=True)
    terms = jnp.exp2((scores - top) * factor)
    return terms * (1.0 / jnp.sum(terms, axis=1, keepdims=True))


def bias_rows(rows):
    start = rows // (2 * HALF) * HALF + rows % HALF
    return slice(start, start + CHUNK)


def run_pairs(pairs, scored, weighted, spread):
    interleave(scored(0, 0))

    def two(index, carry):
        pair = 2 * index
        interleave(scored(pair + 1, 1), weighted(0), spread(pair - 1, 1))
        interleave(scored(jnp.minimum(pair + 2, pairs - 1), 0), weighted(1), spread(pair, 0))
        return carry

    lax.fori_loop(0, pairs // 2, two, 0)
    interleave(spread(pairs - 1, 1))


def forward_kernel(
    head_dim, kv_own, x_side, weights, w_out, queries, bias, out_ref, kv, acc, scores0, scores1, probs0, probs1
):
    width = queries.shape[1]
    factor = head_dim**-0.5 * math.log2(math.e)
    scores, probs = (scores0, scores1), (probs0, probs1)
    acc[...] = jnp.zeros_like(acc)
    fill_keys(kv_own, x_side, weights, kv)

    def scored(pair, u):
        start, masks = pair_lanes(pair, head_dim, width)
        return span_products(stacked(queries, start, masks), kv, start, scores[u])

    def weighted(u):
        def one(rows):
            part = slice(rows, rows + CHUNK)
            attention = softmax_rows(scores[u][part, :], bias[bias_rows(rows), :], factor)
            probs[u][part, :] = attention.astype(jnp.bfloat16)

        return [functools.partial(one, rows) for rows in range(0, 4 * HALF, CHUNK)]

    def spread(pair, u):
        start, masks = pair_lanes(pair, head_dim, width)
        return [lambda: add_heads(acc, start, masks, span_mix(probs[u], kv, start + width))]

    run_pairs(width // head_dim // 2, scored, weighted, spread)
    attended = acc[...].astype(jnp.bfloat16)
    out_ref[...] = jnp.dot(attended, w_out[...], preferred_element_type=jnp.float32).astype(out_ref.dtype)


def backward_kernel(
    head_dim, kv_own, x_side, weights, queries, cotangents, bias, down_ref, dq_ref, dside_ref,
    queries_t, cotangents_t, kv, dkv, acc, scores0, scores1, grads0, grads1, probs0, probs1, dscores0, dscores1
):
    width = queries.shape[1]
    scaling = head_dim**-0.5
    factor = scaling * math.log2(math.e)
    scores, grads = (scores0, scores1), (grads0, grads1)
    probs, dscores = (probs0, probs1), (dscores0, dscores1)
    acc[...] = jnp.zeros_like(acc)
    turned(queries, queries_t)
    turned(cotangents, cotangents_t)
    fill_keys(kv_own, x_side, weights, kv)

    def scored(pair, u):
        start, masks = pair_lanes(pair, head_dim, width)
        one = span_products(stacked(queries, start, masks), kv, start, scores[u])
        other = span_products(stacked(cotangents, start, masks), kv, start + width, grads[u])
        return [step for both in zip(one, other) for step in both]

    def weighted(u):
        def one(rows):
            part = slice(rows, rows + CHUNK)
            attention = softmax_rows(scores[u][part, :], bias[bias_rows(rows), :], factor)
            grad = grads[u][part, :]
            centre = jnp.sum(attention * grad, axis=1, keepdims=True)
            probs[u][part, :] = attention.astype(jnp.bfloat16)
            dscores[u][part, :] = (attention * (grad - centre) * scaling).astype(jnp.bfloat16)

        return [functools.partial(one, rows) for rows in range(0, 4 * HALF, CHUNK)]

    def spread(pair, u):
        start, masks = pair_lanes(pair, head_dim, width)
        here = jnp.maximum(pair, 0)

        def query_part():
            add_heads(acc, start, masks, span_mix(dscores[u], kv, start))

        def head_part(source, spans, head, group):
            low = spans[HALF * head : HALF * (head + 1), GROUP * group : GROUP * (group + 1)] if group < 3 else None
            place = slice(GROUP * (group - 1), GROUP * group)
            high = spans[HALF * (head + 2) : HALF * (head + 3), place] if group > 0 else None
            features = source[2 * here + head]
            if group == 0:
                features, span = features[:, :HALF], low
            elif group == 3:
                features, span = features[:, HALF:], high
            else:
                span = jnp.concatenate([low, high], 0)
            return jnp.dot(features, span, preferred_element_type=jnp.float32)

        def key_part(index, group):
            source, spans = ((queries_t, dscores[u]), (cotangents_t, probs[u]))[index]
            both = jnp.concatenate([head_part(source, spans, head, group) for head in range(2)], 0)
            both = both.astype(jnp.bfloat16)
            rows = pl.ds(pl.multiple_of(2 * head_dim * here + index * width, 16), 2 * head_dim)
            place = slice(HALF * group, HALF * (group + 1))
            down_ref[rows, place] = both[:, :HALF]
            dkv[rows, place] = both[:, HALF:]

        parts = [functools.partial(key_part, index, group) for index in range(2) for group in range(4)]
        return parts[:4] + [query_part] + parts[4:]

    run_pairs(width // head_dim // 2, scored, weighted, spread)

    dq_ref[...] = acc[...].astype(dq_ref.dtype)
    for start in range(0, dside_ref.shape[0], GROUP):
        part = jnp.dot(weights[:, width:], dkv[:, start : start + GROUP], preferred_element_type=jnp.float32)
        dside_ref[start : start + GROUP, :] = jnp.transpose(part).astype(dside_ref.dtype)


def call_kernel(kernel, args, out_shape, scratch, flops, name):
    return pl.pallas_call(
        kernel,
        out_shape=out_shape,
        scratch_shapes=scratch,
        compiler_params=pltpu.CompilerParams(vmem_limit_bytes=LIMIT),
        cost_estimate=pl.CostEstimate(flops=flops, bytes_accessed=16 * 2**20, transcendentals=2**22),
        name=name,
    )(*args)


def own_keys(x_parts, w_qkv):
    width, columns = w_qkv.shape
    out_shape = jax.ShapeDtypeStruct((KEYS // 2, columns - width), jnp.bfloat16)
    return call_kernel(own_keys_kernel, [*x_parts, w_qkv], out_shape, [], 2 * KEYS * width * width, "own_keys")


def own_gradient(dkv, dq, w_qkv):
    out_shape = jax.ShapeDtypeStruct((KEYS // 2, dq.shape[1]), jnp.float32)
    flops = 2 * KEYS * dq.shape[1] ** 2
    return call_kernel(own_gradient_kernel, [dkv, dq, w_qkv], out_shape, [], flops, "own_gradient")


def attention_forward(kv_own, x_side, w_qkv, w_out, queries, bias, heads):
    tokens, width = queries.shape
    half, full = jnp.bfloat16, jnp.float32
    square = (2 * tokens, SPAN)
    scratch = [pltpu.VMEM((KEYS, 2 * width), half), pltpu.VMEM((tokens, width), full)]
    scratch += [pltpu.VMEM(square, full)] * 2 + [pltpu.VMEM(square, half)] * 2
    return call_kernel(
        functools.partial(forward_kernel, width // heads),
        [kv_own, x_side, w_qkv, w_out, queries, bias],
        jax.ShapeDtypeStruct(queries.shape, half),
        scratch,
        2 * KEYS * width * width + 4 * heads * tokens * KEYS * LANES,
        "attention_forward",
    )


def attention_backward(kv_own, x_side, w_qkv, queries, cotangents, bias, heads):
    tokens, width = queries.shape
    head_dim = width // heads
    square = (2 * tokens, SPAN)
    half, full = jnp.bfloat16, jnp.float32
    by_head = (heads, head_dim, tokens)
    scratch = [
        pltpu.VMEM(by_head, half),
        pltpu.VMEM(by_head, half),
        pltpu.VMEM((KEYS, 2 * width), half),
        pltpu.VMEM((2 * width, KEYS // 2), half),
        pltpu.VMEM((tokens, width), full),
    ]
    scratch += [pltpu.VMEM(square, full)] * 4 + [pltpu.VMEM(square, half)] * 4
    return call_kernel(
        functools.partial(backward_kernel, head_dim),
        [kv_own, x_side, w_qkv, queries, cotangents, bias],
        [
            jax.ShapeDtypeStruct((2 * width, KEYS // 2), half),
            jax.ShapeDtypeStruct(queries.shape, half),
            jax.ShapeDtypeStruct((KEYS // 2, width), half),
        ],
        scratch,
        4 * KEYS * width * width + 10 * heads * tokens * KEYS * LANES,
        "attention_backward",
    )


def project(x, w):
    return jnp.dot(x, w, preferred_element_type=jnp.float32).astype(jnp.bfloat16)


def body(x_forward, x_backward, grad_out, w_qkv, w_out):
    rows, cols, width = x_forward.shape
    heads = lax.axis_size("heads")
    w_q = w_qkv[:, :width]
    flat = lambda x: x.reshape(-1, width)
    bias = window_bias()

    parts_backward = row_halos(x_backward)
    q_backward = project(flat(x_backward), w_q)
    q_forward = project(flat(x_forward), w_q)
    grad_heads = lax.dot_general(
        flat(grad_out), w_out, (((1,), (1,)), ((), ())), preferred_element_type=jnp.float32
    ).astype(jnp.bfloat16)
    sends_backward, q_backward, q_forward, grad_heads, bias = lax.optimization_barrier(
        (column_sends(parts_backward), q_backward, q_forward, grad_heads, bias)
    )
    side_backward = flat(side_columns(sends_backward))
    x_forward, _ = lax.optimization_barrier((x_forward, sends_backward))
    parts_forward = row_halos(x_forward)
    parts_backward, _ = lax.optimization_barrier((parts_backward, sends_backward))
    own_backward = own_keys([flat(part) for part in parts_backward], w_qkv)

    dkv_own, dq, dx_side = attention_backward(
        own_backward, side_backward, w_qkv, q_backward, grad_heads, bias, heads
    )
    dx_side = dx_side.reshape(2 * SIDE, SIDE, width)
    from_right = shifted(dx_side[:, :8], "heads", -1)
    from_left = shifted(dx_side[:, 8:], "heads", 1)
    dx_own = own_gradient(dkv_own, dq, w_qkv).reshape(2 * SIDE, SIDE, width)
    parts_forward, _ = lax.optimization_barrier((parts_forward, dx_own))
    sends_forward = column_sends(parts_forward)
    side_forward = flat(side_columns(sends_forward))
    parts_forward, _ = lax.optimization_barrier((parts_forward, sends_forward))
    own_forward = own_keys([flat(part) for part in parts_forward], w_qkv)
    from_left, from_right, own_forward = lax.optimization_barrier((from_left, from_right, own_forward))
    total = dx_own + jnp.concatenate([from_left, from_right], 1).astype(jnp.float32)
    from_below = shifted(total[:RADIUS].astype(jnp.bfloat16), "rows", -1)
    from_above = shifted(total[RADIUS + SIDE : 2 * RADIUS + SIDE].astype(jnp.bfloat16), "rows", 1)
    side_forward, middle = lax.optimization_barrier((side_forward, total[RADIUS : RADIUS + SIDE]))
    y_forward = attention_forward(own_forward, side_forward, w_qkv, w_out, q_forward, bias, heads)

    gap = jnp.zeros((rows - RADIUS, cols, width), jnp.float32)
    dx = (
        middle
        + jnp.concatenate([from_above.astype(jnp.float32), gap], 0)
        + jnp.concatenate([gap, from_below.astype(jnp.float32)], 0)
    )
    return (y_forward.reshape(rows, cols, width), dx.astype(jnp.bfloat16))


def solution(mesh):
    spec = P("rows", "heads", None)
    return jax.shard_map(
        body, mesh=mesh, in_specs=(spec, spec, spec, P(), P()), out_specs=(spec, spec), check_vma=False
    )
```

```python
import functools
import math

import jax
import jax.numpy as jnp
from jax import lax
from jax.experimental import pallas as pl
from jax.experimental.pallas import tpu as pltpu
from jax.sharding import PartitionSpec as P

RADIUS = 7
SIDE = 16
LANES = 256
GROUP = 256
HALF = 128
SPAN = 3 * GROUP
KEYS = 4 * GROUP
NEG = -1e30
CHUNK = 32
LIMIT = 40 * 2**20


def shifted(value, axis, step):
    count = lax.axis_size(axis)
    return lax.ppermute(value, axis, [(i, (i + step) % count) for i in range(count)])


def row_halos(x):
    return shifted(x[SIDE - RADIUS :], "rows", 1), x, shifted(x[:RADIUS], "rows", -1)


def column_sends(parts):
    zeros = jnp.zeros((2, 8) + parts[0].shape[2:], parts[0].dtype)
    return [jnp.concatenate([part[:, side] for part in parts] + [zeros], 0) for side in (slice(8, 16), slice(0, 8))]


def side_columns(sends):
    return jnp.concatenate([shifted(sends[0], "heads", 1), shifted(sends[1], "heads", -1)], 1)


def window_bias():
    row_start = lax.axis_index("rows") * SIDE
    col_start = lax.axis_index("heads") * SIDE
    rows_total = lax.axis_size("rows") * SIDE
    cols_total = lax.axis_size("heads") * SIDE
    query = lax.broadcasted_iota(jnp.int32, (2 * HALF, SPAN), 0)
    place = lax.broadcasted_iota(jnp.int32, (2 * HALF, SPAN), 1)
    half = query // HALF
    query_row, query_col = query // SIDE, query % SIDE
    group, rest = place // GROUP + half, place % GROUP
    side, inner = rest // HALF, rest % HALF
    key_row, column = group * 8 + inner // SIDE, inner % SIDE
    key_col = jnp.where(side == 0, column, jnp.where(column < 8, column - 8, column + 8))
    image_row = row_start + key_row - RADIUS
    image_col = col_start + key_col
    row_gap, col_gap = key_row - query_row, key_col - query_col
    valid = (row_gap >= 0) & (row_gap <= 2 * RADIUS) & (col_gap >= -RADIUS) & (col_gap <= RADIUS)
    valid &= (image_row >= 0) & (image_row < rows_total) & (image_col >= 0) & (image_col < cols_total)
    return jnp.where(valid, 0.0, NEG).astype(jnp.float32)


def pair_lanes(pair, head_dim, width):
    tile = jnp.clip(2 * pair * head_dim // 128, 0, (width - LANES) // 128)
    offset = 2 * pair * head_dim - tile * 128
    lane = lax.broadcasted_iota(jnp.int32, (1, LANES), 1)
    live = pair >= 0
    first = (lane >= offset) & (lane < offset + head_dim) & live
    second = (lane >= offset + head_dim) & (lane < offset + 2 * head_dim) & live
    return tile * 128, (first, second)


def stacked(ref, start, masks):
    block = ref[:, at_lanes(start)]
    halves = (block[:HALF], block[HALF:])
    return jnp.concatenate([jnp.where(mask, half, 0) for half in halves for mask in masks], 0)


def add_heads(acc, start, masks, parts):
    for half, part in enumerate(parts):
        rows = slice(HALF * half, HALF * (half + 1))
        acc[rows, at_lanes(start)] += jnp.where(masks[0], part[:HALF], jnp.where(masks[1], part[HALF:], 0.0))


def span_mix(weights, kv, start):
    low = jnp.dot(weights[: 2 * HALF, :], kv[:SPAN, at_lanes(start)], preferred_element_type=jnp.float32)
    high = jnp.dot(weights[2 * HALF :, :], kv[GROUP:, at_lanes(start)], preferred_element_type=jnp.float32)
    return low, high


def at_lanes(start):
    return pl.ds(pl.multiple_of(start, 128), LANES)


def own_keys_kernel(above, own, below, weights, out_ref):
    skip = weights.shape[1] - out_ref.shape[1]
    for start in range(0, out_ref.shape[1], GROUP):
        low = 0
        for x_ref in (above, own, below):
            part = jnp.dot(
                x_ref[...], weights[:, skip + start : skip + start + GROUP], preferred_element_type=jnp.float32
            )
            out_ref[low : low + x_ref.shape[0], start : start + GROUP] = part.astype(out_ref.dtype)
            low += x_ref.shape[0]
        out_ref[low:, start : start + GROUP] = jnp.zeros((out_ref.shape[0] - low, GROUP), out_ref.dtype)


def own_gradient_kernel(dkv, dq, weights, out_ref):
    width = dq.shape[1]
    for start in range(0, out_ref.shape[0], GROUP):
        part = jnp.dot(weights[:, width:], dkv[:, start : start + GROUP], preferred_element_type=jnp.float32)
        out_ref[start : start + GROUP, :] = jnp.transpose(part)
    mine = slice(RADIUS * SIDE, RADIUS * SIDE + dq.shape[0])
    out_ref[mine, :] += lax.dot_general(
        dq[...], weights[:, :width], (((1,), (1,)), ((), ())), preferred_element_type=jnp.float32
    )


def fetch(pairs, sems):
    copies = [pltpu.make_async_copy(source, target, sems.at[i]) for i, (source, target) in enumerate(pairs)]
    for copy in copies:
        copy.start()
    return copies


def key_weights(w_ref, w_kv):
    skip, columns = w_ref.shape[1] - w_kv.shape[1], w_kv.shape[1]
    return [
        (w_ref.at[:, pl.ds(skip + start, SPAN)], w_kv.at[:, pl.ds(start, SPAN)]) for start in range(0, columns, SPAN)
    ]


def fill_keys(kv_own, x_side, w_kv, copies, kv):
    for group in range(4):
        kv[GROUP * group : GROUP * group + HALF, :] = kv_own[HALF * group : HALF * (group + 1), :]
    for start in range(0, kv.shape[1], GROUP):
        if start % SPAN == 0:
            copies[start // SPAN].wait()
        part = jnp.dot(x_side[...], w_kv[:, start : start + GROUP], preferred_element_type=jnp.float32)
        part = part.astype(kv.dtype)
        for group in range(4):
            low = GROUP * group + HALF
            kv[low : low + HALF, start : start + GROUP] = part[HALF * group : HALF * (group + 1)]


def turned(source, target):
    heads, head_dim, _ = target.shape
    flipped = jnp.transpose(source[...].astype(jnp.float32))
    for head in range(heads):
        target[head] = flipped[head * head_dim : (head + 1) * head_dim].astype(target.dtype)


def span_products(rows, kv, start, out_ref):
    def one(group):
        low = 0 if group < 3 else 2 * HALF
        high = 4 * HALF if group > 0 else 2 * HALF
        keys = kv[GROUP * group : GROUP * (group + 1), at_lanes(start)]
        part = lax.dot_general(
            rows[low:high], keys, (((1,), (1,)), ((), ())), preferred_element_type=jnp.float32
        )
        if group < 3:
            out_ref[: 2 * HALF, GROUP * group : GROUP * (group + 1)] = part[: 2 * HALF]
        if group > 0:
            out_ref[2 * HALF :, GROUP * (group - 1) : GROUP * group] = part[-2 * HALF :]

    return [functools.partial(one, group) for group in range(4)]


def interleave(*streams):
    marks = [((i + 0.5) / len(stream), n, step) for n, stream in enumerate(streams) for i, step in enumerate(stream)]
    for _, _, step in sorted(marks, key=lambda mark: mark[:2]):
        step()


def softmax_rows(scores, bias, factor):
    scores = scores + bias
    top = jnp.max(scores, axis=1, keepdims=True)
    terms = jnp.exp2((scores - top) * factor)
    return terms * (1.0 / jnp.sum(terms, axis=1, keepdims=True))


def bias_rows(rows):
    start = rows // (2 * HALF) * HALF + rows % HALF
    return slice(start, start + CHUNK)


def run_pairs(pairs, scored, weighted, spread):
    interleave(scored(0, 0))

    def two(index, carry):
        pair = 2 * index
        interleave(scored(pair + 1, 1), weighted(0), spread(pair - 1, 1))
        interleave(scored(jnp.minimum(pair + 2, pairs - 1), 0), weighted(1), spread(pair, 0))
        return carry

    lax.fori_loop(0, pairs // 2, two, 0)
    interleave(spread(pairs - 1, 1))


def forward_kernel(
    head_dim, kv_own, x_side, w_ref, wo_ref, queries, bias, out_ref,
    w_kv, w_out, kv, acc, scores0, scores1, probs0, probs1, sems
):
    width = queries.shape[1]
    factor = head_dim**-0.5 * math.log2(math.e)
    scores, probs = (scores0, scores1), (probs0, probs1)
    copies = fetch(key_weights(w_ref, w_kv) + [(wo_ref, w_out)], sems)
    acc[...] = jnp.zeros_like(acc)
    fill_keys(kv_own, x_side, w_kv, copies, kv)

    def scored(pair, u):
        start, masks = pair_lanes(pair, head_dim, width)
        return span_products(stacked(queries, start, masks), kv, start, scores[u])

    def weighted(u):
        def one(rows):
            part = slice(rows, rows + CHUNK)
            attention = softmax_rows(scores[u][part, :], bias[bias_rows(rows), :], factor)
            probs[u][part, :] = attention.astype(jnp.bfloat16)

        return [functools.partial(one, rows) for rows in range(0, 4 * HALF, CHUNK)]

    def spread(pair, u):
        start, masks = pair_lanes(pair, head_dim, width)
        return [lambda: add_heads(acc, start, masks, span_mix(probs[u], kv, start + width))]

    run_pairs(width // head_dim // 2, scored, weighted, spread)
    attended = acc[...].astype(jnp.bfloat16)
    copies[-1].wait()
    out_ref[...] = jnp.dot(attended, w_out[...], preferred_element_type=jnp.float32).astype(out_ref.dtype)


def backward_kernel(
    head_dim, kv_own, x_side, w_ref, queries, cotangents, bias, down_ref, dq_ref, dside_ref,
    w_kv, queries_t, cotangents_t, kv, dkv, acc,
    scores0, scores1, grads0, grads1, probs0, probs1, dscores0, dscores1, sems
):
    width = queries.shape[1]
    scaling = head_dim**-0.5
    factor = scaling * math.log2(math.e)
    scores, grads = (scores0, scores1), (grads0, grads1)
    probs, dscores = (probs0, probs1), (dscores0, dscores1)
    copies = fetch(key_weights(w_ref, w_kv), sems)
    acc[...] = jnp.zeros_like(acc)
    turned(queries, queries_t)
    turned(cotangents, cotangents_t)
    fill_keys(kv_own, x_side, w_kv, copies, kv)

    def scored(pair, u):
        start, masks = pair_lanes(pair, head_dim, width)
        one = span_products(stacked(queries, start, masks), kv, start, scores[u])
        other = span_products(stacked(cotangents, start, masks), kv, start + width, grads[u])
        return [step for both in zip(one, other) for step in both]

    def weighted(u):
        def one(rows):
            part = slice(rows, rows + CHUNK)
            attention = softmax_rows(scores[u][part, :], bias[bias_rows(rows), :], factor)
            grad = grads[u][part, :]
            centre = jnp.sum(attention * grad, axis=1, keepdims=True)
            probs[u][part, :] = attention.astype(jnp.bfloat16)
            dscores[u][part, :] = (attention * (grad - centre) * scaling).astype(jnp.bfloat16)

        return [functools.partial(one, rows) for rows in range(0, 4 * HALF, CHUNK)]

    def spread(pair, u):
        start, masks = pair_lanes(pair, head_dim, width)
        here = jnp.maximum(pair, 0)

        def query_part():
            add_heads(acc, start, masks, span_mix(dscores[u], kv, start))

        def head_part(source, spans, head, group):
            low = spans[HALF * head : HALF * (head + 1), GROUP * group : GROUP * (group + 1)] if group < 3 else None
            place = slice(GROUP * (group - 1), GROUP * group)
            high = spans[HALF * (head + 2) : HALF * (head + 3), place] if group > 0 else None
            features = source[2 * here + head]
            if group == 0:
                features, span = features[:, :HALF], low
            elif group == 3:
                features, span = features[:, HALF:], high
            else:
                span = jnp.concatenate([low, high], 0)
            return jnp.dot(features, span, preferred_element_type=jnp.float32)

        def key_part(index, group):
            source, spans = ((queries_t, dscores[u]), (cotangents_t, probs[u]))[index]
            both = jnp.concatenate([head_part(source, spans, head, group) for head in range(2)], 0)
            both = both.astype(jnp.bfloat16)
            rows = pl.ds(pl.multiple_of(2 * head_dim * here + index * width, 16), 2 * head_dim)
            place = slice(HALF * group, HALF * (group + 1))
            down_ref[rows, place] = both[:, :HALF]
            dkv[rows, place] = both[:, HALF:]

        parts = [functools.partial(key_part, index, group) for index in range(2) for group in range(4)]
        return parts[:4] + [query_part] + parts[4:]

    run_pairs(width // head_dim // 2, scored, weighted, spread)

    dq_ref[...] = acc[...].astype(dq_ref.dtype)
    for start in range(0, dside_ref.shape[0], GROUP):
        part = jnp.dot(w_kv[...], dkv[:, start : start + GROUP], preferred_element_type=jnp.float32)
        dside_ref[start : start + GROUP, :] = jnp.transpose(part).astype(dside_ref.dtype)


def call_kernel(kernel, args, out_shape, scratch, flops, name, fetched=()):
    spaces = [pl.ANY if i in fetched else pltpu.VMEM for i in range(len(args))]
    return pl.pallas_call(
        kernel,
        in_specs=[pl.BlockSpec(memory_space=space) for space in spaces],
        out_shape=out_shape,
        scratch_shapes=scratch,
        compiler_params=pltpu.CompilerParams(vmem_limit_bytes=LIMIT),
        cost_estimate=pl.CostEstimate(flops=flops, bytes_accessed=16 * 2**20, transcendentals=2**22),
        name=name,
    )(*args)


def own_keys(x_parts, w_qkv):
    width, columns = w_qkv.shape
    out_shape = jax.ShapeDtypeStruct((KEYS // 2, columns - width), jnp.bfloat16)
    return call_kernel(own_keys_kernel, [*x_parts, w_qkv], out_shape, [], 2 * KEYS * width * width, "own_keys")


def own_gradient(dkv, dq, w_qkv):
    out_shape = jax.ShapeDtypeStruct((KEYS // 2, dq.shape[1]), jnp.float32)
    flops = 2 * KEYS * dq.shape[1] ** 2
    return call_kernel(own_gradient_kernel, [dkv, dq, w_qkv], out_shape, [], flops, "own_gradient")


def attention_forward(kv_own, x_side, w_qkv, w_out, queries, bias, heads):
    tokens, width = queries.shape
    half, full = jnp.bfloat16, jnp.float32
    square = (2 * tokens, SPAN)
    scratch = [
        pltpu.VMEM((width, 2 * width), half),
        pltpu.VMEM(w_out.shape, half),
        pltpu.VMEM((KEYS, 2 * width), half),
        pltpu.VMEM((tokens, width), full),
    ]
    scratch += [pltpu.VMEM(square, full)] * 2 + [pltpu.VMEM(square, half)] * 2
    scratch += [pltpu.SemaphoreType.DMA((2 * width // SPAN + 1,))]
    return call_kernel(
        functools.partial(forward_kernel, width // heads),
        [kv_own, x_side, w_qkv, w_out, queries, bias],
        jax.ShapeDtypeStruct(queries.shape, half),
        scratch,
        2 * KEYS * width * width + 4 * heads * tokens * KEYS * LANES,
        "attention_forward",
        fetched=(2, 3),
    )


def attention_backward(kv_own, x_side, w_qkv, queries, cotangents, bias, heads):
    tokens, width = queries.shape
    head_dim = width // heads
    square = (2 * tokens, SPAN)
    half, full = jnp.bfloat16, jnp.float32
    by_head = (heads, head_dim, tokens)
    scratch = [
        pltpu.VMEM((width, 2 * width), half),
        pltpu.VMEM(by_head, half),
        pltpu.VMEM(by_head, half),
        pltpu.VMEM((KEYS, 2 * width), half),
        pltpu.VMEM((2 * width, KEYS // 2), half),
        pltpu.VMEM((tokens, width), full),
    ]
    scratch += [pltpu.VMEM(square, full)] * 4 + [pltpu.VMEM(square, half)] * 4
    scratch += [pltpu.SemaphoreType.DMA((2 * width // SPAN,))]
    return call_kernel(
        functools.partial(backward_kernel, head_dim),
        [kv_own, x_side, w_qkv, queries, cotangents, bias],
        [
            jax.ShapeDtypeStruct((2 * width, KEYS // 2), half),
            jax.ShapeDtypeStruct(queries.shape, half),
            jax.ShapeDtypeStruct((KEYS // 2, width), half),
        ],
        scratch,
        4 * KEYS * width * width + 10 * heads * tokens * KEYS * LANES,
        "attention_backward",
        fetched=(2,),
    )


def project(x, w):
    return jnp.dot(x, w, preferred_element_type=jnp.float32).astype(jnp.bfloat16)


def body(x_forward, x_backward, grad_out, w_qkv, w_out):
    rows, cols, width = x_forward.shape
    heads = lax.axis_size("heads")
    w_q = w_qkv[:, :width]
    flat = lambda x: x.reshape(-1, width)
    bias = window_bias()

    parts_backward = row_halos(x_backward)
    q_backward = project(flat(x_backward), w_q)
    q_forward = project(flat(x_forward), w_q)
    grad_heads = lax.dot_general(
        flat(grad_out), w_out, (((1,), (1,)), ((), ())), preferred_element_type=jnp.float32
    ).astype(jnp.bfloat16)
    sends_backward, q_backward, q_forward, grad_heads, bias = lax.optimization_barrier(
        (column_sends(parts_backward), q_backward, q_forward, grad_heads, bias)
    )
    side_backward = flat(side_columns(sends_backward))
    x_forward, _ = lax.optimization_barrier((x_forward, sends_backward))
    parts_forward = row_halos(x_forward)
    parts_backward, _ = lax.optimization_barrier((parts_backward, sends_backward))
    own_backward = own_keys([flat(part) for part in parts_backward], w_qkv)

    dkv_own, dq, dx_side = attention_backward(
        own_backward, side_backward, w_qkv, q_backward, grad_heads, bias, heads
    )
    dx_side = dx_side.reshape(2 * SIDE, SIDE, width)
    from_right = shifted(dx_side[:, :8], "heads", -1)
    from_left = shifted(dx_side[:, 8:], "heads", 1)
    dx_own = own_gradient(dkv_own, dq, w_qkv).reshape(2 * SIDE, SIDE, width)
    parts_forward, _ = lax.optimization_barrier((parts_forward, dx_own))
    sends_forward = column_sends(parts_forward)
    side_forward = flat(side_columns(sends_forward))
    parts_forward, _ = lax.optimization_barrier((parts_forward, sends_forward))
    own_forward = own_keys([flat(part) for part in parts_forward], w_qkv)
    from_left, from_right, own_forward = lax.optimization_barrier((from_left, from_right, own_forward))
    total = dx_own + jnp.concatenate([from_left, from_right], 1).astype(jnp.float32)
    from_below = shifted(total[:RADIUS].astype(jnp.bfloat16), "rows", -1)
    from_above = shifted(total[RADIUS + SIDE : 2 * RADIUS + SIDE].astype(jnp.bfloat16), "rows", 1)
    side_forward, middle = lax.optimization_barrier((side_forward, total[RADIUS : RADIUS + SIDE]))
    y_forward = attention_forward(own_forward, side_forward, w_qkv, w_out, q_forward, bias, heads)

    gap = jnp.zeros((rows - RADIUS, cols, width), jnp.float32)
    dx = (
        middle
        + jnp.concatenate([from_above.astype(jnp.float32), gap], 0)
        + jnp.concatenate([gap, from_below.astype(jnp.float32)], 0)
    )
    return (y_forward.reshape(rows, cols, width), dx.astype(jnp.bfloat16))


def solution(mesh):
    spec = P("rows", "heads", None)
    return jax.shard_map(
        body, mesh=mesh, in_specs=(spec, spec, spec, P(), P()), out_specs=(spec, spec), check_vma=False
    )
```

```python
import functools
import math

import jax
import jax.numpy as jnp
from jax import lax
from jax.experimental import pallas as pl
from jax.experimental.pallas import tpu as pltpu
from jax.sharding import PartitionSpec as P

RADIUS = 7
SIDE = 16
LANES = 256
GROUP = 256
HALF = 128
SPAN = 3 * GROUP
KEYS = 4 * GROUP
NEG = -1e30
CHUNK = 32
LIMIT = 40 * 2**20


def shifted(value, axis, step):
    count = lax.axis_size(axis)
    return lax.ppermute(value, axis, [(i, (i + step) % count) for i in range(count)])


def row_halos(x):
    return shifted(x[SIDE - RADIUS :], "rows", 1), x, shifted(x[:RADIUS], "rows", -1)


def column_sends(parts):
    zeros = jnp.zeros((2, 8) + parts[0].shape[2:], parts[0].dtype)
    return [jnp.concatenate([part[:, side] for part in parts] + [zeros], 0) for side in (slice(8, 16), slice(0, 8))]


def side_columns(sends):
    return jnp.concatenate([shifted(sends[0], "heads", 1), shifted(sends[1], "heads", -1)], 1)


def window_bias():
    row_start = lax.axis_index("rows") * SIDE
    col_start = lax.axis_index("heads") * SIDE
    rows_total = lax.axis_size("rows") * SIDE
    cols_total = lax.axis_size("heads") * SIDE
    query = lax.broadcasted_iota(jnp.int32, (2 * HALF, SPAN), 0)
    place = lax.broadcasted_iota(jnp.int32, (2 * HALF, SPAN), 1)
    half = query // HALF
    query_row, query_col = query // SIDE, query % SIDE
    group, rest = place // GROUP + half, place % GROUP
    side, inner = rest // HALF, rest % HALF
    key_row, column = group * 8 + inner // SIDE, inner % SIDE
    key_col = jnp.where(side == 0, column, jnp.where(column < 8, column - 8, column + 8))
    image_row = row_start + key_row - RADIUS
    image_col = col_start + key_col
    row_gap, col_gap = key_row - query_row, key_col - query_col
    valid = (row_gap >= 0) & (row_gap <= 2 * RADIUS) & (col_gap >= -RADIUS) & (col_gap <= RADIUS)
    valid &= (image_row >= 0) & (image_row < rows_total) & (image_col >= 0) & (image_col < cols_total)
    return jnp.where(valid, 0.0, NEG).astype(jnp.float32)


def pair_lanes(pair, head_dim, width):
    tile = jnp.clip(2 * pair * head_dim // 128, 0, (width - LANES) // 128)
    offset = 2 * pair * head_dim - tile * 128
    lane = lax.broadcasted_iota(jnp.int32, (1, LANES), 1)
    live = pair >= 0
    first = (lane >= offset) & (lane < offset + head_dim) & live
    second = (lane >= offset + head_dim) & (lane < offset + 2 * head_dim) & live
    return tile * 128, (first, second)


def stacked(ref, start, masks):
    block = ref[:, at_lanes(start)]
    halves = (block[:HALF], block[HALF:])
    return jnp.concatenate([jnp.where(mask, half, 0) for half in halves for mask in masks], 0)


def add_heads(acc, start, masks, parts):
    for half, part in enumerate(parts):
        rows = slice(HALF * half, HALF * (half + 1))
        acc[rows, at_lanes(start)] += jnp.where(masks[0], part[:HALF], jnp.where(masks[1], part[HALF:], 0.0))


def span_mix(weights, kv, start):
    low = jnp.dot(weights[: 2 * HALF, :], kv[:SPAN, at_lanes(start)], preferred_element_type=jnp.float32)
    high = jnp.dot(weights[2 * HALF :, :], kv[GROUP:, at_lanes(start)], preferred_element_type=jnp.float32)
    return low, high


def at_lanes(start):
    return pl.ds(pl.multiple_of(start, 128), LANES)


def own_keys_kernel(above, own, below, weights, out_ref):
    skip = weights.shape[1] - out_ref.shape[1]
    for start in range(0, out_ref.shape[1], GROUP):
        low = 0
        for x_ref in (above, own, below):
            part = jnp.dot(
                x_ref[...], weights[:, skip + start : skip + start + GROUP], preferred_element_type=jnp.float32
            )
            out_ref[low : low + x_ref.shape[0], start : start + GROUP] = part.astype(out_ref.dtype)
            low += x_ref.shape[0]
        out_ref[low:, start : start + GROUP] = jnp.zeros((out_ref.shape[0] - low, GROUP), out_ref.dtype)


def own_gradient_kernel(dkv, dq, weights, out_ref):
    width = dq.shape[1]
    for start in range(0, out_ref.shape[0], GROUP):
        part = jnp.dot(weights[:, width:], dkv[:, start : start + GROUP], preferred_element_type=jnp.float32)
        out_ref[start : start + GROUP, :] = jnp.transpose(part)
    mine = slice(RADIUS * SIDE, RADIUS * SIDE + dq.shape[0])
    out_ref[mine, :] += lax.dot_general(
        dq[...], weights[:, :width], (((1,), (1,)), ((), ())), preferred_element_type=jnp.float32
    )


def fetch(pairs, sems):
    copies = [pltpu.make_async_copy(source, target, sems.at[i]) for i, (source, target) in enumerate(pairs)]
    for copy in copies:
        copy.start()
    return copies


def key_weights(w_ref, w_kv):
    skip, columns = w_ref.shape[1] - w_kv.shape[1], w_kv.shape[1]
    return [
        (w_ref.at[:, pl.ds(skip + start, SPAN)], w_kv.at[:, pl.ds(start, SPAN)]) for start in range(0, columns, SPAN)
    ]


def fill_keys(kv_own, x_side, w_kv, copies, kv):
    for group in range(4):
        kv[GROUP * group : GROUP * group + HALF, :] = kv_own[HALF * group : HALF * (group + 1), :]
    for start in range(0, kv.shape[1], GROUP):
        if start % SPAN == 0:
            copies[start // SPAN].wait()
        part = jnp.dot(x_side[...], w_kv[:, start : start + GROUP], preferred_element_type=jnp.float32)
        part = part.astype(kv.dtype)
        for group in range(4):
            low = GROUP * group + HALF
            kv[low : low + HALF, start : start + GROUP] = part[HALF * group : HALF * (group + 1)]


def turned(source, target):
    heads, head_dim, _ = target.shape
    flipped = jnp.transpose(source[...].astype(jnp.float32))
    for head in range(heads):
        target[head] = flipped[head * head_dim : (head + 1) * head_dim].astype(target.dtype)


def span_products(rows, kv, start, out_ref):
    def one(group):
        low = 0 if group < 3 else 2 * HALF
        high = 4 * HALF if group > 0 else 2 * HALF
        keys = kv[GROUP * group : GROUP * (group + 1), at_lanes(start)]
        part = lax.dot_general(
            rows[low:high], keys, (((1,), (1,)), ((), ())), preferred_element_type=jnp.float32
        )
        if group < 3:
            out_ref[: 2 * HALF, GROUP * group : GROUP * (group + 1)] = part[: 2 * HALF]
        if group > 0:
            out_ref[2 * HALF :, GROUP * (group - 1) : GROUP * group] = part[-2 * HALF :]

    return [functools.partial(one, group) for group in range(4)]


def interleave(*streams):
    marks = [((i + 0.5) / len(stream), n, step) for n, stream in enumerate(streams) for i, step in enumerate(stream)]
    for _, _, step in sorted(marks, key=lambda mark: mark[:2]):
        step()


def softmax_rows(scores, bias, factor):
    scores = scores + bias
    top = jnp.max(scores, axis=1, keepdims=True)
    terms = jnp.exp2((scores - top) * factor)
    return terms * (1.0 / jnp.sum(terms, axis=1, keepdims=True))


def bias_rows(rows):
    start = rows // (2 * HALF) * HALF + rows % HALF
    return slice(start, start + CHUNK)


def run_pairs(pairs, scored, weighted, spread):
    interleave(scored(0, 0))

    def two(index, carry):
        pair = 2 * index
        interleave(scored(pair + 1, 1), weighted(0), spread(pair - 1, 1))
        interleave(scored(jnp.minimum(pair + 2, pairs - 1), 0), weighted(1), spread(pair, 0))
        return carry

    lax.fori_loop(0, pairs // 2, two, 0)
    interleave(spread(pairs - 1, 1))


def forward_kernel(
    head_dim, kv_own, x_side, w_ref, wo_ref, queries, bias, out_ref,
    w_kv, w_out, kv, acc, scores0, scores1, probs0, probs1, sems
):
    width = queries.shape[1]
    factor = head_dim**-0.5 * math.log2(math.e)
    scores, probs = (scores0, scores1), (probs0, probs1)
    copies = fetch(key_weights(w_ref, w_kv) + [(wo_ref, w_out)], sems)
    acc[...] = jnp.zeros_like(acc)
    fill_keys(kv_own, x_side, w_kv, copies, kv)

    def scored(pair, u):
        start, masks = pair_lanes(pair, head_dim, width)
        return span_products(stacked(queries, start, masks), kv, start, scores[u])

    def weighted(u):
        def one(rows):
            part = slice(rows, rows + CHUNK)
            attention = softmax_rows(scores[u][part, :], bias[bias_rows(rows), :], factor)
            probs[u][part, :] = attention.astype(jnp.bfloat16)

        return [functools.partial(one, rows) for rows in range(0, 4 * HALF, CHUNK)]

    def spread(pair, u):
        start, masks = pair_lanes(pair, head_dim, width)
        return [lambda: add_heads(acc, start, masks, span_mix(probs[u], kv, start + width))]

    run_pairs(width // head_dim // 2, scored, weighted, spread)
    attended = acc[...].astype(jnp.bfloat16)
    copies[-1].wait()
    out_ref[...] = jnp.dot(attended, w_out[...], preferred_element_type=jnp.float32).astype(out_ref.dtype)


def backward_kernel(
    head_dim, kv_own, x_side, w_ref, queries, cotangents, bias, down_ref, dq_ref, dside_ref,
    w_kv, queries_t, cotangents_t, kv, dkv, acc,
    scores0, scores1, grads0, grads1, probs0, probs1, dscores0, dscores1, sems
):
    width = queries.shape[1]
    scaling = head_dim**-0.5
    factor = scaling * math.log2(math.e)
    scores, grads = (scores0, scores1), (grads0, grads1)
    probs, dscores = (probs0, probs1), (dscores0, dscores1)
    copies = fetch(key_weights(w_ref, w_kv), sems)
    acc[...] = jnp.zeros_like(acc)
    turned(queries, queries_t)
    turned(cotangents, cotangents_t)
    fill_keys(kv_own, x_side, w_kv, copies, kv)

    def scored(pair, u):
        start, masks = pair_lanes(pair, head_dim, width)
        one = span_products(stacked(queries, start, masks), kv, start, scores[u])
        other = span_products(stacked(cotangents, start, masks), kv, start + width, grads[u])
        return [step for both in zip(one, other) for step in both]

    def weighted(u):
        def one(rows):
            part = slice(rows, rows + CHUNK)
            attention = softmax_rows(scores[u][part, :], bias[bias_rows(rows), :], factor)
            grad = grads[u][part, :]
            centre = jnp.sum(attention * grad, axis=1, keepdims=True)
            probs[u][part, :] = attention.astype(jnp.bfloat16)
            dscores[u][part, :] = (attention * (grad - centre) * scaling).astype(jnp.bfloat16)

        return [functools.partial(one, rows) for rows in range(0, 4 * HALF, CHUNK)]

    def spread(pair, u):
        start, masks = pair_lanes(pair, head_dim, width)
        here = jnp.maximum(pair, 0)

        def query_part():
            add_heads(acc, start, masks, span_mix(dscores[u], kv, start))

        def head_part(source, spans, head, group):
            low = spans[HALF * head : HALF * (head + 1), GROUP * group : GROUP * (group + 1)] if group < 3 else None
            place = slice(GROUP * (group - 1), GROUP * group)
            high = spans[HALF * (head + 2) : HALF * (head + 3), place] if group > 0 else None
            features = source[2 * here + head]
            if group == 0:
                features, span = features[:, :HALF], low
            elif group == 3:
                features, span = features[:, HALF:], high
            else:
                span = jnp.concatenate([low, high], 0)
            return jnp.dot(features, span, preferred_element_type=jnp.float32)

        def key_part(index, group):
            source, spans = ((queries_t, dscores[u]), (cotangents_t, probs[u]))[index]
            both = jnp.concatenate([head_part(source, spans, head, group) for head in range(2)], 0)
            both = both.astype(jnp.bfloat16)
            rows = pl.ds(pl.multiple_of(2 * head_dim * here + index * width, 16), 2 * head_dim)
            place = slice(HALF * group, HALF * (group + 1))
            down_ref[rows, place] = both[:, :HALF]
            dkv[rows, place] = both[:, HALF:]

        parts = [functools.partial(key_part, index, group) for index in range(2) for group in range(4)]
        return parts[:4] + [query_part] + parts[4:]

    run_pairs(width // head_dim // 2, scored, weighted, spread)

    dq_ref[...] = acc[...].astype(dq_ref.dtype)
    for start in range(0, dside_ref.shape[0], GROUP):
        part = jnp.dot(w_kv[...], dkv[:, start : start + GROUP], preferred_element_type=jnp.float32)
        dside_ref[start : start + GROUP, :] = jnp.transpose(part).astype(dside_ref.dtype)


def call_kernel(kernel, args, out_shape, scratch, flops, name, fetched=()):
    spaces = [pl.ANY if i in fetched else pltpu.VMEM for i in range(len(args))]
    return pl.pallas_call(
        kernel,
        in_specs=[pl.BlockSpec(memory_space=space) for space in spaces],
        out_shape=out_shape,
        scratch_shapes=scratch,
        compiler_params=pltpu.CompilerParams(vmem_limit_bytes=LIMIT),
        cost_estimate=pl.CostEstimate(flops=flops, bytes_accessed=16 * 2**20, transcendentals=2**22),
        name=name,
    )(*args)


def own_keys(x_parts, w_qkv):
    width, columns = w_qkv.shape
    out_shape = jax.ShapeDtypeStruct((KEYS // 2, columns - width), jnp.bfloat16)
    return call_kernel(own_keys_kernel, [*x_parts, w_qkv], out_shape, [], 2 * KEYS * width * width, "own_keys")


def own_gradient(dkv, dq, w_qkv):
    out_shape = jax.ShapeDtypeStruct((KEYS // 2, dq.shape[1]), jnp.float32)
    flops = 2 * KEYS * dq.shape[1] ** 2
    return call_kernel(own_gradient_kernel, [dkv, dq, w_qkv], out_shape, [], flops, "own_gradient")


def attention_forward(kv_own, x_side, w_qkv, w_out, queries, bias, heads):
    tokens, width = queries.shape
    half, full = jnp.bfloat16, jnp.float32
    square = (2 * tokens, SPAN)
    scratch = [
        pltpu.VMEM((width, 2 * width), half),
        pltpu.VMEM(w_out.shape, half),
        pltpu.VMEM((KEYS, 2 * width), half),
        pltpu.VMEM((tokens, width), full),
    ]
    scratch += [pltpu.VMEM(square, full)] * 2 + [pltpu.VMEM(square, half)] * 2
    scratch += [pltpu.SemaphoreType.DMA((2 * width // SPAN + 1,))]
    return call_kernel(
        functools.partial(forward_kernel, width // heads),
        [kv_own, x_side, w_qkv, w_out, queries, bias],
        jax.ShapeDtypeStruct(queries.shape, half),
        scratch,
        2 * KEYS * width * width + 4 * heads * tokens * KEYS * LANES,
        "attention_forward",
        fetched=(2, 3),
    )


def attention_backward(kv_own, x_side, w_qkv, queries, cotangents, bias, heads):
    tokens, width = queries.shape
    head_dim = width // heads
    square = (2 * tokens, SPAN)
    half, full = jnp.bfloat16, jnp.float32
    by_head = (heads, head_dim, tokens)
    scratch = [
        pltpu.VMEM((width, 2 * width), half),
        pltpu.VMEM(by_head, half),
        pltpu.VMEM(by_head, half),
        pltpu.VMEM((KEYS, 2 * width), half),
        pltpu.VMEM((2 * width, KEYS // 2), half),
        pltpu.VMEM((tokens, width), full),
    ]
    scratch += [pltpu.VMEM(square, full)] * 4 + [pltpu.VMEM(square, half)] * 4
    scratch += [pltpu.SemaphoreType.DMA((2 * width // SPAN,))]
    return call_kernel(
        functools.partial(backward_kernel, head_dim),
        [kv_own, x_side, w_qkv, queries, cotangents, bias],
        [
            jax.ShapeDtypeStruct((2 * width, KEYS // 2), half),
            jax.ShapeDtypeStruct(queries.shape, half),
            jax.ShapeDtypeStruct((KEYS // 2, width), half),
        ],
        scratch,
        4 * KEYS * width * width + 10 * heads * tokens * KEYS * LANES,
        "attention_backward",
        fetched=(2,),
    )


def project(x, w):
    return jnp.dot(x, w, preferred_element_type=jnp.float32).astype(jnp.bfloat16)


def body(x_forward, x_backward, grad_out, w_qkv, w_out):
    rows, cols, width = x_forward.shape
    heads = lax.axis_size("heads")
    w_q = w_qkv[:, :width]
    flat = lambda x: x.reshape(-1, width)
    bias = window_bias()

    parts_backward = row_halos(x_backward)
    q_backward = project(flat(x_backward), w_q)
    q_forward = project(flat(x_forward), w_q)
    grad_heads = lax.dot_general(
        flat(grad_out), w_out, (((1,), (1,)), ((), ())), preferred_element_type=jnp.float32
    ).astype(jnp.bfloat16)
    sends_backward, q_backward, q_forward, grad_heads, bias = lax.optimization_barrier(
        (column_sends(parts_backward), q_backward, q_forward, grad_heads, bias)
    )
    side_backward = flat(side_columns(sends_backward))
    x_forward, _ = lax.optimization_barrier((x_forward, sends_backward))
    parts_forward = row_halos(x_forward)
    parts_backward, _ = lax.optimization_barrier((parts_backward, sends_backward))
    own_backward = own_keys([flat(part) for part in parts_backward], w_qkv)

    dkv_own, dq, dx_side = attention_backward(
        own_backward, side_backward, w_qkv, q_backward, grad_heads, bias, heads
    )
    dx_side = dx_side.reshape(2 * SIDE, SIDE, width)
    parts_forward, _ = lax.optimization_barrier((parts_forward, dx_side))
    to_right, to_left = column_sends(parts_forward)
    from_left = shifted(jnp.concatenate([dx_side[:, 8:], to_right], 0), "heads", 1)
    from_right = shifted(jnp.concatenate([dx_side[:, :8], to_left], 0), "heads", -1)
    own_forward = own_keys([flat(part) for part in parts_forward], w_qkv)
    dx_own = own_gradient(dkv_own, dq, w_qkv).reshape(2 * SIDE, SIDE, width)
    from_left, from_right, own_forward = lax.optimization_barrier((from_left, from_right, own_forward))
    side_forward = flat(jnp.concatenate([from_left[2 * SIDE :], from_right[2 * SIDE :]], 1))
    from_left, from_right = from_left[: 2 * SIDE], from_right[: 2 * SIDE]
    total = dx_own + jnp.concatenate([from_left, from_right], 1).astype(jnp.float32)
    from_below = shifted(total[:RADIUS].astype(jnp.bfloat16), "rows", -1)
    from_above = shifted(total[RADIUS + SIDE : 2 * RADIUS + SIDE].astype(jnp.bfloat16), "rows", 1)
    side_forward, middle = lax.optimization_barrier((side_forward, total[RADIUS : RADIUS + SIDE]))
    y_forward = attention_forward(own_forward, side_forward, w_qkv, w_out, q_forward, bias, heads)

    gap = jnp.zeros((rows - RADIUS, cols, width), jnp.float32)
    dx = (
        middle
        + jnp.concatenate([from_above.astype(jnp.float32), gap], 0)
        + jnp.concatenate([gap, from_below.astype(jnp.float32)], 0)
    )
    return (y_forward.reshape(rows, cols, width), dx.astype(jnp.bfloat16))


def solution(mesh):
    spec = P("rows", "heads", None)
    return jax.shard_map(
        body, mesh=mesh, in_specs=(spec, spec, spec, P(), P()), out_specs=(spec, spec), check_vma=False
    )
```

```python
import functools
import math

import jax
import jax.numpy as jnp
from jax import lax
from jax.experimental import pallas as pl
from jax.experimental.pallas import tpu as pltpu
from jax.sharding import PartitionSpec as P

RADIUS = 7
SIDE = 16
LANES = 256
GROUP = 256
HALF = 128
SPAN = 3 * GROUP
KEYS = 4 * GROUP
NEG = -1e30
CHUNK = 32
LIMIT = 40 * 2**20


def shifted(value, axis, step):
    count = lax.axis_size(axis)
    return lax.ppermute(value, axis, [(i, (i + step) % count) for i in range(count)])


def row_halos(x):
    return shifted(x[SIDE - RADIUS :], "rows", 1), x, shifted(x[:RADIUS], "rows", -1)


def column_sends(parts):
    return [jnp.concatenate([part[:, side] for part in parts], 0) for side in (slice(8, 16), slice(0, 8))]


def side_columns(sends):
    both = jnp.concatenate([shifted(sends[0], "heads", 1), shifted(sends[1], "heads", -1)], 1)
    return jnp.pad(both, ((0, 2 * SIDE - both.shape[0]), (0, 0), (0, 0)))


def window_bias():
    row_start = lax.axis_index("rows") * SIDE
    col_start = lax.axis_index("heads") * SIDE
    rows_total = lax.axis_size("rows") * SIDE
    cols_total = lax.axis_size("heads") * SIDE
    query = lax.broadcasted_iota(jnp.int32, (2 * HALF, SPAN), 0)
    place = lax.broadcasted_iota(jnp.int32, (2 * HALF, SPAN), 1)
    half = query // HALF
    query_row, query_col = query // SIDE, query % SIDE
    group, rest = place // GROUP + half, place % GROUP
    side, inner = rest // HALF, rest % HALF
    key_row, column = group * 8 + inner // SIDE, inner % SIDE
    key_col = jnp.where(side == 0, column, jnp.where(column < 8, column - 8, column + 8))
    image_row = row_start + key_row - RADIUS
    image_col = col_start + key_col
    row_gap, col_gap = key_row - query_row, key_col - query_col
    valid = (row_gap >= 0) & (row_gap <= 2 * RADIUS) & (col_gap >= -RADIUS) & (col_gap <= RADIUS)
    valid &= (image_row >= 0) & (image_row < rows_total) & (image_col >= 0) & (image_col < cols_total)
    return jnp.where(valid, 0.0, NEG).astype(jnp.float32)


def pair_lanes(pair, head_dim, width):
    tile = jnp.clip(2 * pair * head_dim // 128, 0, (width - LANES) // 128)
    offset = 2 * pair * head_dim - tile * 128
    lane = lax.broadcasted_iota(jnp.int32, (1, LANES), 1)
    live = pair >= 0
    first = (lane >= offset) & (lane < offset + head_dim) & live
    second = (lane >= offset + head_dim) & (lane < offset + 2 * head_dim) & live
    return tile * 128, (first, second)


def stacked(ref, start, masks):
    block = ref[:, at_lanes(start)]
    halves = (block[:HALF], block[HALF:])
    return jnp.concatenate([jnp.where(mask, half, 0) for half in halves for mask in masks], 0)


def add_heads(acc, start, masks, parts):
    for half, part in enumerate(parts):
        rows = slice(HALF * half, HALF * (half + 1))
        acc[rows, at_lanes(start)] += jnp.where(masks[0], part[:HALF], jnp.where(masks[1], part[HALF:], 0.0))


def span_mix(weights, kv, start):
    low = jnp.dot(weights[: 2 * HALF, :], kv[:SPAN, at_lanes(start)], preferred_element_type=jnp.float32)
    high = jnp.dot(weights[2 * HALF :, :], kv[GROUP:, at_lanes(start)], preferred_element_type=jnp.float32)
    return low, high


def at_lanes(start):
    return pl.ds(pl.multiple_of(start, 128), LANES)


def own_keys_kernel(above, own, below, weights, out_ref):
    skip = weights.shape[1] - out_ref.shape[1]
    for start in range(0, out_ref.shape[1], GROUP):
        low = 0
        for x_ref in (above, own, below):
            part = jnp.dot(
                x_ref[...], weights[:, skip + start : skip + start + GROUP], preferred_element_type=jnp.float32
            )
            out_ref[low : low + x_ref.shape[0], start : start + GROUP] = part.astype(out_ref.dtype)
            low += x_ref.shape[0]
        out_ref[low:, start : start + GROUP] = jnp.zeros((out_ref.shape[0] - low, GROUP), out_ref.dtype)


def own_gradient_kernel(dkv, dq, weights, out_ref):
    width = dq.shape[1]
    for start in range(0, out_ref.shape[0], GROUP):
        part = jnp.dot(weights[:, width:], dkv[:, start : start + GROUP], preferred_element_type=jnp.float32)
        out_ref[start : start + GROUP, :] = jnp.transpose(part)
    mine = slice(RADIUS * SIDE, RADIUS * SIDE + dq.shape[0])
    out_ref[mine, :] += lax.dot_general(
        dq[...], weights[:, :width], (((1,), (1,)), ((), ())), preferred_element_type=jnp.float32
    )


def fetch(pairs, sems):
    copies = [pltpu.make_async_copy(source, target, sems.at[i]) for i, (source, target) in enumerate(pairs)]
    for copy in copies:
        copy.start()
    return copies


def key_weights(w_ref, w_kv):
    skip, columns = w_ref.shape[1] - w_kv.shape[1], w_kv.shape[1]
    return [
        (w_ref.at[:, pl.ds(skip + start, SPAN)], w_kv.at[:, pl.ds(start, SPAN)]) for start in range(0, columns, SPAN)
    ]


def fill_keys(kv_own, x_side, w_kv, copies, kv):
    for group in range(4):
        kv[GROUP * group : GROUP * group + HALF, :] = kv_own[HALF * group : HALF * (group + 1), :]
    for start in range(0, kv.shape[1], GROUP):
        if start % SPAN == 0:
            copies[start // SPAN].wait()
        part = jnp.dot(x_side[...], w_kv[:, start : start + GROUP], preferred_element_type=jnp.float32)
        part = part.astype(kv.dtype)
        for group in range(4):
            low = GROUP * group + HALF
            kv[low : low + HALF, start : start + GROUP] = part[HALF * group : HALF * (group + 1)]


def turned(source, target):
    heads, head_dim, _ = target.shape
    flipped = jnp.transpose(source[...].astype(jnp.float32))
    for head in range(heads):
        target[head] = flipped[head * head_dim : (head + 1) * head_dim].astype(target.dtype)


def span_products(rows, kv, start, out_ref):
    def one(group):
        low = 0 if group < 3 else 2 * HALF
        high = 4 * HALF if group > 0 else 2 * HALF
        keys = kv[GROUP * group : GROUP * (group + 1), at_lanes(start)]
        part = lax.dot_general(
            rows[low:high], keys, (((1,), (1,)), ((), ())), preferred_element_type=jnp.float32
        )
        if group < 3:
            out_ref[: 2 * HALF, GROUP * group : GROUP * (group + 1)] = part[: 2 * HALF]
        if group > 0:
            out_ref[2 * HALF :, GROUP * (group - 1) : GROUP * group] = part[-2 * HALF :]

    return [functools.partial(one, group) for group in range(4)]


def interleave(*streams):
    marks = [((i + 0.5) / len(stream), n, step) for n, stream in enumerate(streams) for i, step in enumerate(stream)]
    for _, _, step in sorted(marks, key=lambda mark: mark[:2]):
        step()


def softmax_rows(scores, bias, factor):
    scores = scores + bias
    top = jnp.max(scores, axis=1, keepdims=True)
    terms = jnp.exp2((scores - top) * factor)
    return terms * (1.0 / jnp.sum(terms, axis=1, keepdims=True))


def bias_rows(rows):
    start = rows // (2 * HALF) * HALF + rows % HALF
    return slice(start, start + CHUNK)


def run_pairs(pairs, scored, weighted, spread):
    interleave(scored(0, 0))

    def two(index, carry):
        pair = 2 * index
        interleave(scored(pair + 1, 1), weighted(0), spread(pair - 1, 1))
        interleave(scored(jnp.minimum(pair + 2, pairs - 1), 0), weighted(1), spread(pair, 0))
        return carry

    lax.fori_loop(0, pairs // 2, two, 0)
    interleave(spread(pairs - 1, 1))


def forward_kernel(
    head_dim, kv_own, x_side, w_ref, wo_ref, queries, bias, out_ref,
    w_kv, w_out, kv, acc, scores0, scores1, probs0, probs1, sems
):
    width = queries.shape[1]
    factor = head_dim**-0.5 * math.log2(math.e)
    scores, probs = (scores0, scores1), (probs0, probs1)
    copies = fetch(key_weights(w_ref, w_kv) + [(wo_ref, w_out)], sems)
    acc[...] = jnp.zeros_like(acc)
    fill_keys(kv_own, x_side, w_kv, copies, kv)

    def scored(pair, u):
        start, masks = pair_lanes(pair, head_dim, width)
        return span_products(stacked(queries, start, masks), kv, start, scores[u])

    def weighted(u):
        def one(rows):
            part = slice(rows, rows + CHUNK)
            attention = softmax_rows(scores[u][part, :], bias[bias_rows(rows), :], factor)
            probs[u][part, :] = attention.astype(jnp.bfloat16)

        return [functools.partial(one, rows) for rows in range(0, 4 * HALF, CHUNK)]

    def spread(pair, u):
        start, masks = pair_lanes(pair, head_dim, width)
        return [lambda: add_heads(acc, start, masks, span_mix(probs[u], kv, start + width))]

    run_pairs(width // head_dim // 2, scored, weighted, spread)
    attended = acc[...].astype(jnp.bfloat16)
    copies[-1].wait()
    out_ref[...] = jnp.dot(attended, w_out[...], preferred_element_type=jnp.float32).astype(out_ref.dtype)


def backward_kernel(
    head_dim, kv_own, x_side, w_ref, queries, cotangents, bias, down_ref, dq_ref, dside_ref,
    w_kv, queries_t, cotangents_t, kv, dkv, acc,
    scores0, scores1, grads0, grads1, probs0, probs1, dscores0, dscores1, sems
):
    width = queries.shape[1]
    scaling = head_dim**-0.5
    factor = scaling * math.log2(math.e)
    scores, grads = (scores0, scores1), (grads0, grads1)
    probs, dscores = (probs0, probs1), (dscores0, dscores1)
    copies = fetch(key_weights(w_ref, w_kv), sems)
    acc[...] = jnp.zeros_like(acc)
    turned(queries, queries_t)
    turned(cotangents, cotangents_t)
    fill_keys(kv_own, x_side, w_kv, copies, kv)

    def scored(pair, u):
        start, masks = pair_lanes(pair, head_dim, width)
        one = span_products(stacked(queries, start, masks), kv, start, scores[u])
        other = span_products(stacked(cotangents, start, masks), kv, start + width, grads[u])
        return [step for both in zip(one, other) for step in both]

    def weighted(u):
        def one(rows):
            part = slice(rows, rows + CHUNK)
            attention = softmax_rows(scores[u][part, :], bias[bias_rows(rows), :], factor)
            grad = grads[u][part, :]
            centre = jnp.sum(attention * grad, axis=1, keepdims=True)
            probs[u][part, :] = attention.astype(jnp.bfloat16)
            dscores[u][part, :] = (attention * (grad - centre) * scaling).astype(jnp.bfloat16)

        return [functools.partial(one, rows) for rows in range(0, 4 * HALF, CHUNK)]

    def spread(pair, u):
        start, masks = pair_lanes(pair, head_dim, width)
        here = jnp.maximum(pair, 0)

        def query_part():
            add_heads(acc, start, masks, span_mix(dscores[u], kv, start))

        def head_part(source, spans, head, group):
            low = spans[HALF * head : HALF * (head + 1), GROUP * group : GROUP * (group + 1)] if group < 3 else None
            place = slice(GROUP * (group - 1), GROUP * group)
            high = spans[HALF * (head + 2) : HALF * (head + 3), place] if group > 0 else None
            features = source[2 * here + head]
            if group == 0:
                features, span = features[:, :HALF], low
            elif group == 3:
                features, span = features[:, HALF:], high
            else:
                span = jnp.concatenate([low, high], 0)
            return jnp.dot(features, span, preferred_element_type=jnp.float32)

        def key_part(index, group):
            source, spans = ((queries_t, dscores[u]), (cotangents_t, probs[u]))[index]
            both = jnp.concatenate([head_part(source, spans, head, group) for head in range(2)], 0)
            both = both.astype(jnp.bfloat16)
            rows = pl.ds(pl.multiple_of(2 * head_dim * here + index * width, 16), 2 * head_dim)
            place = slice(HALF * group, HALF * (group + 1))
            down_ref[rows, place] = both[:, :HALF]
            dkv[rows, place] = both[:, HALF:]

        parts = [functools.partial(key_part, index, group) for index in range(2) for group in range(4)]
        return parts[:4] + [query_part] + parts[4:]

    run_pairs(width // head_dim // 2, scored, weighted, spread)

    dq_ref[...] = acc[...].astype(dq_ref.dtype)
    for start in range(0, dside_ref.shape[0], GROUP):
        part = jnp.dot(w_kv[...], dkv[:, start : start + GROUP], preferred_element_type=jnp.float32)
        dside_ref[start : start + GROUP, :] = jnp.transpose(part).astype(dside_ref.dtype)


def call_kernel(kernel, args, out_shape, scratch, flops, name, fetched=()):
    spaces = [pl.ANY if i in fetched else pltpu.VMEM for i in range(len(args))]
    return pl.pallas_call(
        kernel,
        in_specs=[pl.BlockSpec(memory_space=space) for space in spaces],
        out_shape=out_shape,
        scratch_shapes=scratch,
        compiler_params=pltpu.CompilerParams(vmem_limit_bytes=LIMIT),
        cost_estimate=pl.CostEstimate(flops=flops, bytes_accessed=16 * 2**20, transcendentals=2**22),
        name=name,
    )(*args)


def own_keys(x_parts, w_qkv):
    width, columns = w_qkv.shape
    out_shape = jax.ShapeDtypeStruct((KEYS // 2, columns - width), jnp.bfloat16)
    return call_kernel(own_keys_kernel, [*x_parts, w_qkv], out_shape, [], 2 * KEYS * width * width, "own_keys")


def own_gradient(dkv, dq, w_qkv):
    out_shape = jax.ShapeDtypeStruct((KEYS // 2, dq.shape[1]), jnp.float32)
    flops = 2 * KEYS * dq.shape[1] ** 2
    return call_kernel(own_gradient_kernel, [dkv, dq, w_qkv], out_shape, [], flops, "own_gradient")


def attention_forward(kv_own, x_side, w_qkv, w_out, queries, bias, heads):
    tokens, width = queries.shape
    half, full = jnp.bfloat16, jnp.float32
    square = (2 * tokens, SPAN)
    scratch = [
        pltpu.VMEM((width, 2 * width), half),
        pltpu.VMEM(w_out.shape, half),
        pltpu.VMEM((KEYS, 2 * width), half),
        pltpu.VMEM((tokens, width), full),
    ]
    scratch += [pltpu.VMEM(square, full)] * 2 + [pltpu.VMEM(square, half)] * 2
    scratch += [pltpu.SemaphoreType.DMA((2 * width // SPAN + 1,))]
    return call_kernel(
        functools.partial(forward_kernel, width // heads),
        [kv_own, x_side, w_qkv, w_out, queries, bias],
        jax.ShapeDtypeStruct(queries.shape, half),
        scratch,
        2 * KEYS * width * width + 4 * heads * tokens * KEYS * LANES,
        "attention_forward",
        fetched=(2, 3),
    )


def attention_backward(kv_own, x_side, w_qkv, queries, cotangents, bias, heads):
    tokens, width = queries.shape
    head_dim = width // heads
    square = (2 * tokens, SPAN)
    half, full = jnp.bfloat16, jnp.float32
    by_head = (heads, head_dim, tokens)
    scratch = [
        pltpu.VMEM((width, 2 * width), half),
        pltpu.VMEM(by_head, half),
        pltpu.VMEM(by_head, half),
        pltpu.VMEM((KEYS, 2 * width), half),
        pltpu.VMEM((2 * width, KEYS // 2), half),
        pltpu.VMEM((tokens, width), full),
    ]
    scratch += [pltpu.VMEM(square, full)] * 4 + [pltpu.VMEM(square, half)] * 4
    scratch += [pltpu.SemaphoreType.DMA((2 * width // SPAN,))]
    return call_kernel(
        functools.partial(backward_kernel, head_dim),
        [kv_own, x_side, w_qkv, queries, cotangents, bias],
        [
            jax.ShapeDtypeStruct((2 * width, KEYS // 2), half),
            jax.ShapeDtypeStruct(queries.shape, half),
            jax.ShapeDtypeStruct((KEYS // 2, width), half),
        ],
        scratch,
        4 * KEYS * width * width + 10 * heads * tokens * KEYS * LANES,
        "attention_backward",
        fetched=(2,),
    )


def project(x, w):
    return jnp.dot(x, w, preferred_element_type=jnp.float32).astype(jnp.bfloat16)


def body(x_forward, x_backward, grad_out, w_qkv, w_out):
    rows, cols, width = x_forward.shape
    heads = lax.axis_size("heads")
    w_q = w_qkv[:, :width]
    flat = lambda x: x.reshape(-1, width)
    bias = window_bias()

    parts_backward = row_halos(x_backward)
    q_backward = project(flat(x_backward), w_q)
    q_forward = project(flat(x_forward), w_q)
    grad_heads = lax.dot_general(
        flat(grad_out), w_out, (((1,), (1,)), ((), ())), preferred_element_type=jnp.float32
    ).astype(jnp.bfloat16)
    sends_backward, q_backward, q_forward, grad_heads, bias = lax.optimization_barrier(
        (column_sends(parts_backward), q_backward, q_forward, grad_heads, bias)
    )
    side_backward = flat(side_columns(sends_backward))
    x_forward, _ = lax.optimization_barrier((x_forward, sends_backward))
    parts_forward = row_halos(x_forward)
    parts_backward, _ = lax.optimization_barrier((parts_backward, sends_backward))
    own_backward = own_keys([flat(part) for part in parts_backward], w_qkv)

    dkv_own, dq, dx_side = attention_backward(
        own_backward, side_backward, w_qkv, q_backward, grad_heads, bias, heads
    )
    dx_side = dx_side.reshape(2 * SIDE, SIDE, width)[: SIDE + 2 * RADIUS]
    from_right = shifted(dx_side[:, :8], "heads", -1)
    from_left = shifted(dx_side[:, 8:], "heads", 1)
    dx_own = own_gradient(dkv_own, dq, w_qkv).reshape(2 * SIDE, SIDE, width)
    parts_forward, _ = lax.optimization_barrier((parts_forward, dx_own))
    sends_forward = column_sends(parts_forward)
    side_forward = flat(side_columns(sends_forward))
    parts_forward, _ = lax.optimization_barrier((parts_forward, sends_forward))
    own_forward = own_keys([flat(part) for part in parts_forward], w_qkv)
    from_left, from_right, own_forward = lax.optimization_barrier((from_left, from_right, own_forward))
    total = dx_own[: SIDE + 2 * RADIUS] + jnp.concatenate([from_left, from_right], 1).astype(jnp.float32)
    from_below = shifted(total[:RADIUS].astype(jnp.bfloat16), "rows", -1)
    from_above = shifted(total[RADIUS + SIDE : 2 * RADIUS + SIDE].astype(jnp.bfloat16), "rows", 1)
    side_forward, middle = lax.optimization_barrier((side_forward, total[RADIUS : RADIUS + SIDE]))
    y_forward = attention_forward(own_forward, side_forward, w_qkv, w_out, q_forward, bias, heads)

    gap = jnp.zeros((rows - RADIUS, cols, width), jnp.float32)
    dx = (
        middle
        + jnp.concatenate([from_above.astype(jnp.float32), gap], 0)
        + jnp.concatenate([gap, from_below.astype(jnp.float32)], 0)
    )
    return (y_forward.reshape(rows, cols, width), dx.astype(jnp.bfloat16))


def solution(mesh):
    spec = P("rows", "heads", None)
    return jax.shard_map(
        body, mesh=mesh, in_specs=(spec, spec, spec, P(), P()), out_specs=(spec, spec), check_vma=False
    )
```

```python
import functools
import math

import jax
import jax.numpy as jnp
from jax import lax
from jax.experimental import pallas as pl
from jax.experimental.pallas import tpu as pltpu
from jax.sharding import PartitionSpec as P

RADIUS = 7
SIDE = 16
LANES = 256
GROUP = 256
HALF = 128
SPAN = 3 * GROUP
KEYS = 4 * GROUP
NEG = -1e30
CHUNK = 32
LIMIT = 40 * 2**20


def shifted(value, axis, step):
    count = lax.axis_size(axis)
    return lax.ppermute(value, axis, [(i, (i + step) % count) for i in range(count)])


def row_halos(x):
    return shifted(x[SIDE - RADIUS :], "rows", 1), x, shifted(x[:RADIUS], "rows", -1)


def column_sends(parts):
    zeros = jnp.zeros((2, 8) + parts[0].shape[2:], parts[0].dtype)
    return [jnp.concatenate([part[:, side] for part in parts] + [zeros], 0) for side in (slice(8, 16), slice(0, 8))]


def side_columns(sends):
    return jnp.concatenate([shifted(sends[0], "heads", 1), shifted(sends[1], "heads", -1)], 1)


def window_bias():
    row_start = lax.axis_index("rows") * SIDE
    col_start = lax.axis_index("heads") * SIDE
    rows_total = lax.axis_size("rows") * SIDE
    cols_total = lax.axis_size("heads") * SIDE
    query = lax.broadcasted_iota(jnp.int32, (2 * HALF, SPAN), 0)
    place = lax.broadcasted_iota(jnp.int32, (2 * HALF, SPAN), 1)
    half = query // HALF
    query_row, query_col = query // SIDE, query % SIDE
    group, rest = place // GROUP + half, place % GROUP
    side, inner = rest // HALF, rest % HALF
    key_row, column = group * 8 + inner // SIDE, inner % SIDE
    key_col = jnp.where(side == 0, column, jnp.where(column < 8, column - 8, column + 8))
    image_row = row_start + key_row - RADIUS
    image_col = col_start + key_col
    row_gap, col_gap = key_row - query_row, key_col - query_col
    valid = (row_gap >= 0) & (row_gap <= 2 * RADIUS) & (col_gap >= -RADIUS) & (col_gap <= RADIUS)
    valid &= (image_row >= 0) & (image_row < rows_total) & (image_col >= 0) & (image_col < cols_total)
    return jnp.where(valid, 0.0, NEG).astype(jnp.float32)


def pair_lanes(pair, head_dim, width):
    tile = jnp.clip(2 * pair * head_dim // 128, 0, (width - LANES) // 128)
    offset = 2 * pair * head_dim - tile * 128
    lane = lax.broadcasted_iota(jnp.int32, (1, LANES), 1)
    live = pair >= 0
    first = (lane >= offset) & (lane < offset + head_dim) & live
    second = (lane >= offset + head_dim) & (lane < offset + 2 * head_dim) & live
    return tile * 128, (first, second)


def stacked(ref, start, masks):
    block = ref[:, at_lanes(start)]
    halves = (block[:HALF], block[HALF:])
    return jnp.concatenate([jnp.where(mask, half, 0) for half in halves for mask in masks], 0)


def add_heads(acc, start, masks, parts):
    for half, part in enumerate(parts):
        rows = slice(HALF * half, HALF * (half + 1))
        acc[rows, at_lanes(start)] += jnp.where(masks[0], part[:HALF], jnp.where(masks[1], part[HALF:], 0.0))


def span_mix(weights, kv, start):
    low = jnp.dot(weights[: 2 * HALF, :], kv[:SPAN, at_lanes(start)], preferred_element_type=jnp.float32)
    high = jnp.dot(weights[2 * HALF :, :], kv[GROUP:, at_lanes(start)], preferred_element_type=jnp.float32)
    return low, high


def at_lanes(start):
    return pl.ds(pl.multiple_of(start, 128), LANES)


def own_keys_kernel(above, own, below, weights, out_ref):
    skip = weights.shape[1] - out_ref.shape[1]
    for start in range(0, out_ref.shape[1], GROUP):
        low = 0
        for x_ref in (above, own, below):
            part = jnp.dot(
                x_ref[...], weights[:, skip + start : skip + start + GROUP], preferred_element_type=jnp.float32
            )
            out_ref[low : low + x_ref.shape[0], start : start + GROUP] = part.astype(out_ref.dtype)
            low += x_ref.shape[0]
        out_ref[low:, start : start + GROUP] = jnp.zeros((out_ref.shape[0] - low, GROUP), out_ref.dtype)


def own_gradient_kernel(dkv, dq, weights, out_ref):
    width = dq.shape[1]
    for start in range(0, out_ref.shape[0], GROUP):
        part = jnp.dot(weights[:, width:], dkv[:, start : start + GROUP], preferred_element_type=jnp.float32)
        out_ref[start : start + GROUP, :] = jnp.transpose(part)
    mine = slice(RADIUS * SIDE, RADIUS * SIDE + dq.shape[0])
    out_ref[mine, :] += lax.dot_general(
        dq[...], weights[:, :width], (((1,), (1,)), ((), ())), preferred_element_type=jnp.float32
    )


def fetch(pairs, sems):
    copies = [pltpu.make_async_copy(source, target, sems.at[i]) for i, (source, target) in enumerate(pairs)]
    for copy in copies:
        copy.start()
    return copies


def key_weights(w_ref, w_kv):
    skip, columns = w_ref.shape[1] - w_kv.shape[1], w_kv.shape[1]
    return [
        (w_ref.at[:, pl.ds(skip + start, SPAN)], w_kv.at[:, pl.ds(start, SPAN)]) for start in range(0, columns, SPAN)
    ]


def fill_keys(kv_own, x_side, w_kv, copies, kv):
    for group in range(4):
        kv[GROUP * group : GROUP * group + HALF, :] = kv_own[HALF * group : HALF * (group + 1), :]
    for start in range(0, kv.shape[1], GROUP):
        if start % SPAN == 0:
            copies[start // SPAN].wait()
        part = jnp.dot(x_side[...], w_kv[:, start : start + GROUP], preferred_element_type=jnp.float32)
        part = part.astype(kv.dtype)
        for group in range(4):
            low = GROUP * group + HALF
            kv[low : low + HALF, start : start + GROUP] = part[HALF * group : HALF * (group + 1)]


def turned(source, target):
    heads, head_dim, _ = target.shape
    flipped = jnp.transpose(source[...].astype(jnp.float32))
    for head in range(heads):
        target[head] = flipped[head * head_dim : (head + 1) * head_dim].astype(target.dtype)


def span_products(rows, kv, start, out_ref):
    def one(group):
        low = 0 if group < 3 else 2 * HALF
        high = 4 * HALF if group > 0 else 2 * HALF
        keys = kv[GROUP * group : GROUP * (group + 1), at_lanes(start)]
        part = lax.dot_general(
            rows[low:high], keys, (((1,), (1,)), ((), ())), preferred_element_type=jnp.float32
        )
        if group < 3:
            out_ref[: 2 * HALF, GROUP * group : GROUP * (group + 1)] = part[: 2 * HALF]
        if group > 0:
            out_ref[2 * HALF :, GROUP * (group - 1) : GROUP * group] = part[-2 * HALF :]

    return [functools.partial(one, group) for group in range(4)]


def interleave(*streams):
    marks = [((i + 0.5) / len(stream), n, step) for n, stream in enumerate(streams) for i, step in enumerate(stream)]
    for _, _, step in sorted(marks, key=lambda mark: mark[:2]):
        step()


def softmax_rows(scores, bias, factor):
    scores = scores + bias
    top = jnp.max(scores, axis=1, keepdims=True)
    terms = jnp.exp2((scores - top) * factor)
    return terms * (1.0 / jnp.sum(terms, axis=1, keepdims=True))


def bias_rows(rows):
    start = rows // (2 * HALF) * HALF + rows % HALF
    return slice(start, start + CHUNK)


def run_pairs(pairs, scored, weighted, spread):
    interleave(scored(0, 0))

    def two(index, carry):
        pair = 2 * index
        interleave(scored(pair + 1, 1), weighted(0), spread(pair - 1, 1))
        interleave(scored(jnp.minimum(pair + 2, pairs - 1), 0), weighted(1), spread(pair, 0))
        return carry

    lax.fori_loop(0, pairs // 2, two, 0)
    interleave(spread(pairs - 1, 1))


def forward_kernel(
    head_dim, kv_own, x_side, w_ref, wo_ref, queries, bias, out_ref,
    w_kv, w_out, kv, acc, scores0, scores1, probs0, probs1, sems
):
    width = queries.shape[1]
    factor = head_dim**-0.5 * math.log2(math.e)
    scores, probs = (scores0, scores1), (probs0, probs1)
    copies = fetch(key_weights(w_ref, w_kv) + [(wo_ref, w_out)], sems)
    acc[...] = jnp.zeros_like(acc)
    fill_keys(kv_own, x_side, w_kv, copies, kv)

    def scored(pair, u):
        start, masks = pair_lanes(pair, head_dim, width)
        return span_products(stacked(queries, start, masks), kv, start, scores[u])

    def weighted(u):
        def one(rows):
            part = slice(rows, rows + CHUNK)
            attention = softmax_rows(scores[u][part, :], bias[bias_rows(rows), :], factor)
            probs[u][part, :] = attention.astype(jnp.bfloat16)

        return [functools.partial(one, rows) for rows in range(0, 4 * HALF, CHUNK)]

    def spread(pair, u):
        start, masks = pair_lanes(pair, head_dim, width)
        return [lambda: add_heads(acc, start, masks, span_mix(probs[u], kv, start + width))]

    run_pairs(width // head_dim // 2, scored, weighted, spread)
    attended = acc[...].astype(jnp.bfloat16)
    copies[-1].wait()
    out_ref[...] = jnp.dot(attended, w_out[...], preferred_element_type=jnp.float32).astype(out_ref.dtype)


def backward_kernel(
    head_dim, kv_own, x_side, w_ref, queries, cotangents, bias, down_ref, dq_ref, dside_ref,
    w_kv, queries_t, cotangents_t, kv, dkv, acc,
    scores0, scores1, grads0, grads1, probs0, probs1, dscores0, dscores1, sems
):
    width = queries.shape[1]
    scaling = head_dim**-0.5
    factor = scaling * math.log2(math.e)
    scores, grads = (scores0, scores1), (grads0, grads1)
    probs, dscores = (probs0, probs1), (dscores0, dscores1)
    copies = fetch(key_weights(w_ref, w_kv), sems)
    acc[...] = jnp.zeros_like(acc)
    turned(queries, queries_t)
    turned(cotangents, cotangents_t)
    fill_keys(kv_own, x_side, w_kv, copies, kv)

    def scored(pair, u):
        start, masks = pair_lanes(pair, head_dim, width)
        one = span_products(stacked(queries, start, masks), kv, start, scores[u])
        other = span_products(stacked(cotangents, start, masks), kv, start + width, grads[u])
        return [step for both in zip(one, other) for step in both]

    def weighted(u):
        def one(rows):
            part = slice(rows, rows + CHUNK)
            attention = softmax_rows(scores[u][part, :], bias[bias_rows(rows), :], factor)
            grad = grads[u][part, :]
            centre = jnp.sum(attention * grad, axis=1, keepdims=True)
            probs[u][part, :] = attention.astype(jnp.bfloat16)
            dscores[u][part, :] = (attention * (grad - centre) * scaling).astype(jnp.bfloat16)

        return [functools.partial(one, rows) for rows in range(0, 4 * HALF, CHUNK)]

    def spread(pair, u):
        start, masks = pair_lanes(pair, head_dim, width)
        here = jnp.maximum(pair, 0)

        def query_part():
            add_heads(acc, start, masks, span_mix(dscores[u], kv, start))

        def head_part(source, spans, head, group):
            low = spans[HALF * head : HALF * (head + 1), GROUP * group : GROUP * (group + 1)] if group < 3 else None
            place = slice(GROUP * (group - 1), GROUP * group)
            high = spans[HALF * (head + 2) : HALF * (head + 3), place] if group > 0 else None
            features = source[2 * here + head]
            if group == 0:
                features, span = features[:, :HALF], low
            elif group == 3:
                features, span = features[:, HALF:], high
            else:
                span = jnp.concatenate([low, high], 0)
            return jnp.dot(features, span, preferred_element_type=jnp.float32)

        def key_part(index, group):
            source, spans = ((queries_t, dscores[u]), (cotangents_t, probs[u]))[index]
            both = jnp.concatenate([head_part(source, spans, head, group) for head in range(2)], 0)
            both = both.astype(jnp.bfloat16)
            rows = pl.ds(pl.multiple_of(2 * head_dim * here + index * width, 16), 2 * head_dim)
            place = slice(HALF * group, HALF * (group + 1))
            down_ref[rows, place] = both[:, :HALF]
            dkv[rows, place] = both[:, HALF:]

        parts = [functools.partial(key_part, index, group) for index in range(2) for group in range(4)]
        return parts[:4] + [query_part] + parts[4:]

    run_pairs(width // head_dim // 2, scored, weighted, spread)

    dq_ref[...] = acc[...].astype(dq_ref.dtype)
    for start in range(0, dside_ref.shape[0], GROUP):
        part = jnp.dot(w_kv[...], dkv[:, start : start + GROUP], preferred_element_type=jnp.float32)
        dside_ref[start : start + GROUP, :] = jnp.transpose(part).astype(dside_ref.dtype)


def call_kernel(kernel, args, out_shape, scratch, flops, name, fetched=()):
    spaces = [pl.ANY if i in fetched else pltpu.VMEM for i in range(len(args))]
    return pl.pallas_call(
        kernel,
        in_specs=[pl.BlockSpec(memory_space=space) for space in spaces],
        out_shape=out_shape,
        scratch_shapes=scratch,
        compiler_params=pltpu.CompilerParams(vmem_limit_bytes=LIMIT),
        cost_estimate=pl.CostEstimate(flops=flops, bytes_accessed=16 * 2**20, transcendentals=2**22),
        name=name,
    )(*args)


def own_keys(x_parts, w_qkv):
    width, columns = w_qkv.shape
    out_shape = jax.ShapeDtypeStruct((KEYS // 2, columns - width), jnp.bfloat16)
    return call_kernel(own_keys_kernel, [*x_parts, w_qkv], out_shape, [], 2 * KEYS * width * width, "own_keys")


def own_gradient(dkv, dq, w_qkv):
    out_shape = jax.ShapeDtypeStruct((KEYS // 2, dq.shape[1]), jnp.float32)
    flops = 2 * KEYS * dq.shape[1] ** 2
    return call_kernel(own_gradient_kernel, [dkv, dq, w_qkv], out_shape, [], flops, "own_gradient")


def attention_forward(kv_own, x_side, w_qkv, w_out, queries, bias, heads):
    tokens, width = queries.shape
    half, full = jnp.bfloat16, jnp.float32
    square = (2 * tokens, SPAN)
    scratch = [
        pltpu.VMEM((width, 2 * width), half),
        pltpu.VMEM(w_out.shape, half),
        pltpu.VMEM((KEYS, 2 * width), half),
        pltpu.VMEM((tokens, width), full),
    ]
    scratch += [pltpu.VMEM(square, full)] * 2 + [pltpu.VMEM(square, half)] * 2
    scratch += [pltpu.SemaphoreType.DMA((2 * width // SPAN + 1,))]
    return call_kernel(
        functools.partial(forward_kernel, width // heads),
        [kv_own, x_side, w_qkv, w_out, queries, bias],
        jax.ShapeDtypeStruct(queries.shape, half),
        scratch,
        2 * KEYS * width * width + 4 * heads * tokens * KEYS * LANES,
        "attention_forward",
        fetched=(2, 3),
    )


def attention_backward(kv_own, x_side, w_qkv, queries, cotangents, bias, heads):
    tokens, width = queries.shape
    head_dim = width // heads
    square = (2 * tokens, SPAN)
    half, full = jnp.bfloat16, jnp.float32
    by_head = (heads, head_dim, tokens)
    scratch = [
        pltpu.VMEM((width, 2 * width), half),
        pltpu.VMEM(by_head, half),
        pltpu.VMEM(by_head, half),
        pltpu.VMEM((KEYS, 2 * width), half),
        pltpu.VMEM((2 * width, KEYS // 2), half),
        pltpu.VMEM((tokens, width), full),
    ]
    scratch += [pltpu.VMEM(square, full)] * 4 + [pltpu.VMEM(square, half)] * 4
    scratch += [pltpu.SemaphoreType.DMA((2 * width // SPAN,))]
    return call_kernel(
        functools.partial(backward_kernel, head_dim),
        [kv_own, x_side, w_qkv, queries, cotangents, bias],
        [
            jax.ShapeDtypeStruct((2 * width, KEYS // 2), half),
            jax.ShapeDtypeStruct(queries.shape, half),
            jax.ShapeDtypeStruct((KEYS // 2, width), half),
        ],
        scratch,
        4 * KEYS * width * width + 10 * heads * tokens * KEYS * LANES,
        "attention_backward",
        fetched=(2,),
    )


def project(x, w):
    return jnp.dot(x, w, preferred_element_type=jnp.float32).astype(jnp.bfloat16)


def body(x_forward, x_backward, grad_out, w_qkv, w_out):
    rows, cols, width = x_forward.shape
    heads = lax.axis_size("heads")
    w_q = w_qkv[:, :width]
    flat = lambda x: x.reshape(-1, width)
    bias = window_bias()

    parts_backward = row_halos(x_backward)
    q_backward = project(flat(x_backward), w_q)
    q_forward = project(flat(x_forward), w_q)
    grad_heads = lax.dot_general(
        flat(grad_out), w_out, (((1,), (1,)), ((), ())), preferred_element_type=jnp.float32
    ).astype(jnp.bfloat16)
    sends_backward, q_backward, q_forward, grad_heads, bias = lax.optimization_barrier(
        (column_sends(parts_backward), q_backward, q_forward, grad_heads, bias)
    )
    side_backward = flat(side_columns(sends_backward))
    parts_backward, _ = lax.optimization_barrier((parts_backward, sends_backward))
    own_backward = own_keys([flat(part) for part in parts_backward], w_qkv)
    x_forward, _ = lax.optimization_barrier((x_forward, own_backward))
    parts_forward = row_halos(x_forward)

    dkv_own, dq, dx_side = attention_backward(
        own_backward, side_backward, w_qkv, q_backward, grad_heads, bias, heads
    )
    dx_side = dx_side.reshape(2 * SIDE, SIDE, width)
    from_right = shifted(dx_side[:, :8], "heads", -1)
    from_left = shifted(dx_side[:, 8:], "heads", 1)
    dx_own = own_gradient(dkv_own, dq, w_qkv).reshape(2 * SIDE, SIDE, width)
    parts_forward, _ = lax.optimization_barrier((parts_forward, dx_own))
    sends_forward = column_sends(parts_forward)
    side_forward = flat(side_columns(sends_forward))
    parts_forward, _ = lax.optimization_barrier((parts_forward, sends_forward))
    own_forward = own_keys([flat(part) for part in parts_forward], w_qkv)
    from_left, from_right, own_forward = lax.optimization_barrier((from_left, from_right, own_forward))
    total = dx_own + jnp.concatenate([from_left, from_right], 1).astype(jnp.float32)
    from_below = shifted(total[:RADIUS].astype(jnp.bfloat16), "rows", -1)
    from_above = shifted(total[RADIUS + SIDE : 2 * RADIUS + SIDE].astype(jnp.bfloat16), "rows", 1)
    side_forward, middle = lax.optimization_barrier((side_forward, total[RADIUS : RADIUS + SIDE]))
    y_forward = attention_forward(own_forward, side_forward, w_qkv, w_out, q_forward, bias, heads)

    gap = jnp.zeros((rows - RADIUS, cols, width), jnp.float32)
    dx = (
        middle
        + jnp.concatenate([from_above.astype(jnp.float32), gap], 0)
        + jnp.concatenate([gap, from_below.astype(jnp.float32)], 0)
    )
    return (y_forward.reshape(rows, cols, width), dx.astype(jnp.bfloat16))


def solution(mesh):
    spec = P("rows", "heads", None)
    return jax.shard_map(
        body, mesh=mesh, in_specs=(spec, spec, spec, P(), P()), out_specs=(spec, spec), check_vma=False
    )
```

```python
import functools
import math

import jax
import jax.numpy as jnp
from jax import lax
from jax.experimental import pallas as pl
from jax.experimental.pallas import tpu as pltpu
from jax.sharding import PartitionSpec as P

RADIUS = 7
SIDE = 16
LANES = 256
GROUP = 256
HALF = 128
SPAN = 3 * GROUP
KEYS = 4 * GROUP
NEG = -1e30
CHUNK = 32
LIMIT = 40 * 2**20


def shifted(value, axis, step):
    count = lax.axis_size(axis)
    return lax.ppermute(value, axis, [(i, (i + step) % count) for i in range(count)])


def row_halos(x):
    return shifted(x[SIDE - RADIUS :], "rows", 1), x, shifted(x[:RADIUS], "rows", -1)


def column_sends(parts):
    zeros = jnp.zeros((2, 8) + parts[0].shape[2:], parts[0].dtype)
    return [jnp.concatenate([part[:, side] for part in parts] + [zeros], 0) for side in (slice(8, 16), slice(0, 8))]


def side_columns(sends):
    return jnp.concatenate([shifted(sends[0], "heads", 1), shifted(sends[1], "heads", -1)], 1)


def window_bias():
    row_start = lax.axis_index("rows") * SIDE
    col_start = lax.axis_index("heads") * SIDE
    rows_total = lax.axis_size("rows") * SIDE
    cols_total = lax.axis_size("heads") * SIDE
    query = lax.broadcasted_iota(jnp.int32, (2 * HALF, SPAN), 0)
    place = lax.broadcasted_iota(jnp.int32, (2 * HALF, SPAN), 1)
    half = query // HALF
    query_row, query_col = query // SIDE, query % SIDE
    group, rest = place // GROUP + half, place % GROUP
    side, inner = rest // HALF, rest % HALF
    key_row, column = group * 8 + inner // SIDE, inner % SIDE
    key_col = jnp.where(side == 0, column, jnp.where(column < 8, column - 8, column + 8))
    image_row = row_start + key_row - RADIUS
    image_col = col_start + key_col
    row_gap, col_gap = key_row - query_row, key_col - query_col
    valid = (row_gap >= 0) & (row_gap <= 2 * RADIUS) & (col_gap >= -RADIUS) & (col_gap <= RADIUS)
    valid &= (image_row >= 0) & (image_row < rows_total) & (image_col >= 0) & (image_col < cols_total)
    return jnp.where(valid, 0.0, NEG).astype(jnp.float32)


def pair_lanes(pair, head_dim, width):
    tile = jnp.clip(2 * pair * head_dim // 128, 0, (width - LANES) // 128)
    offset = 2 * pair * head_dim - tile * 128
    lane = lax.broadcasted_iota(jnp.int32, (1, LANES), 1)
    live = pair >= 0
    first = (lane >= offset) & (lane < offset + head_dim) & live
    second = (lane >= offset + head_dim) & (lane < offset + 2 * head_dim) & live
    return tile * 128, (first, second)


def stacked(ref, start, masks):
    block = ref[:, at_lanes(start)]
    halves = (block[:HALF], block[HALF:])
    return jnp.concatenate([jnp.where(mask, half, 0) for half in halves for mask in masks], 0)


def add_heads(acc, start, masks, parts):
    for half, part in enumerate(parts):
        rows = slice(HALF * half, HALF * (half + 1))
        acc[rows, at_lanes(start)] += jnp.where(masks[0], part[:HALF], jnp.where(masks[1], part[HALF:], 0.0))


def span_mix(weights, kv, start):
    low = jnp.dot(weights[: 2 * HALF, :], kv[:SPAN, at_lanes(start)], preferred_element_type=jnp.float32)
    high = jnp.dot(weights[2 * HALF :, :], kv[GROUP:, at_lanes(start)], preferred_element_type=jnp.float32)
    return low, high


def at_lanes(start):
    return pl.ds(pl.multiple_of(start, 128), LANES)


def own_keys_kernel(above, own, below, weights, out_ref):
    skip = weights.shape[1] - out_ref.shape[1]
    for start in range(0, out_ref.shape[1], GROUP):
        low = 0
        for x_ref in (above, own, below):
            part = jnp.dot(
                x_ref[...], weights[:, skip + start : skip + start + GROUP], preferred_element_type=jnp.float32
            )
            out_ref[low : low + x_ref.shape[0], start : start + GROUP] = part.astype(out_ref.dtype)
            low += x_ref.shape[0]
        out_ref[low:, start : start + GROUP] = jnp.zeros((out_ref.shape[0] - low, GROUP), out_ref.dtype)


def own_gradient_kernel(dkv, dq, weights, out_ref):
    width = dq.shape[1]
    for start in range(0, out_ref.shape[0], GROUP):
        part = jnp.dot(weights[:, width:], dkv[:, start : start + GROUP], preferred_element_type=jnp.float32)
        out_ref[start : start + GROUP, :] = jnp.transpose(part)
    mine = slice(RADIUS * SIDE, RADIUS * SIDE + dq.shape[0])
    out_ref[mine, :] += lax.dot_general(
        dq[...], weights[:, :width], (((1,), (1,)), ((), ())), preferred_element_type=jnp.float32
    )


def fetch(pairs, sems):
    copies = [pltpu.make_async_copy(source, target, sems.at[i]) for i, (source, target) in enumerate(pairs)]
    for copy in copies:
        copy.start()
    return copies


def key_weights(w_ref, w_kv):
    skip, columns = w_ref.shape[1] - w_kv.shape[1], w_kv.shape[1]
    return [
        (w_ref.at[:, pl.ds(skip + start, SPAN)], w_kv.at[:, pl.ds(start, SPAN)]) for start in range(0, columns, SPAN)
    ]


def fill_keys(kv_own, x_side, w_kv, copies, kv):
    for group in range(4):
        kv[GROUP * group : GROUP * group + HALF, :] = kv_own[HALF * group : HALF * (group + 1), :]
    for start in range(0, kv.shape[1], GROUP):
        if start % SPAN == 0:
            copies[start // SPAN].wait()
        part = jnp.dot(x_side[...], w_kv[:, start : start + GROUP], preferred_element_type=jnp.float32)
        part = part.astype(kv.dtype)
        for group in range(4):
            low = GROUP * group + HALF
            kv[low : low + HALF, start : start + GROUP] = part[HALF * group : HALF * (group + 1)]


def turned(source, target):
    heads, head_dim, _ = target.shape
    flipped = jnp.transpose(source[...].astype(jnp.float32))
    for head in range(heads):
        target[head] = flipped[head * head_dim : (head + 1) * head_dim].astype(target.dtype)


def span_products(rows, kv, start, out_ref):
    def one(group):
        low = 0 if group < 3 else 2 * HALF
        high = 4 * HALF if group > 0 else 2 * HALF
        keys = kv[GROUP * group : GROUP * (group + 1), at_lanes(start)]
        part = lax.dot_general(
            rows[low:high], keys, (((1,), (1,)), ((), ())), preferred_element_type=jnp.float32
        )
        if group < 3:
            out_ref[: 2 * HALF, GROUP * group : GROUP * (group + 1)] = part[: 2 * HALF]
        if group > 0:
            out_ref[2 * HALF :, GROUP * (group - 1) : GROUP * group] = part[-2 * HALF :]

    return [functools.partial(one, group) for group in range(4)]


def interleave(*streams):
    marks = [((i + 0.5) / len(stream), n, step) for n, stream in enumerate(streams) for i, step in enumerate(stream)]
    for _, _, step in sorted(marks, key=lambda mark: mark[:2]):
        step()


def softmax_rows(scores, bias, factor):
    scores = scores + bias
    top = jnp.max(scores, axis=1, keepdims=True)
    terms = jnp.exp2((scores - top) * factor)
    return terms * (1.0 / jnp.sum(terms, axis=1, keepdims=True))


def bias_rows(rows):
    start = rows // (2 * HALF) * HALF + rows % HALF
    return slice(start, start + CHUNK)


def run_pairs(pairs, scored, weighted, spread):
    interleave(scored(0, 0))

    def two(index, carry):
        pair = 2 * index
        interleave(scored(pair + 1, 1), weighted(0), spread(pair - 1, 1))
        interleave(scored(jnp.minimum(pair + 2, pairs - 1), 0), weighted(1), spread(pair, 0))
        return carry

    lax.fori_loop(0, pairs // 2, two, 0)
    interleave(spread(pairs - 1, 1))


def forward_kernel(
    head_dim, kv_own, x_side, w_ref, wo_ref, queries, bias, out_ref,
    w_kv, w_out, kv, acc, scores0, scores1, probs0, probs1, sems
):
    width = queries.shape[1]
    factor = head_dim**-0.5 * math.log2(math.e)
    scores, probs = (scores0, scores1), (probs0, probs1)
    copies = fetch(key_weights(w_ref, w_kv) + [(wo_ref, w_out)], sems)
    acc[...] = jnp.zeros_like(acc)
    fill_keys(kv_own, x_side, w_kv, copies, kv)

    def scored(pair, u):
        start, masks = pair_lanes(pair, head_dim, width)
        return span_products(stacked(queries, start, masks), kv, start, scores[u])

    def weighted(u):
        def one(rows):
            part = slice(rows, rows + CHUNK)
            attention = softmax_rows(scores[u][part, :], bias[bias_rows(rows), :], factor)
            probs[u][part, :] = attention.astype(jnp.bfloat16)

        return [functools.partial(one, rows) for rows in range(0, 4 * HALF, CHUNK)]

    def spread(pair, u):
        start, masks = pair_lanes(pair, head_dim, width)
        return [lambda: add_heads(acc, start, masks, span_mix(probs[u], kv, start + width))]

    run_pairs(width // head_dim // 2, scored, weighted, spread)
    attended = acc[...].astype(jnp.bfloat16)
    copies[-1].wait()
    out_ref[...] = jnp.dot(attended, w_out[...], preferred_element_type=jnp.float32).astype(out_ref.dtype)


def backward_kernel(
    head_dim, kv_own, x_side, w_ref, queries, cotangents, queries_t, cotangents_t, bias,
    down_ref, dq_ref, dside_ref, w_kv, kv, dkv, acc,
    scores0, scores1, grads0, grads1, probs0, probs1, dscores0, dscores1, sems
):
    width = queries.shape[1]
    scaling = head_dim**-0.5
    factor = scaling * math.log2(math.e)
    scores, grads = (scores0, scores1), (grads0, grads1)
    probs, dscores = (probs0, probs1), (dscores0, dscores1)
    copies = fetch(key_weights(w_ref, w_kv), sems)
    acc[...] = jnp.zeros_like(acc)
    fill_keys(kv_own, x_side, w_kv, copies, kv)

    def scored(pair, u):
        start, masks = pair_lanes(pair, head_dim, width)
        one = span_products(stacked(queries, start, masks), kv, start, scores[u])
        other = span_products(stacked(cotangents, start, masks), kv, start + width, grads[u])
        return [step for both in zip(one, other) for step in both]

    def weighted(u):
        def one(rows):
            part = slice(rows, rows + CHUNK)
            attention = softmax_rows(scores[u][part, :], bias[bias_rows(rows), :], factor)
            grad = grads[u][part, :]
            centre = jnp.sum(attention * grad, axis=1, keepdims=True)
            probs[u][part, :] = attention.astype(jnp.bfloat16)
            dscores[u][part, :] = (attention * (grad - centre) * scaling).astype(jnp.bfloat16)

        return [functools.partial(one, rows) for rows in range(0, 4 * HALF, CHUNK)]

    def spread(pair, u):
        start, masks = pair_lanes(pair, head_dim, width)
        here = jnp.maximum(pair, 0)

        def query_part():
            add_heads(acc, start, masks, span_mix(dscores[u], kv, start))

        def head_part(source, spans, head, group):
            low = spans[HALF * head : HALF * (head + 1), GROUP * group : GROUP * (group + 1)] if group < 3 else None
            place = slice(GROUP * (group - 1), GROUP * group)
            high = spans[HALF * (head + 2) : HALF * (head + 3), place] if group > 0 else None
            features = source[2 * here + head]
            if group == 0:
                features, span = features[:, :HALF], low
            elif group == 3:
                features, span = features[:, HALF:], high
            else:
                span = jnp.concatenate([low, high], 0)
            return jnp.dot(features, span, preferred_element_type=jnp.float32)

        def key_part(index, group):
            source, spans = ((queries_t, dscores[u]), (cotangents_t, probs[u]))[index]
            both = jnp.concatenate([head_part(source, spans, head, group) for head in range(2)], 0)
            both = both.astype(jnp.bfloat16)
            rows = pl.ds(pl.multiple_of(2 * head_dim * here + index * width, 16), 2 * head_dim)
            place = slice(HALF * group, HALF * (group + 1))
            down_ref[rows, place] = both[:, :HALF]
            dkv[rows, place] = both[:, HALF:]

        parts = [functools.partial(key_part, index, group) for index in range(2) for group in range(4)]
        return parts[:4] + [query_part] + parts[4:]

    run_pairs(width // head_dim // 2, scored, weighted, spread)

    dq_ref[...] = acc[...].astype(dq_ref.dtype)
    for start in range(0, dside_ref.shape[0], GROUP):
        part = jnp.dot(w_kv[...], dkv[:, start : start + GROUP], preferred_element_type=jnp.float32)
        dside_ref[start : start + GROUP, :] = jnp.transpose(part).astype(dside_ref.dtype)


def call_kernel(kernel, args, out_shape, scratch, flops, name, fetched=()):
    spaces = [pl.ANY if i in fetched else pltpu.VMEM for i in range(len(args))]
    return pl.pallas_call(
        kernel,
        in_specs=[pl.BlockSpec(memory_space=space) for space in spaces],
        out_shape=out_shape,
        scratch_shapes=scratch,
        compiler_params=pltpu.CompilerParams(vmem_limit_bytes=LIMIT),
        cost_estimate=pl.CostEstimate(flops=flops, bytes_accessed=16 * 2**20, transcendentals=2**22),
        name=name,
    )(*args)


def both_turned_kernel(queries, cotangents, queries_t, cotangents_t):
    turned(queries, queries_t)
    turned(cotangents, cotangents_t)


def both_turned(queries, cotangents, heads):
    tokens, width = queries.shape
    out_shape = [jax.ShapeDtypeStruct((heads, width // heads, tokens), jnp.bfloat16)] * 2
    return call_kernel(both_turned_kernel, [queries, cotangents], out_shape, [], 0, "both_turned")


def own_keys(x_parts, w_qkv):
    width, columns = w_qkv.shape
    out_shape = jax.ShapeDtypeStruct((KEYS // 2, columns - width), jnp.bfloat16)
    return call_kernel(own_keys_kernel, [*x_parts, w_qkv], out_shape, [], 2 * KEYS * width * width, "own_keys")


def own_gradient(dkv, dq, w_qkv):
    out_shape = jax.ShapeDtypeStruct((KEYS // 2, dq.shape[1]), jnp.float32)
    flops = 2 * KEYS * dq.shape[1] ** 2
    return call_kernel(own_gradient_kernel, [dkv, dq, w_qkv], out_shape, [], flops, "own_gradient")


def attention_forward(kv_own, x_side, w_qkv, w_out, queries, bias, heads):
    tokens, width = queries.shape
    half, full = jnp.bfloat16, jnp.float32
    square = (2 * tokens, SPAN)
    scratch = [
        pltpu.VMEM((width, 2 * width), half),
        pltpu.VMEM(w_out.shape, half),
        pltpu.VMEM((KEYS, 2 * width), half),
        pltpu.VMEM((tokens, width), full),
    ]
    scratch += [pltpu.VMEM(square, full)] * 2 + [pltpu.VMEM(square, half)] * 2
    scratch += [pltpu.SemaphoreType.DMA((2 * width // SPAN + 1,))]
    return call_kernel(
        functools.partial(forward_kernel, width // heads),
        [kv_own, x_side, w_qkv, w_out, queries, bias],
        jax.ShapeDtypeStruct(queries.shape, half),
        scratch,
        2 * KEYS * width * width + 4 * heads * tokens * KEYS * LANES,
        "attention_forward",
        fetched=(2, 3),
    )


def attention_backward(kv_own, x_side, w_qkv, queries, cotangents, flipped, bias, heads):
    tokens, width = queries.shape
    head_dim = width // heads
    square = (2 * tokens, SPAN)
    half, full = jnp.bfloat16, jnp.float32
    scratch = [
        pltpu.VMEM((width, 2 * width), half),
        pltpu.VMEM((KEYS, 2 * width), half),
        pltpu.VMEM((2 * width, KEYS // 2), half),
        pltpu.VMEM((tokens, width), full),
    ]
    scratch += [pltpu.VMEM(square, full)] * 4 + [pltpu.VMEM(square, half)] * 4
    scratch += [pltpu.SemaphoreType.DMA((2 * width // SPAN,))]
    return call_kernel(
        functools.partial(backward_kernel, head_dim),
        [kv_own, x_side, w_qkv, queries, cotangents, *flipped, bias],
        [
            jax.ShapeDtypeStruct((2 * width, KEYS // 2), half),
            jax.ShapeDtypeStruct(queries.shape, half),
            jax.ShapeDtypeStruct((KEYS // 2, width), half),
        ],
        scratch,
        4 * KEYS * width * width + 10 * heads * tokens * KEYS * LANES,
        "attention_backward",
        fetched=(2,),
    )


def project(x, w):
    return jnp.dot(x, w, preferred_element_type=jnp.float32).astype(jnp.bfloat16)


def body(x_forward, x_backward, grad_out, w_qkv, w_out):
    rows, cols, width = x_forward.shape
    heads = lax.axis_size("heads")
    w_q = w_qkv[:, :width]
    flat = lambda x: x.reshape(-1, width)
    bias = window_bias()

    parts_backward = row_halos(x_backward)
    q_backward = project(flat(x_backward), w_q)
    q_forward = project(flat(x_forward), w_q)
    grad_heads = lax.dot_general(
        flat(grad_out), w_out, (((1,), (1,)), ((), ())), preferred_element_type=jnp.float32
    ).astype(jnp.bfloat16)
    flipped = both_turned(q_backward, grad_heads, heads)
    sends_backward, q_backward, q_forward, grad_heads, flipped, bias = lax.optimization_barrier(
        (column_sends(parts_backward), q_backward, q_forward, grad_heads, flipped, bias)
    )
    side_backward = flat(side_columns(sends_backward))
    parts_backward, _ = lax.optimization_barrier((parts_backward, sends_backward))
    own_backward = own_keys([flat(part) for part in parts_backward], w_qkv)
    x_forward, _ = lax.optimization_barrier((x_forward, own_backward))
    parts_forward = row_halos(x_forward)

    dkv_own, dq, dx_side = attention_backward(
        own_backward, side_backward, w_qkv, q_backward, grad_heads, flipped, bias, heads
    )
    dx_side = dx_side.reshape(2 * SIDE, SIDE, width)
    from_right = shifted(dx_side[:, :8], "heads", -1)
    from_left = shifted(dx_side[:, 8:], "heads", 1)
    dx_own = own_gradient(dkv_own, dq, w_qkv).reshape(2 * SIDE, SIDE, width)
    parts_forward, _ = lax.optimization_barrier((parts_forward, dx_own))
    sends_forward = column_sends(parts_forward)
    side_forward = flat(side_columns(sends_forward))
    parts_forward, _ = lax.optimization_barrier((parts_forward, sends_forward))
    own_forward = own_keys([flat(part) for part in parts_forward], w_qkv)
    from_left, from_right, own_forward = lax.optimization_barrier((from_left, from_right, own_forward))
    total = dx_own + jnp.concatenate([from_left, from_right], 1).astype(jnp.float32)
    from_below = shifted(total[:RADIUS].astype(jnp.bfloat16), "rows", -1)
    from_above = shifted(total[RADIUS + SIDE : 2 * RADIUS + SIDE].astype(jnp.bfloat16), "rows", 1)
    side_forward, middle = lax.optimization_barrier((side_forward, total[RADIUS : RADIUS + SIDE]))
    y_forward = attention_forward(own_forward, side_forward, w_qkv, w_out, q_forward, bias, heads)

    gap = jnp.zeros((rows - RADIUS, cols, width), jnp.float32)
    dx = (
        middle
        + jnp.concatenate([from_above.astype(jnp.float32), gap], 0)
        + jnp.concatenate([gap, from_below.astype(jnp.float32)], 0)
    )
    return (y_forward.reshape(rows, cols, width), dx.astype(jnp.bfloat16))


def solution(mesh):
    spec = P("rows", "heads", None)
    return jax.shard_map(
        body, mesh=mesh, in_specs=(spec, spec, spec, P(), P()), out_specs=(spec, spec), check_vma=False
    )
```
